32 devices in a mesh: dp: 16 (over z, y, x), mp: 2 (over core).
Axes of the slice: x: 2, y: 2, z: 4, core: 2. Of those that a mesh axis runs over, the one named last changes fastest.
Arguments:
- media: bfloat16 [12288, 1024], P('dp'), may hold values from -6 to 6
- latents: bfloat16 [3072, 1024], P('dp'), may hold values from -6 to 6
- patch_rows: int32 [48], P('dp'), may hold values from 128 to 256, as said below
- image_count: int32 [16], P('dp'), may hold values from 1 to 3, as said below
- cotangent: bfloat16 [3072, 1024], P('dp'), may hold values from -6 to 6
- w_query: bfloat16 [2, 1024, 512], P(None, 'dp', 'mp'), may hold values from -0.1875 to 0.1875
- w_key: bfloat16 [2, 1024, 512], P(None, 'dp', 'mp'), may hold values from -0.1875 to 0.1875
- w_value: bfloat16 [2, 1024, 512], P(None, 'dp', 'mp'), may hold values from -0.1875 to 0.1875
- w_out: bfloat16 [2, 512, 1024], P(None, 'mp', 'dp'), may hold values from -1.5 to 1.5
- w_up: bfloat16 [2, 1024, 4096], P(None, 'dp', 'mp'), may hold values from -0.1875 to 0.1875
- w_down: bfloat16 [2, 4096, 1024], P(None, 'mp', 'dp'), may hold values from -0.09375 to 0.09375
- norm_gains: bfloat16 [2, 3, 1024], P(None, None, 'dp'), may hold values from 0.25 to 1.75
- norm_shifts: bfloat16 [2, 3, 1024], P(None, None, 'dp'), may hold values from -3 to 3
Outputs:
- latents_out: bfloat16 [3072, 1024], P('dp')
- media_grad: float32 [12288, 1024], P('dp')
- latents_grad: float32 [3072, 1024], P('dp')
- query_grad: float32 [2, 1024, 512], P(None, 'dp', 'mp')
- key_grad: float32 [2, 1024, 512], P(None, 'dp', 'mp')
- value_grad: float32 [2, 1024, 512], P(None, 'dp', 'mp')
- output_grad: float32 [2, 512, 1024], P(None, 'mp', 'dp')
- up_grad: float32 [2, 1024, 4096], P(None, 'dp', 'mp')
- down_grad: float32 [2, 4096, 1024], P(None, 'mp', 'dp')
- gains_grad: float32 [2, 2, 1024], P(None, None, 'dp')
- shifts_grad: float32 [2, 2, 1024], P(None, None, 'dp')
- feed_norm_grad: float32 [2, 2, 1024], P(None, None, 'dp')
The draws below stay inside these ranges and needn't reach their ends.
Inputs may be any that keep to these rules, and one draw needn't show every extreme that they name: The first image_count of a device's 3 slots hold images, the others are empty; some device has all 3 in every draw. The first patch_rows of a slot's 256 patch rows are valid; some slot has all 256 in every draw.
All inputs are finite; a program needn't handle non-finite values.
Results may differ from the reference program's by a relative error of at most 0.023.
Values may be sent and summed in bfloat16 or wider, within the bound.
A program may use at most 192 MiB of HBM per device.

```python
import jax
import jax.numpy as jnp
from jax import lax

D = 1024
HEADS = 8
HEAD_DIM = 64
FF = 4096
LATENTS = 64
PATCH = 256
LAYERS = 2
IMG_DEV = 3
IMAGES = 48


def draw_image_count(key, part):
    key = jax.random.fold_in(key, 11)
    devices = IMAGES // IMG_DEV
    first, second = jax.random.split(key)
    counts = jax.random.randint(first, (devices,), 1, IMG_DEV + 1)
    busiest = jax.random.randint(second, (), 0, devices)
    return jnp.where(jnp.arange(devices) == busiest, IMG_DEV, counts).astype(jnp.int32)


def draw_patch_rows(key, part):
    key = jax.random.fold_in(key, 23)
    first, second = jax.random.split(key)
    rows = jax.random.randint(first, (IMAGES,), PATCH // 2, PATCH + 1)
    fullest = jax.random.randint(second, (), 0, IMAGES)
    return jnp.where(jnp.arange(IMAGES) == fullest, PATCH, rows).astype(jnp.int32)


def steps_of(own_key, shape, cuts, smallest, top_value):
    factor_of, own = 1.0, jax.random.fold_in(own_key, 6)
    for axis_at, shards_of in cuts:
        steps = jnp.exp(jax.random.uniform(jax.random.fold_in(own, axis_at), (shards_of,), jnp.float32, smallest / len(cuts), top_value / len(cuts)))
        factor_of = factor_of * jnp.repeat(steps, shape[axis_at] // shards_of).reshape([-1 if axis == axis_at else 1 for axis in range(len(shape))])
    return factor_of


def centred(stream_key, extent, width, reach, cuts=(), kind=jnp.bfloat16):
    entries = jax.random.normal(stream_key, extent, jnp.float32) * width
    if len(cuts) > 0:
        entries = steps_of(stream_key, extent, cuts, -0.22, 0.18) * entries
    return jnp.clip(entries, min=-reach, max=reach).astype(kind)


def setup_inputs(seed: int = 0) -> dict:
    key_list = jax.random.split(jax.random.key(seed), 14)
    media = centred(key_list[0], (IMAGES * PATCH, D), 1.0, 6.0, ((0, 16),))
    latents = centred(key_list[1], (IMAGES * LATENTS, D), 1.0, 6.0, ((0, 16),))
    patch_rows = draw_patch_rows(jax.random.fold_in(key_list[13], 71), 0)
    image_count = draw_image_count(jax.random.fold_in(key_list[13], 71), 0)
    cotangent = centred(key_list[4], (IMAGES * LATENTS, D), 1.0, 6.0, ((0, 16),))
    w_query = centred(key_list[5], (LAYERS, D, HEADS * HEAD_DIM), D ** -0.5, 0.1875, ((1, 16), (2, 2)))
    w_key = centred(key_list[6], (LAYERS, D, HEADS * HEAD_DIM), D ** -0.5, 0.1875, ((1, 16), (2, 2)))
    w_value = centred(key_list[7], (LAYERS, D, HEADS * HEAD_DIM), D ** -0.5, 0.1875, ((1, 16), (2, 2)))
    w_out = centred(key_list[8], (LAYERS, HEADS * HEAD_DIM, D), (D // 64) ** -0.5, 1.5, ((1, 2), (2, 16)))
    w_up = centred(key_list[9], (LAYERS, D, FF), D ** -0.5, 0.1875, ((1, 16), (2, 2)))
    w_down = centred(key_list[10], (LAYERS, FF, D), FF ** -0.5, 0.09375, ((1, 2), (2, 16)))
    norm_gains = jnp.clip(1.0 + 0.15 * jax.random.normal(key_list[11], (LAYERS, 3, D), jnp.float32), 0.25, 1.75).astype(jnp.bfloat16)
    norm_shifts = centred(key_list[12], (LAYERS, 3, D), 0.5, 3.0, ((2, 16),))
    return {"media": media, "latents": latents, "patch_rows": patch_rows, "image_count": image_count, "cotangent": cotangent, "w_query": w_query, "w_key": w_key, "w_value": w_value, "w_out": w_out, "w_up": w_up, "w_down": w_down, "norm_gains": norm_gains, "norm_shifts": norm_shifts}


@jax.custom_vjp
def low(v):
    return lax.optimization_barrier(v.astype(jnp.bfloat16)).astype(jnp.float32)

@jax.custom_vjp
def low_back(v):
    return v

def low_keep(v):
    return (low(v), None)

def low_pass(kept, grad):
    return (grad,)

def back_keep(v):
    return (v, None)

def back_low(kept, grad):
    return (low(grad),)
low.defvjp(low_keep, low_pass)
low_back.defvjp(back_keep, back_low)
HIGH = lax.Precision.HIGHEST

def normalize(values, gain, shift):
    centre = values - lax.optimization_barrier(jnp.mean(values, -1, keepdims=True))
    spread = lax.optimization_barrier(jnp.mean(centre * centre, -1, keepdims=True))
    return centre * lax.rsqrt(spread + 1e-05) * gain + shift

def project(left, right):
    return jnp.einsum('gnd,de->gne', left, right, precision=HIGH)

def resampler_layer(state, media_rows, key_mask, weights):
    w_query, w_key, w_value, w_out, w_up, w_down, gains, shifts = weights
    groups = state.shape[0]
    media_low = low(normalize(media_rows, gains[0], shifts[0]))
    latent_low = low(normalize(state, gains[1], shifts[1]))
    query = low(low_back(project(latent_low, w_query)))
    joined = jnp.concatenate([media_low, latent_low], 1)
    keys = low(low_back(project(joined, w_key)))
    values = low(low_back(project(joined, w_value)))
    query = query.reshape(groups, LATENTS, HEADS, HEAD_DIM)
    keys = keys.reshape(groups, PATCH + LATENTS, HEADS, HEAD_DIM)
    values = values.reshape(groups, PATCH + LATENTS, HEADS, HEAD_DIM)
    scores = low_back(jnp.einsum('gqhd,gkhd->ghqk', query, keys, precision=HIGH) * 0.125)
    scores = jnp.where(key_mask[:, None, None, :], scores, -1000000000.0)
    probs = low(jax.nn.softmax(scores, -1))
    mixed = low(low_back(jnp.einsum('ghqk,gkhd->gqhd', probs, values, precision=HIGH)))
    mixed = mixed.reshape(groups, LATENTS, HEADS * HEAD_DIM)
    middle = state + low_back(project(mixed, w_out))
    hidden = low(normalize(middle, gains[2], shifts[2]))
    pre_act = low_back(project(hidden, w_up))
    act = low(jax.nn.gelu(pre_act, approximate=False))
    return middle + low_back(project(act, w_down))

def reference(media, latents, patch_rows, image_count, cotangent, w_query, w_key, w_value, w_out, w_up, w_down, norm_gains, norm_shifts):
    slots = jnp.arange(IMAGES, dtype=jnp.int32)
    live = (slots % IMG_DEV < image_count[slots // IMG_DEV]).astype(jnp.float32)
    key_mask = jnp.concatenate([jnp.arange(PATCH, dtype=jnp.int32)[None, :] < patch_rows[:, None], jnp.ones((IMAGES, LATENTS), bool)], 1)
    params = tuple((a.astype(jnp.float32) for a in (w_query, w_key, w_value, w_out, w_up, w_down, norm_gains, norm_shifts)))
    media_full = media.astype(jnp.float32)
    latent_full = latents.astype(jnp.float32)
    blocks = IMAGES // IMG_DEV

    def forward(media_in, latent_in, weights):

        def group(args):
            media_rows, state, mask_rows = args
            for layer in range(LAYERS):
                state = resampler_layer(state, media_rows, mask_rows, tuple((w[layer] for w in weights)))
            return state
        result = lax.map(jax.checkpoint(group), (media_in.reshape(blocks, IMG_DEV, PATCH, D), latent_in.reshape(blocks, IMG_DEV, LATENTS, D), key_mask.reshape(blocks, IMG_DEV, PATCH + LATENTS)))
        return result.reshape(IMAGES, LATENTS, D) * live[:, None, None]
    result, pull = jax.vjp(forward, media_full, latent_full, params)
    grad_media, grad_latents, grads = pull(cotangent.astype(jnp.float32).reshape(IMAGES, LATENTS, D))
    feed_norm = jnp.stack([grads[6][:, 2], grads[7][:, 2]], 1)
    return (result.reshape(IMAGES * LATENTS, D).astype(jnp.bfloat16), grad_media.reshape(IMAGES * PATCH, D), grad_latents.reshape(IMAGES * LATENTS, D), grads[0], grads[1], grads[2], grads[3], grads[4], grads[5], grads[6][:, :2], grads[7][:, :2], feed_norm)
```

```python
from functools import partial

import jax
import jax.numpy as jnp
from jax import lax
from jax.experimental import pallas as pl
from jax.experimental.pallas import tpu as pltpu
from jax.sharding import PartitionSpec as P

HEAD_DIM = 64
LATENTS = 64
PATCH = 256


NEGATIVE = -1000000000.0


def normalize(values, gain, shift):
    centre = values - jnp.mean(values, -1, keepdims=True)
    spread = jnp.mean(centre * centre, -1, keepdims=True)
    return centre * lax.rsqrt(spread + 1e-05) * gain + shift


def product(left, right):
    return jnp.dot(left, right, preferred_element_type=jnp.float32)


def outer_sum(left, right):
    return lax.dot_general(
        left, right, (((0,), (0,)), ((), ())), preferred_element_type=jnp.float32
    )


def back_product(left, right):
    return lax.dot_general(
        left, right, (((1,), (1,)), ((), ())), preferred_element_type=jnp.float32
    )


def forward_reduce(values):
    return lax.psum(values.astype(jnp.bfloat16), "mp").astype(jnp.float32)


def backward_reduce(values):
    return lax.psum(values.astype(jnp.bfloat16), "mp").astype(jnp.float32)


def key_scores(query_heads, key_heads, key_mask):
    scores = (
        jnp.einsum("iqhd,ikhd->ihqk", query_heads, key_heads, preferred_element_type=jnp.float32)
        * 0.125
    )
    return jnp.where(key_mask[:, None, None, :], scores, NEGATIVE)


def local(
    media,
    latents,
    patch_rows,
    image_count,
    cotangent,
    w_query,
    w_key,
    w_value,
    w_out,
    w_up,
    w_down,
    norm_gains,
    norm_shifts,
):
    images = patch_rows.shape[0]
    width = media.shape[1]
    heads_here = w_query.shape[2] // HEAD_DIM
    layers = w_query.shape[0]
    keys_len = PATCH + LATENTS
    key_mask = jnp.concatenate(
        [
            jnp.arange(PATCH, dtype=jnp.int32)[None, :] < patch_rows[:, None],
            jnp.ones((images, LATENTS), bool),
        ],
        1,
    )
    live = (jnp.arange(images, dtype=jnp.int32) < image_count[0]).astype(jnp.float32)
    live_rows = jnp.repeat(live, LATENTS)[:, None]
    media_full = media.astype(jnp.float32)
    state = latents.astype(jnp.float32)
    saved = []
    for layer in range(layers):
        gathered = (
            lax.all_gather(w_query[layer], "dp", axis=0, tiled=True),
            lax.all_gather(w_key[layer], "dp", axis=0, tiled=True),
            lax.all_gather(w_value[layer], "dp", axis=0, tiled=True),
            lax.all_gather(w_out[layer], "dp", axis=1, tiled=True),
            lax.all_gather(w_up[layer], "dp", axis=0, tiled=True),
            lax.all_gather(w_down[layer], "dp", axis=1, tiled=True),
            lax.all_gather(norm_gains[layer], "dp", axis=1, tiled=True),
            lax.all_gather(norm_shifts[layer], "dp", axis=1, tiled=True),
        )
        full_query, full_key, full_value, full_out, full_up, full_down, gain_rows, shift_rows = (
            gathered
        )
        gains = gain_rows.astype(jnp.float32)
        shifts = shift_rows.astype(jnp.float32)
        media_low = normalize(media_full, gains[0], shifts[0]).astype(jnp.bfloat16)
        latent_low = normalize(state, gains[1], shifts[1]).astype(jnp.bfloat16)
        query = product(latent_low, full_query).astype(jnp.bfloat16)
        joined = jnp.concatenate(
            [media_low.reshape(images, PATCH, width), latent_low.reshape(images, LATENTS, width)], 1
        ).reshape(images * keys_len, width)
        keys = product(joined, full_key).astype(jnp.bfloat16)
        values = product(joined, full_value).astype(jnp.bfloat16)
        scores = key_scores(
            query.reshape(images, LATENTS, heads_here, HEAD_DIM),
            keys.reshape(images, keys_len, heads_here, HEAD_DIM),
            key_mask,
        )
        top = jnp.max(scores, -1, keepdims=True)
        expo = jnp.exp(scores - top)
        total = jnp.sum(expo, -1, keepdims=True)
        probs_low = (expo / total).astype(jnp.bfloat16)
        log_total = top + jnp.log(total)
        mixed = jnp.einsum(
            "ihqk,ikhd->iqhd",
            probs_low,
            values.reshape(images, keys_len, heads_here, HEAD_DIM),
            preferred_element_type=jnp.float32,
        )
        mixed_low = mixed.astype(jnp.bfloat16).reshape(images * LATENTS, heads_here * HEAD_DIM)
        middle = state + forward_reduce(product(mixed_low, full_out))
        hidden_low = normalize(middle, gains[2], shifts[2]).astype(jnp.bfloat16)
        pre_act = product(hidden_low, full_up)
        act_low = jax.nn.gelu(pre_act, approximate=False).astype(jnp.bfloat16)
        kept_weights = None
        saved.append(
            (
                kept_weights,
                state,
                latent_low,
                joined,
                query,
                keys,
                values,
                log_total,
                mixed_low,
                middle,
                hidden_low,
                pre_act,
                act_low,
            )
        )
        state = middle + forward_reduce(product(act_low, full_down))
    result = (state * live_rows).astype(jnp.bfloat16)
    grad_state = cotangent.astype(jnp.float32) * live_rows
    media_part = jnp.zeros_like(media_full)
    grads = [None] * layers
    for layer in reversed(range(layers)):
        (
            kept_weights,
            state_in,
            latent_low,
            joined,
            query,
            keys,
            values,
            log_total,
            mixed_low,
            middle,
            hidden_low,
            pre_act,
            act_low,
        ) = saved[layer]
        weights_now = (
            lax.all_gather(w_query[layer], "dp", axis=0, tiled=True),
            lax.all_gather(w_key[layer], "dp", axis=0, tiled=True),
            lax.all_gather(w_value[layer], "dp", axis=0, tiled=True),
            lax.all_gather(w_out[layer], "dp", axis=1, tiled=True),
            lax.all_gather(w_up[layer], "dp", axis=0, tiled=True),
            lax.all_gather(w_down[layer], "dp", axis=1, tiled=True),
            lax.all_gather(norm_gains[layer], "dp", axis=1, tiled=True),
            lax.all_gather(norm_shifts[layer], "dp", axis=1, tiled=True),
        )
        full_query, full_key, full_value, full_out, full_up, full_down, gain_rows, shift_rows = (
            weights_now
        )
        gains = gain_rows.astype(jnp.float32)
        shifts = shift_rows.astype(jnp.float32)
        down_low = grad_state.astype(jnp.bfloat16)
        grad_down = outer_sum(act_low, down_low)
        grad_act = back_product(down_low, full_down)
        unused, gelu_pull = jax.vjp(partial(jax.nn.gelu, approximate=False), pre_act)
        up_low = gelu_pull(grad_act)[0].astype(jnp.bfloat16)
        grad_up = outer_sum(hidden_low, up_low)
        grad_hidden = backward_reduce(back_product(up_low, full_up))
        unused, norm_pull = jax.vjp(normalize, middle, gains[2], shifts[2])
        grad_middle, gain_feed, shift_feed = norm_pull(grad_hidden)
        grad_middle = grad_middle + grad_state
        out_low = grad_middle.astype(jnp.bfloat16)
        grad_out = outer_sum(mixed_low, out_low)
        grad_mixed = (
            back_product(out_low, full_out)
            .astype(jnp.bfloat16)
            .reshape(images, LATENTS, heads_here, HEAD_DIM)
        )
        query_heads = query.reshape(images, LATENTS, heads_here, HEAD_DIM)
        key_heads = keys.reshape(images, keys_len, heads_here, HEAD_DIM)
        value_heads = values.reshape(images, keys_len, heads_here, HEAD_DIM)
        probs = jnp.exp(key_scores(query_heads, key_heads, key_mask) - log_total)
        probs_low = probs.astype(jnp.bfloat16)
        grad_probs = jnp.einsum(
            "iqhd,ikhd->ihqk", grad_mixed, value_heads, preferred_element_type=jnp.float32
        )
        grad_scores = (
            probs * (grad_probs - jnp.sum(grad_probs * probs, -1, keepdims=True))
        ).astype(jnp.bfloat16)
        grad_values = jnp.einsum(
            "ihqk,iqhd->ikhd", probs_low, grad_mixed, preferred_element_type=jnp.float32
        ).astype(jnp.bfloat16)
        grad_query = (
            jnp.einsum(
                "ihqk,ikhd->iqhd", grad_scores, key_heads, preferred_element_type=jnp.float32
            )
            * 0.125
        ).astype(jnp.bfloat16)
        grad_keys = (
            jnp.einsum(
                "ihqk,iqhd->ikhd", grad_scores, query_heads, preferred_element_type=jnp.float32
            )
            * 0.125
        ).astype(jnp.bfloat16)
        grad_query = grad_query.reshape(images * LATENTS, heads_here * HEAD_DIM)
        grad_keys = grad_keys.reshape(images * keys_len, heads_here * HEAD_DIM)
        grad_values = grad_values.reshape(images * keys_len, heads_here * HEAD_DIM)
        grad_wq = outer_sum(latent_low, grad_query)
        grad_wk = outer_sum(joined, grad_keys)
        grad_wv = outer_sum(joined, grad_values)
        grad_joined = (
            back_product(grad_keys, full_key) + back_product(grad_values, full_value)
        ).reshape(images, keys_len, width)
        grad_latent = backward_reduce(
            back_product(grad_query, full_query)
            + grad_joined[:, PATCH:].reshape(images * LATENTS, width)
        )
        unused, norm_pull = jax.vjp(normalize, state_in, gains[1], shifts[1])
        grad_in, gain_latent, shift_latent = norm_pull(grad_latent)
        grad_state = grad_middle + grad_in
        unused, media_pull = jax.vjp(normalize, media_full, gains[0], shifts[0])
        grad_media_layer, gain_media, shift_media = media_pull(
            grad_joined[:, :PATCH].reshape(images * PATCH, width)
        )
        media_part = media_part + grad_media_layer
        grads[layer] = (
            grad_wq,
            grad_wk,
            grad_wv,
            grad_out,
            grad_up,
            grad_down,
            gain_media,
            shift_media,
            gain_latent,
            shift_latent,
            gain_feed,
            shift_feed,
        )
    media_total, gain_media_all, shift_media_all = (
        lax.psum(media_part.astype(jnp.bfloat16), "mp").astype(jnp.float32),
        lax.psum(jnp.stack([g[6] for g in grads]).astype(jnp.bfloat16), "mp").astype(jnp.float32),
        lax.psum(jnp.stack([g[7] for g in grads]).astype(jnp.bfloat16), "mp").astype(jnp.float32),
    )
    gain_stack = jnp.stack(
        [jnp.stack([gain_media_all[layer], grads[layer][8]]) for layer in range(layers)]
    )
    shift_stack = jnp.stack(
        [jnp.stack([shift_media_all[layer], grads[layer][9]]) for layer in range(layers)]
    )
    feed_stack = jnp.stack(
        [jnp.stack([grads[layer][10], grads[layer][11]]) for layer in range(layers)]
    )
    summed = (
        lax.psum_scatter(jnp.stack([g[0] for g in grads]), "dp", scatter_dimension=1, tiled=True),
        lax.psum_scatter(jnp.stack([g[1] for g in grads]), "dp", scatter_dimension=1, tiled=True),
        lax.psum_scatter(jnp.stack([g[2] for g in grads]), "dp", scatter_dimension=1, tiled=True),
        lax.psum_scatter(jnp.stack([g[3] for g in grads]), "dp", scatter_dimension=2, tiled=True),
        lax.psum_scatter(jnp.stack([g[4] for g in grads]), "dp", scatter_dimension=1, tiled=True),
        lax.psum_scatter(jnp.stack([g[5] for g in grads]), "dp", scatter_dimension=2, tiled=True),
        lax.psum_scatter(gain_stack, "dp", scatter_dimension=2, tiled=True),
        lax.psum_scatter(shift_stack, "dp", scatter_dimension=2, tiled=True),
        lax.psum_scatter(feed_stack, "dp", scatter_dimension=2, tiled=True),
    )
    return (
        result,
        media_total,
        grad_state,
        summed[0],
        summed[1],
        summed[2],
        summed[3],
        summed[4],
        summed[5],
        summed[6],
        summed[7],
        summed[8],
    )


MESH = pl.DeviceIdType.MESH
F32 = jnp.float32
BF16 = jnp.bfloat16
SLOTS = 3
HEADS_HERE = 4
PLANE = 4
ROWS = SLOTS * LATENTS
HALF = ROWS // 2
WIDTH = 1024
KEYS = PATCH + LATENTS
HEAD_COLS = HEADS_HERE * HEAD_DIM
UNITS = 512
COPIES = 200


class Copies:
    def __init__(self, send_sems, recv_sems):
        self.send_sems, self.recv_sems = send_sems, recv_sems
        self.used = 0
        self.sending = []

    def start(self, source, target, device):
        copy = pltpu.make_async_remote_copy(
            src_ref=source,
            dst_ref=target,
            send_sem=self.send_sems.at[self.used],
            recv_sem=self.recv_sems.at[self.used],
            device_id=device,
            device_id_type=MESH,
        )
        self.used += 1
        copy.start()
        self.sending.append(copy)
        return copy

    def sent(self, copies):
        for copy in copies:
            copy.wait_send()
            self.sending = [kept for kept in self.sending if kept is not copy]


def matmul(left, right):
    return jnp.dot(left, right, preferred_element_type=F32)


def matmul_nt(left, right):
    return lax.dot_general(left, right, (((1,), (1,)), ((), ())), preferred_element_type=F32)


def matmul_tn(left, right):
    return lax.dot_general(left, right, (((0,), (0,)), ((), ())), preferred_element_type=F32)


def loop(count, body):
    def step(index, carry):
        body(index)
        return carry

    lax.fori_loop(0, count, step, 0)


def centred(values):
    centre = values - jnp.mean(values, -1, keepdims=True)
    scale = lax.rsqrt(jnp.mean(centre * centre, -1, keepdims=True) + 1e-05)
    return centre * scale, scale


def norm_back(grad, gain, unit, scale):
    inner = grad * gain
    return scale * (
        inner
        - jnp.mean(inner, -1, keepdims=True)
        - unit * jnp.mean(inner * unit, -1, keepdims=True)
    )


def column_sums(values):
    return jnp.sum(values, 0, keepdims=True)


def fused_kernel(
    patch_rows,
    image_count,
    media,
    latents,
    cotangent,
    vectors,
    w_attn,
    w_up,
    w_down_t,
    out_latents,
    out_media,
    out_state,
    out_attn,
    out_up,
    out_down_t,
    out_vectors,
    AW,
    FW,
    VG,
    GS,
    J,
    X,
    Y,
    Q,
    KV,
    O,
    PR,
    H,
    GP,
    G,
    DY,
    DU,
    ZP,
    PS,
    PRECV,
    TS,
    TR,
    AS,
    AR,
    DX,
    DH,
    DV,
    DAB,
    DQ,
    DKV,
    RF1,
    RF2,
    RF3,
    RA1A,
    RA1B,
    RA2A,
    RA2B,
    RA3,
    RA4,
    VS,
    VR,
    MASK,
    send_sems,
    recv_sems,
    local_sems,
):
    me = lax.axis_index("dp")
    half = lax.axis_index("mp")
    z, c = me // 4, me % 4
    zh, zl = z // 2, z % 2
    y, x = c // 2, c % 2
    columns = (c, y * 2 + 1 - x, (1 - y) * 2 + x, 3 - c)
    plane = tuple((z * 4 + column, half) for column in columns)
    near = ((zh * 2 + 1 - zl) * 4 + c, half)
    far = (((1 - zh) * 2 + zl) * 4 + c, half)
    sibling = (me, 1 - half)
    copies = Copies(send_sems, recv_sems)
    mine = pl.ds(pl.multiple_of(half * HALF, 32), HALF)
    other = pl.ds(pl.multiple_of((1 - half) * HALF, 32), HALF)
    first = jnp.where(half == 0, 1.0, 0.0).astype(F32)

    barrier = pltpu.get_barrier_semaphore()
    for step in range(1, 16):
        pl.semaphore_signal(barrier, inc=1, device_id=((me + step) % 16, half), device_id_type=MESH)
    pl.semaphore_signal(barrier, inc=1, device_id=sibling, device_id_type=MESH)
    pl.semaphore_wait(barrier, 16)


    def unit_columns(index):
        return pl.ds(pl.multiple_of(columns[index] * UNITS, UNITS), UNITS)

    vector_copies = [
        copies.start(vectors, VG.at[me], ((me + step) % 16, half)) for step in range(1, 16)
    ]
    local_copies = []
    for layer in range(2):
        for index, (source, target) in enumerate(
            (
                (w_attn.at[layer], AW.at[layer, zh, zl, y, x]),
                (w_up.at[layer, :, unit_columns(0)], FW.at[layer, zh, zl, c, :, 0:UNITS]),
                (w_down_t.at[layer, :, unit_columns(0)], FW.at[layer, zh, zl, c, :, UNITS:]),
            )
        ):
            copy = pltpu.make_async_copy(source, target, local_sems.at[layer * 3 + index])
            copy.start()
            local_copies.append(copy)

    def feed_scatter(layer):
        started = []
        for source, part in ((w_up, pl.ds(0, UNITS)), (w_down_t, pl.ds(UNITS, UNITS))):
            for index in (1, 2, 3):
                started.append(
                    copies.start(
                        source.at[layer, :, unit_columns(index)],
                        FW.at[layer, zh, zl, c, :, part],
                        plane[index],
                    )
                )
        return started

    def feed_far(layer, part):
        block = FW.at[layer, zh, zl, :, :, part]
        return copies.start(block, block, far)

    def feed_near(layer, part):
        block = FW.at[layer, :, zl, :, :, part]
        return copies.start(block, block, near)

    def attn_far(layer):
        return copies.start(w_attn.at[layer], AW.at[layer, zh, zl, y, x], far)

    def attn_near(layer):
        block = AW.at[layer, :, zl, y, x]
        return copies.start(block, block, near)

    def attn_plane_first(layer):
        block_a = AW.at[layer, :, :, y, x, :, 0:512]
        block_b = AW.at[layer, :, :, y, x, :, 512:]
        return [copies.start(block_a, block_a, plane[1]), copies.start(block_b, block_b, plane[2])]

    def attn_plane_second(layer):
        block_a = AW.at[layer, :, :, y, :, :, 0:512]
        block_b = AW.at[layer, :, :, :, x, :, 512:]
        return [copies.start(block_a, block_a, plane[2]), copies.start(block_b, block_b, plane[1])]

    def arrived(started):
        for copy in started if isinstance(started, list) else [started]:
            copy.wait_recv()

    up_part, down_part = pl.ds(0, UNITS), pl.ds(UNITS, UNITS)
    attn0 = attn_far(0)
    scatter0 = feed_scatter(0)

    head_row = lax.broadcasted_iota(jnp.int32, (HEAD_COLS, HEAD_COLS), 0) // HEAD_DIM
    head_column = lax.broadcasted_iota(jnp.int32, (HEAD_COLS, HEAD_COLS), 1) // HEAD_DIM
    MASK[...] = jnp.where(head_row == head_column, 1.0, 0.0).astype(F32)
    VG[me] = vectors[...]
    VS[...] = jnp.zeros_like(VS)

    def load_state(slot):
        rows = pl.ds(pl.multiple_of(slot * LATENTS, LATENTS), LATENTS)
        X[0, rows, :] = latents[rows, :].astype(F32)
        live = jnp.where(slot < image_count[0], 1.0, 0.0).astype(F32)
        grad = cotangent[rows, :].astype(F32) * live
        DX[rows, :] = grad
        DY[1, 0, rows, :] = grad.astype(BF16)

    loop(SLOTS, load_state)
    arrived(vector_copies)
    for tile in range(8):
        GS[:, tile * 128 : tile * 128 + 128] = VG[2 * tile].astype(F32) + VG[2 * tile + 1].astype(F32)

    def gain(layer, which):
        return GS[layer * 3 + which : layer * 3 + which + 1, :]

    def shift(layer, which):
        return GS[6 + layer * 3 + which : 7 + layer * 3 + which, :]

    def media_norm(index):
        rows = pl.ds(pl.multiple_of(index * 64, 64), 64)
        unit, _ = centred(media[rows, :].astype(F32))
        slot, part = index // 4, index % 4
        keys = pl.ds(pl.multiple_of(part * 64, 64), 64)
        for layer in range(2):
            J[layer, slot, keys, :] = (unit * gain(layer, 0) + shift(layer, 0)).astype(BF16)

    def latent_norm(layer):
        def body(slot):
            rows = pl.ds(pl.multiple_of(slot * LATENTS, LATENTS), LATENTS)
            unit, _ = centred(X[layer, rows, :])
            J[layer, slot, PATCH:, :] = (unit * gain(layer, 1) + shift(layer, 1)).astype(BF16)

        loop(SLOTS, body)

    loop(4, media_norm)
    for copy in local_copies:
        copy.wait()
    arrived(attn0)
    attn0 = attn_near(0)
    loop(4, lambda index: media_norm(index + 4))
    arrived(scatter0)
    feed0_up = feed_far(0, up_part)
    arrived(attn0)
    attn0 = attn_plane_first(0)
    loop(4, lambda index: media_norm(index + 8))
    latent_norm(0)
    arrived(attn0)
    attn0 = attn_plane_second(0)
    arrived(feed0_up)
    feed0_up = feed_near(0, up_part)
    feed0_down = feed_far(0, down_part)
    scatter1 = feed_scatter(1)
    arrived(attn0)

    def attn_weight(layer, low, high):
        return AW[layer, :, :, :, :, :, low:high].reshape(WIDTH, high - low)

    def feed_weight(layer, low, high):
        return FW[layer, :, :, :, :, low:high].reshape(WIDTH, high - low)

    def stacked(value):
        return (jnp.concatenate([value.astype(F32)] * HEADS_HERE, 0) * MASK[...]).astype(BF16)

    def unstacked(value):
        return jnp.sum((value * MASK[...]).reshape(HEADS_HERE, LATENTS, HEAD_COLS), 0)

    def attention(layer):
        def body(slot):
            KV[layer, slot] = matmul(J[layer, slot], attn_weight(layer, 256, 768)).astype(BF16)
            query = matmul(J[layer, slot, PATCH:, :], attn_weight(layer, 0, 256)).astype(BF16)
            Q[layer, slot] = query
            scores = matmul_nt(stacked(query), KV[layer, slot, :, 0:256]) * 0.125
            key = lax.broadcasted_iota(jnp.int32, (HEAD_COLS, KEYS), 1)
            scores = jnp.where((key >= PATCH) | (key < patch_rows[slot]), scores, NEGATIVE)
            expo = jnp.exp(scores - jnp.max(scores, -1, keepdims=True))
            probs = expo / jnp.sum(expo, -1, keepdims=True)
            PR[layer, slot] = probs
            mixed = unstacked(matmul(probs.astype(BF16), KV[layer, slot, :, 256:512]))
            O[layer, slot] = mixed.astype(BF16)

        loop(SLOTS, body)
        AS[...] = matmul_nt(
            O[layer].reshape(ROWS, HEAD_COLS), attn_weight(layer, 768, 1024)
        ).astype(BF16)
        return copies.start(AS, AR, sibling)

    def after_attention(layer, exchange):
        arrived(exchange)

        def body(slot):
            rows = pl.ds(pl.multiple_of(slot * LATENTS, LATENTS), LATENTS)
            middle = X[layer, rows, :] + (AS[rows, :].astype(F32) + AR[rows, :].astype(F32))
            Y[layer, rows, :] = middle
            unit, _ = centred(middle)
            H[layer, 0, rows, :] = (unit * gain(layer, 2) + shift(layer, 2)).astype(BF16)

        loop(SLOTS, body)
        copies.sent([exchange])

    def spread(buffer, layer):
        block = buffer.at[layer, 0, mine]
        return [
            copies.start(block, buffer.at[layer, index, mine], plane[index]) for index in (1, 2, 3)
        ]

    def hand_over(buffer, layer, index, started):
        arrived(started[index - 1])
        block = buffer.at[layer, index, mine]
        return copies.start(block, block, sibling)

    def feed_forward(layer, compute, buffer, started, way):
        pair = [None] * 4
        away = []

        def send_away(index):
            arrived(pair[index])
            TS[index - 1] = (ZP[index, mine, :] + PRECV[way, index].astype(F32)).astype(BF16)
            away.append(copies.start(TS.at[index - 1], TR.at[way, index - 1], plane[index]))

        handed = [None] * 4
        for index in range(4):
            if index > 0:
                if index == 1:
                    handed[1] = hand_over(buffer, layer, 1, started)
                    handed[2] = hand_over(buffer, layer, 2, started)
                if index == 3:
                    handed[3] = hand_over(buffer, layer, 3, started)
                arrived(handed[index])
            compute(layer, index)
            PS[index] = ZP[index, other, :].astype(BF16)
            pair[index] = copies.start(PS.at[index], PRECV.at[way, index], sibling)
            if index >= 2:
                send_away(index - 1)
        send_away(3)
        arrived(pair[0])
        return pair, away + handed[1:]

    def feed_sum(way, pair, away):
        arrived(away[:3])
        total = ZP[0, mine, :] + PRECV[way, 0].astype(F32)
        for index in range(3):
            total = total + TR[way, index].astype(F32)
        copies.sent(pair + away)
        return total

    def forward_block(layer, index):
        pre_act = matmul(H[layer, index], feed_weight(layer, 0, UNITS))
        bell = 0.5 * (1.0 + lax.erf(pre_act * 0.7071067811865476))
        GP[layer, index] = bell + pre_act * jnp.exp(-0.5 * pre_act * pre_act) * 0.3989422804014327
        act = (pre_act * bell).astype(BF16)
        G[layer, index] = act
        ZP[index] = matmul_nt(act, feed_weight(layer, UNITS, 2 * UNITS))

    def backward_block(layer, index):
        grad_act = matmul(DY[layer, index], feed_weight(layer, UNITS, 2 * UNITS))
        up_low = (grad_act * GP[layer, index]).astype(BF16)
        DU[index] = up_low
        ZP[index] = matmul_nt(up_low, feed_weight(layer, 0, UNITS))

    exchange = attention(0)
    arrived(feed0_up)
    arrived(feed0_down)
    feed0_down = feed_near(0, down_part)
    attn1 = attn_far(1)
    after_attention(0, exchange)
    started = spread(H, 0)
    arrived(attn1)
    attn1 = attn_near(1)
    arrived(scatter1)
    feed1_up = feed_far(1, up_part)
    arrived(feed0_down)
    pair, away = feed_forward(0, forward_block, H, started, 0)
    arrived(attn1)
    attn1 = attn_plane_first(1)
    arrived(feed1_up)
    feed1_up = feed_near(1, up_part)
    feed1_down = feed_far(1, down_part)
    X[1, mine, :] = Y[0, mine, :] + feed_sum(0, pair, away)
    swap = copies.start(X.at[1, mine], X.at[1, mine], sibling)
    arrived(attn1)
    attn1 = attn_plane_second(1)
    arrived(swap)
    latent_norm(1)
    arrived(attn1)

    exchange = attention(1)
    arrived(feed1_up)
    arrived(feed1_down)
    feed1_down = feed_near(1, down_part)
    after_attention(1, exchange)
    started = spread(H, 1)
    grad_started = spread(DY, 1)
    arrived(feed1_down)
    pair, away = feed_forward(1, forward_block, H, started, 0)
    X[2, mine, :] = Y[1, mine, :] + feed_sum(0, pair, away)
    swap = copies.start(X.at[2, mine], X.at[2, mine], sibling)
    arrived(swap)

    def store_result(slot):
        rows = pl.ds(pl.multiple_of(slot * LATENTS, LATENTS), LATENTS)
        live = jnp.where(slot < image_count[0], 1.0, 0.0).astype(F32)
        out_latents[rows, :] = (X[2, rows, :] * live).astype(BF16)

    loop(SLOTS, store_result)

    def add_into(target, received):
        target[...] = (target[...].astype(F32) + received[...].astype(F32)).astype(BF16)

    def feed_grads(layer):
        def body(index):
            cols = pl.ds(pl.multiple_of(index * 256, 256), 256)
            for low, left, right in ((UNITS, DY, G.at[layer]), (0, H, DU)):
                product_ = matmul_tn(
                    left[layer, :, :, cols].reshape(4 * ROWS, 256),
                    right[...].reshape(4 * ROWS, UNITS),
                )
                FW[layer, index // 2, index % 2, :, :, low : low + UNITS] = product_.astype(
                    BF16
                ).reshape(4, 64, UNITS)

        loop(4, body)

    def feed_sum_near(layer, part):
        return copies.start(
            FW.at[layer, :, 1 - zl, :, :, part], RF1.at[layer, :, :, :, part], near
        )

    def feed_sum_far(layer, part, started):
        arrived(started)

        def body(index):
            add_into(FW.at[layer, index // 4, zl, index % 4, :, part], RF1.at[layer, index // 4, index % 4, :, part])

        loop(8, body)
        return copies.start(FW.at[layer, 1 - zh, zl, :, :, part], RF2.at[layer, :, :, part], far)

    def feed_sum_plane(layer, part, started):
        arrived(started)

        def body(index):
            add_into(FW.at[layer, zh, zl, index, :, part], RF2.at[layer, index, :, part])

        loop(4, body)
        return [
            copies.start(
                FW.at[layer, zh, zl, columns[index], :, part],
                RF3.at[layer, index - 1, :, part],
                plane[index],
            )
            for index in (1, 2, 3)
        ]

    def feed_sum_end(layer, part, target, started):
        target[layer, :, unit_columns(0)] = FW[layer, zh, zl, c, :, part].astype(F32)
        for index in (1, 2, 3):
            arrived(started[index - 1])
            target[layer, :, unit_columns(index)] = RF3[layer, index - 1, :, part].astype(F32)

    def attn_sum_first(layer):
        return [
            copies.start(AW.at[layer, :, :, 1 - y, :, :, 0:512], RA1A.at[layer], plane[2]),
            copies.start(AW.at[layer, :, :, :, 1 - x, :, 512:], RA1B.at[layer], plane[1]),
        ]

    def attn_sum_second(layer, started):
        arrived(started)

        def body(index):
            high, low = index // 2, index % 2
            for side in range(2):
                add_into(AW.at[layer, high, low, y, side, :, 0:512], RA1A.at[layer, high, low, side])
                add_into(AW.at[layer, high, low, side, x, :, 512:], RA1B.at[layer, high, low, side])

        loop(4, body)
        return [
            copies.start(AW.at[layer, :, :, y, 1 - x, :, 0:512], RA2A.at[layer], plane[1]),
            copies.start(AW.at[layer, :, :, 1 - y, x, :, 512:], RA2B.at[layer], plane[2]),
        ]

    def attn_sum_near(layer, started):
        arrived(started)

        def body(index):
            high, low = index // 2, index % 2
            add_into(AW.at[layer, high, low, y, x, :, 0:512], RA2A.at[layer, high, low])
            add_into(AW.at[layer, high, low, y, x, :, 512:], RA2B.at[layer, high, low])

        loop(4, body)
        return copies.start(AW.at[layer, :, 1 - zl, y, x], RA3.at[layer], near)

    def attn_sum_far(layer, started):
        arrived(started)
        for high in range(2):
            add_into(AW.at[layer, high, zl, y, x], RA3.at[layer, high])
        return copies.start(AW.at[layer, 1 - zh, zl, y, x], RA4.at[layer], far)

    def attn_sum_end(layer, started):
        arrived(started)
        out_attn[layer] = AW[layer, zh, zl, y, x].astype(F32) + RA4[layer].astype(F32)

    def swap_feed(layer, pair, away):
        DH[mine, :] = feed_sum(1, pair, away)
        swap = copies.start(DH.at[mine], DH.at[mine], sibling)
        arrived(swap)
        copies.sent([swap])

    def middle_back(layer):
        def body(slot, sums):
            rows = pl.ds(pl.multiple_of(slot * LATENTS, LATENTS), LATENTS)
            unit, scale = centred(Y[layer, rows, :])
            grad = DH[rows, :]
            grad_middle = DX[rows, :] + norm_back(grad, gain(layer, 2), unit, scale)
            DV[rows, :] = grad_middle
            DAB[rows, :] = grad_middle.astype(BF16)
            return sums[0] + column_sums(grad * unit), sums[1] + column_sums(grad)

        zero = jnp.zeros((1, WIDTH), F32)
        gain_sum, shift_sum = lax.fori_loop(0, SLOTS, body, (zero, zero))
        VS[8 + layer * 2 : 9 + layer * 2, :] = gain_sum * first
        VS[9 + layer * 2 : 10 + layer * 2, :] = shift_sum * first

    def attention_back(layer):
        def body(slot):
            rows = pl.ds(pl.multiple_of(slot * LATENTS, LATENTS), LATENTS)
            grad_mixed = matmul(DAB[rows, :], attn_weight(layer, 768, 1024)).astype(BF16)
            grads = stacked(grad_mixed)
            probs = PR[layer, slot]
            grad_probs = matmul_nt(grads, KV[layer, slot, :, 256:512])
            grad_scores = (
                probs * (grad_probs - jnp.sum(grad_probs * probs, -1, keepdims=True))
            ).astype(BF16)
            DKV[slot, :, 256:512] = matmul_tn(probs.astype(BF16), grads).astype(BF16)
            queries = stacked(Q[layer, slot])
            DKV[slot, :, 0:256] = (matmul_tn(grad_scores, queries) * 0.125).astype(BF16)
            DQ[slot] = (
                unstacked(matmul(grad_scores, KV[layer, slot, :, 0:256])) * 0.125
            ).astype(BF16)
            AS[rows, :] = (
                matmul_nt(DQ[slot], attn_weight(layer, 0, 256))
                + matmul_nt(DKV[slot, PATCH:, :], attn_weight(layer, 256, 768))
            ).astype(BF16)

        loop(SLOTS, body)
        return copies.start(AS, AR, sibling)

    def state_back(layer, exchange):
        arrived(exchange)

        def body(slot, sums):
            rows = pl.ds(pl.multiple_of(slot * LATENTS, LATENTS), LATENTS)
            unit, scale = centred(X[layer, rows, :])
            grad = AS[rows, :].astype(F32) + AR[rows, :].astype(F32)
            grad_in = DV[rows, :] + norm_back(grad, gain(layer, 1), unit, scale)
            if layer > 0:
                DX[rows, :] = grad_in
                DY[layer - 1, 0, rows, :] = grad_in.astype(BF16)
            else:
                out_state[rows, :] = grad_in
            return sums[0] + column_sums(grad * unit), sums[1] + column_sums(grad)

        zero = jnp.zeros((1, WIDTH), F32)
        gain_sum, shift_sum = lax.fori_loop(0, SLOTS, body, (zero, zero))
        VS[layer * 2 + 1 : layer * 2 + 2, :] = gain_sum * first
        VS[layer * 2 + 5 : layer * 2 + 6, :] = shift_sum * first
        copies.sent([exchange])

    def media_back(layer):
        def body(index, sums):
            slot, part = index // 2, index % 2
            keys = pl.ds(pl.multiple_of(part * 128, 128), 128)
            rows = pl.ds(pl.multiple_of(index * 128, 128), 128)
            grad = matmul_nt(DKV[slot, keys, :], attn_weight(layer, 256, 768))
            unit, scale = centred(media[rows, :].astype(F32))
            piece = norm_back(grad, gain(layer, 0), unit, scale)
            if layer == 1:
                out_media[rows, :] = piece
            else:
                out_media[rows, :] = out_media[rows, :] + piece
            return sums[0] + column_sums(grad * unit), sums[1] + column_sums(grad)

        zero = jnp.zeros((1, WIDTH), F32)
        gain_sum, shift_sum = lax.fori_loop(0, 6, body, (zero, zero))
        VS[layer * 2 : layer * 2 + 1, :] = gain_sum
        VS[layer * 2 + 4 : layer * 2 + 5, :] = shift_sum

    def attn_grads(layer):
        def body(index):
            cols = pl.ds(pl.multiple_of(index * 256, 256), 256)
            high, low = index // 2, index % 2
            query_part = matmul_tn(
                J[layer, :, PATCH:, cols].reshape(ROWS, 256), DQ[...].reshape(ROWS, HEAD_COLS)
            )
            AW[layer, high, low, :, :, :, 0:256] = query_part.astype(BF16).reshape(2, 2, 64, 256)
            key_part = matmul_tn(
                J[layer, :, :, cols].reshape(SLOTS * KEYS, 256), DKV[...].reshape(SLOTS * KEYS, 512)
            )
            AW[layer, high, low, :, :, :, 256:768] = key_part.astype(BF16).reshape(2, 2, 64, 512)
            out_part = matmul_tn(DAB[:, cols], O[layer].reshape(ROWS, HEAD_COLS))
            AW[layer, high, low, :, :, :, 768:1024] = out_part.astype(BF16).reshape(2, 2, 64, 256)

        loop(4, body)

    copies.sent(list(copies.sending))
    pair, away = feed_forward(1, backward_block, DY, grad_started, 1)
    feed_grads(1)
    down1 = feed_sum_near(1, down_part)
    up1 = feed_sum_near(1, up_part)
    swap_feed(1, pair, away)
    middle_back(1)
    exchange = attention_back(1)
    down1 = feed_sum_far(1, down_part, down1)
    state_back(1, exchange)
    started = spread(DY, 0)
    media_back(1)
    attn_grads(1)
    attn1 = attn_sum_first(1)
    up1 = feed_sum_far(1, up_part, up1)

    pair, away = feed_forward(0, backward_block, DY, started, 1)
    down1 = feed_sum_plane(1, down_part, down1)
    attn1 = attn_sum_second(1, attn1)
    feed_grads(0)
    down0 = feed_sum_near(0, down_part)
    up0 = feed_sum_near(0, up_part)
    swap_feed(0, pair, away)
    middle_back(0)
    exchange = attention_back(0)
    up1 = feed_sum_plane(1, up_part, up1)
    attn1 = attn_sum_near(1, attn1)
    down0 = feed_sum_far(0, down_part, down0)
    state_back(0, exchange)
    media_back(0)
    attn_grads(0)
    attn0 = attn_sum_first(0)

    vector_sums = [
        copies.start(
            VS.at[:, pl.ds(pl.multiple_of((((me + step) % 16) // 2) * 128, 128), 128)],
            VR.at[step],
            ((me + step) % 16, half),
        )
        for step in range(1, 16)
    ]

    def media_low(index):
        rows = pl.ds(pl.multiple_of(index * 192, 192), 192)
        DY[1, index] = out_media[rows, :].astype(BF16)

    loop(4, media_low)
    media_swap = copies.start(DY.at[1], H.at[1], sibling)
    attn1 = attn_sum_far(1, attn1)
    up0 = feed_sum_far(0, up_part, up0)
    feed_sum_end(1, down_part, out_down_t, down1)
    feed_sum_end(1, up_part, out_up, up1)
    attn0 = attn_sum_second(0, attn0)
    attn_sum_end(1, attn1)
    down0 = feed_sum_plane(0, down_part, down0)
    arrived(media_swap)

    def media_sum(index):
        rows = pl.ds(pl.multiple_of(index * 192, 192), 192)
        out_media[rows, :] = DY[1, index].astype(F32) + H[1, index].astype(F32)

    loop(4, media_sum)
    attn0 = attn_sum_near(0, attn0)
    up0 = feed_sum_plane(0, up_part, up0)
    arrived(vector_sums)
    total = VS[:, pl.ds(pl.multiple_of((me // 2) * 128, 128), 128)]
    for step in range(1, 16):
        total = total + VR[step]
    VR[0] = total
    vector_swap = copies.start(VR.at[0], VR.at[16], sibling)
    attn0 = attn_sum_far(0, attn0)
    feed_sum_end(0, down_part, out_down_t, down0)
    feed_sum_end(0, up_part, out_up, up0)
    arrived(vector_swap)
    out_vectors[...] = VR[0] + VR[16]
    attn_sum_end(0, attn0)
    copies.sent(list(copies.sending))


def fused(media, latents, patch_rows, image_count, cotangent, w_query, w_key, w_value, w_out, w_up, w_down, norm_gains, norm_shifts):
    w_attn = jnp.concatenate([w_query, w_key, w_value, jnp.swapaxes(w_out, 1, 2)], 2)
    w_down_t = jnp.swapaxes(w_down, 1, 2)
    piece = norm_gains.shape[2]
    vectors = jnp.concatenate([norm_gains.reshape(6, piece), norm_shifts.reshape(6, piece)], 0)
    vectors = jnp.pad(vectors, ((0, 4), (0, 0)))
    odd = lax.axis_index("dp") % 2 == 1
    blank = jnp.zeros_like(vectors)
    vectors = jnp.concatenate([jnp.where(odd, blank, vectors), jnp.where(odd, vectors, blank)], 1)

    vmem = pl.BlockSpec(memory_space=pltpu.VMEM)
    smem = pl.BlockSpec(memory_space=pltpu.SMEM)
    anywhere = pl.BlockSpec(memory_space=pl.ANY)

    def shape(dims, kind):
        return jax.ShapeDtypeStruct(dims, kind)

    results = pl.pallas_call(
        fused_kernel,
        name="resampler",
        out_shape=[
            shape((ROWS, WIDTH), BF16),
            shape((SLOTS * PATCH, WIDTH), F32),
            shape((ROWS, WIDTH), F32),
            shape((2, 64, WIDTH), F32),
            shape((2, 64, 4 * UNITS), F32),
            shape((2, 64, 4 * UNITS), F32),
            shape((16, 128), F32),
        ],
        in_specs=[smem, smem, vmem, vmem, vmem, vmem, anywhere, anywhere, anywhere],
        out_specs=[vmem] * 7,
        scratch_shapes=[
            pltpu.VMEM((2, 2, 2, 2, 2, 64, 1024), BF16),
            pltpu.VMEM((2, 2, 2, 4, 64, 1024), BF16),
            pltpu.VMEM((16, 16, 128), BF16),
            pltpu.VMEM((16, WIDTH), F32),
            pltpu.VMEM((2, SLOTS, KEYS, WIDTH), BF16),
            pltpu.VMEM((3, ROWS, WIDTH), F32),
            pltpu.VMEM((2, ROWS, WIDTH), F32),
            pltpu.VMEM((2, SLOTS, LATENTS, HEAD_COLS), BF16),
            pltpu.VMEM((2, SLOTS, KEYS, 2 * HEAD_COLS), BF16),
            pltpu.VMEM((2, SLOTS, LATENTS, HEAD_COLS), BF16),
            pltpu.VMEM((2, SLOTS, HEAD_COLS, KEYS), F32),
            pltpu.VMEM((2, PLANE, ROWS, WIDTH), BF16),
            pltpu.VMEM((2, PLANE, ROWS, UNITS), F32),
            pltpu.VMEM((2, PLANE, ROWS, UNITS), BF16),
            pltpu.VMEM((2, PLANE, ROWS, WIDTH), BF16),
            pltpu.VMEM((PLANE, ROWS, UNITS), BF16),
            pltpu.VMEM((PLANE, ROWS, WIDTH), F32),
            pltpu.VMEM((PLANE, HALF, WIDTH), BF16),
            pltpu.VMEM((2, PLANE, HALF, WIDTH), BF16),
            pltpu.VMEM((3, HALF, WIDTH), BF16),
            pltpu.VMEM((2, 3, HALF, WIDTH), BF16),
            pltpu.VMEM((ROWS, WIDTH), BF16),
            pltpu.VMEM((ROWS, WIDTH), BF16),
            pltpu.VMEM((ROWS, WIDTH), F32),
            pltpu.VMEM((ROWS, WIDTH), F32),
            pltpu.VMEM((ROWS, WIDTH), F32),
            pltpu.VMEM((ROWS, WIDTH), BF16),
            pltpu.VMEM((SLOTS, LATENTS, HEAD_COLS), BF16),
            pltpu.VMEM((SLOTS, KEYS, 2 * HEAD_COLS), BF16),
            pltpu.VMEM((2, 2, 4, 64, 1024), BF16),
            pltpu.VMEM((2, 4, 64, 1024), BF16),
            pltpu.VMEM((2, 3, 64, 1024), BF16),
            pltpu.VMEM((2, 2, 2, 2, 64, 512), BF16),
            pltpu.VMEM((2, 2, 2, 2, 64, 512), BF16),
            pltpu.VMEM((2, 2, 2, 64, 512), BF16),
            pltpu.VMEM((2, 2, 2, 64, 512), BF16),
            pltpu.VMEM((2, 2, 64, 1024), BF16),
            pltpu.VMEM((2, 64, 1024), BF16),
            pltpu.VMEM((16, WIDTH), F32),
            pltpu.VMEM((17, 16, 128), F32),
            pltpu.VMEM((HEAD_COLS, HEAD_COLS), F32),
            pltpu.SemaphoreType.DMA((COPIES,)),
            pltpu.SemaphoreType.DMA((COPIES,)),
            pltpu.SemaphoreType.DMA((6,)),
        ],
        compiler_params=pltpu.CompilerParams(
            collective_id=0, has_side_effects=True, vmem_limit_bytes=66 * 2**20 - 2**21
        ),
        cost_estimate=pl.CostEstimate(flops=18 * 10**9, bytes_accessed=20 * 10**6, transcendentals=10**6),
    )(patch_rows, image_count, media, latents, cotangent, vectors, w_attn, w_up, w_down_t)
    out_latents, out_media, out_state, attn, up, down_t, sums = results
    sums = jnp.where(odd, sums[:, piece:], sums[:, :piece])
    return (
        out_latents,
        out_media,
        out_state,
        attn[:, :, 0:256],
        attn[:, :, 256:512],
        attn[:, :, 512:768],
        jnp.swapaxes(attn[:, :, 768:], 1, 2),
        up,
        jnp.swapaxes(down_t, 1, 2),
        sums[0:4].reshape(2, 2, piece),
        sums[4:8].reshape(2, 2, piece),
        sums[8:12].reshape(2, 2, piece),
    )


def solution(mesh):
    body = fused if (mesh.shape["dp"], mesh.shape["mp"]) == (16, 2) else local
    placed = (
        P("dp", None),
        P("dp", None),
        P("dp"),
        P("dp"),
        P("dp", None),
        P(None, "dp", "mp"),
        P(None, "dp", "mp"),
        P(None, "dp", "mp"),
        P(None, "mp", "dp"),
        P(None, "dp", "mp"),
        P(None, "mp", "dp"),
        P(None, None, "dp"),
        P(None, None, "dp"),
    )
    return jax.shard_map(
        body,
        mesh=mesh,
        in_specs=placed,
        out_specs=(
            P("dp", None),
            P("dp", None),
            P("dp", None),
            P(None, "dp", "mp"),
            P(None, "dp", "mp"),
            P(None, "dp", "mp"),
            P(None, "mp", "dp"),
            P(None, "dp", "mp"),
            P(None, "mp", "dp"),
            P(None, None, "dp"),
            P(None, None, "dp"),
            P(None, None, "dp"),
        ),
        check_vma=False,
    )
```

```python
from functools import partial

import jax
import jax.numpy as jnp
from jax import lax
from jax.experimental import pallas as pl
from jax.experimental.pallas import tpu as pltpu
from jax.sharding import PartitionSpec as P

HEAD_DIM = 64
LATENTS = 64
PATCH = 256


NEGATIVE = -1000000000.0


def normalize(values, gain, shift):
    centre = values - jnp.mean(values, -1, keepdims=True)
    spread = jnp.mean(centre * centre, -1, keepdims=True)
    return centre * lax.rsqrt(spread + 1e-05) * gain + shift


def product(left, right):
    return jnp.dot(left, right, preferred_element_type=jnp.float32)


def outer_sum(left, right):
    return lax.dot_general(
        left, right, (((0,), (0,)), ((), ())), preferred_element_type=jnp.float32
    )


def back_product(left, right):
    return lax.dot_general(
        left, right, (((1,), (1,)), ((), ())), preferred_element_type=jnp.float32
    )


def forward_reduce(values):
    return lax.psum(values.astype(jnp.bfloat16), "mp").astype(jnp.float32)


def backward_reduce(values):
    return lax.psum(values.astype(jnp.bfloat16), "mp").astype(jnp.float32)


def key_scores(query_heads, key_heads, key_mask):
    scores = (
        jnp.einsum("iqhd,ikhd->ihqk", query_heads, key_heads, preferred_element_type=jnp.float32)
        * 0.125
    )
    return jnp.where(key_mask[:, None, None, :], scores, NEGATIVE)


def local(
    media,
    latents,
    patch_rows,
    image_count,
    cotangent,
    w_query,
    w_key,
    w_value,
    w_out,
    w_up,
    w_down,
    norm_gains,
    norm_shifts,
):
    images = patch_rows.shape[0]
    width = media.shape[1]
    heads_here = w_query.shape[2] // HEAD_DIM
    layers = w_query.shape[0]
    keys_len = PATCH + LATENTS
    key_mask = jnp.concatenate(
        [
            jnp.arange(PATCH, dtype=jnp.int32)[None, :] < patch_rows[:, None],
            jnp.ones((images, LATENTS), bool),
        ],
        1,
    )
    live = (jnp.arange(images, dtype=jnp.int32) < image_count[0]).astype(jnp.float32)
    live_rows = jnp.repeat(live, LATENTS)[:, None]
    media_full = media.astype(jnp.float32)
    state = latents.astype(jnp.float32)
    saved = []
    for layer in range(layers):
        gathered = (
            lax.all_gather(w_query[layer], "dp", axis=0, tiled=True),
            lax.all_gather(w_key[layer], "dp", axis=0, tiled=True),
            lax.all_gather(w_value[layer], "dp", axis=0, tiled=True),
            lax.all_gather(w_out[layer], "dp", axis=1, tiled=True),
            lax.all_gather(w_up[layer], "dp", axis=0, tiled=True),
            lax.all_gather(w_down[layer], "dp", axis=1, tiled=True),
            lax.all_gather(norm_gains[layer], "dp", axis=1, tiled=True),
            lax.all_gather(norm_shifts[layer], "dp", axis=1, tiled=True),
        )
        full_query, full_key, full_value, full_out, full_up, full_down, gain_rows, shift_rows = (
            gathered
        )
        gains = gain_rows.astype(jnp.float32)
        shifts = shift_rows.astype(jnp.float32)
        media_low = normalize(media_full, gains[0], shifts[0]).astype(jnp.bfloat16)
        latent_low = normalize(state, gains[1], shifts[1]).astype(jnp.bfloat16)
        query = product(latent_low, full_query).astype(jnp.bfloat16)
        joined = jnp.concatenate(
            [media_low.reshape(images, PATCH, width), latent_low.reshape(images, LATENTS, width)], 1
        ).reshape(images * keys_len, width)
        keys = product(joined, full_key).astype(jnp.bfloat16)
        values = product(joined, full_value).astype(jnp.bfloat16)
        scores = key_scores(
            query.reshape(images, LATENTS, heads_here, HEAD_DIM),
            keys.reshape(images, keys_len, heads_here, HEAD_DIM),
            key_mask,
        )
        top = jnp.max(scores, -1, keepdims=True)
        expo = jnp.exp(scores - top)
        total = jnp.sum(expo, -1, keepdims=True)
        probs_low = (expo / total).astype(jnp.bfloat16)
        log_total = top + jnp.log(total)
        mixed = jnp.einsum(
            "ihqk,ikhd->iqhd",
            probs_low,
            values.reshape(images, keys_len, heads_here, HEAD_DIM),
            preferred_element_type=jnp.float32,
        )
        mixed_low = mixed.astype(jnp.bfloat16).reshape(images * LATENTS, heads_here * HEAD_DIM)
        middle = state + forward_reduce(product(mixed_low, full_out))
        hidden_low = normalize(middle, gains[2], shifts[2]).astype(jnp.bfloat16)
        pre_act = product(hidden_low, full_up)
        act_low = jax.nn.gelu(pre_act, approximate=False).astype(jnp.bfloat16)
        kept_weights = None
        saved.append(
            (
                kept_weights,
                state,
                latent_low,
                joined,
                query,
                keys,
                values,
                log_total,
                mixed_low,
                middle,
                hidden_low,
                pre_act,
                act_low,
            )
        )
        state = middle + forward_reduce(product(act_low, full_down))
    result = (state * live_rows).astype(jnp.bfloat16)
    grad_state = cotangent.astype(jnp.float32) * live_rows
    media_part = jnp.zeros_like(media_full)
    grads = [None] * layers
    for layer in reversed(range(layers)):
        (
            kept_weights,
            state_in,
            latent_low,
            joined,
            query,
            keys,
            values,
            log_total,
            mixed_low,
            middle,
            hidden_low,
            pre_act,
            act_low,
        ) = saved[layer]
        weights_now = (
            lax.all_gather(w_query[layer], "dp", axis=0, tiled=True),
            lax.all_gather(w_key[layer], "dp", axis=0, tiled=True),
            lax.all_gather(w_value[layer], "dp", axis=0, tiled=True),
            lax.all_gather(w_out[layer], "dp", axis=1, tiled=True),
            lax.all_gather(w_up[layer], "dp", axis=0, tiled=True),
            lax.all_gather(w_down[layer], "dp", axis=1, tiled=True),
            lax.all_gather(norm_gains[layer], "dp", axis=1, tiled=True),
            lax.all_gather(norm_shifts[layer], "dp", axis=1, tiled=True),
        )
        full_query, full_key, full_value, full_out, full_up, full_down, gain_rows, shift_rows = (
            weights_now
        )
        gains = gain_rows.astype(jnp.float32)
        shifts = shift_rows.astype(jnp.float32)
        down_low = grad_state.astype(jnp.bfloat16)
        grad_down = outer_sum(act_low, down_low)
        grad_act = back_product(down_low, full_down)
        unused, gelu_pull = jax.vjp(partial(jax.nn.gelu, approximate=False), pre_act)
        up_low = gelu_pull(grad_act)[0].astype(jnp.bfloat16)
        grad_up = outer_sum(hidden_low, up_low)
        grad_hidden = backward_reduce(back_product(up_low, full_up))
        unused, norm_pull = jax.vjp(normalize, middle, gains[2], shifts[2])
        grad_middle, gain_feed, shift_feed = norm_pull(grad_hidden)
        grad_middle = grad_middle + grad_state
        out_low = grad_middle.astype(jnp.bfloat16)
        grad_out = outer_sum(mixed_low, out_low)
        grad_mixed = (
            back_product(out_low, full_out)
            .astype(jnp.bfloat16)
            .reshape(images, LATENTS, heads_here, HEAD_DIM)
        )
        query_heads = query.reshape(images, LATENTS, heads_here, HEAD_DIM)
        key_heads = keys.reshape(images, keys_len, heads_here, HEAD_DIM)
        value_heads = values.reshape(images, keys_len, heads_here, HEAD_DIM)
        probs = jnp.exp(key_scores(query_heads, key_heads, key_mask) - log_total)
        probs_low = probs.astype(jnp.bfloat16)
        grad_probs = jnp.einsum(
            "iqhd,ikhd->ihqk", grad_mixed, value_heads, preferred_element_type=jnp.float32
        )
        grad_scores = (
            probs * (grad_probs - jnp.sum(grad_probs * probs, -1, keepdims=True))
        ).astype(jnp.bfloat16)
        grad_values = jnp.einsum(
            "ihqk,iqhd->ikhd", probs_low, grad_mixed, preferred_element_type=jnp.float32
        ).astype(jnp.bfloat16)
        grad_query = (
            jnp.einsum(
                "ihqk,ikhd->iqhd", grad_scores, key_heads, preferred_element_type=jnp.float32
            )
            * 0.125
        ).astype(jnp.bfloat16)
        grad_keys = (
            jnp.einsum(
                "ihqk,iqhd->ikhd", grad_scores, query_heads, preferred_element_type=jnp.float32
            )
            * 0.125
        ).astype(jnp.bfloat16)
        grad_query = grad_query.reshape(images * LATENTS, heads_here * HEAD_DIM)
        grad_keys = grad_keys.reshape(images * keys_len, heads_here * HEAD_DIM)
        grad_values = grad_values.reshape(images * keys_len, heads_here * HEAD_DIM)
        grad_wq = outer_sum(latent_low, grad_query)
        grad_wk = outer_sum(joined, grad_keys)
        grad_wv = outer_sum(joined, grad_values)
        grad_joined = (
            back_product(grad_keys, full_key) + back_product(grad_values, full_value)
        ).reshape(images, keys_len, width)
        grad_latent = backward_reduce(
            back_product(grad_query, full_query)
            + grad_joined[:, PATCH:].reshape(images * LATENTS, width)
        )
        unused, norm_pull = jax.vjp(normalize, state_in, gains[1], shifts[1])
        grad_in, gain_latent, shift_latent = norm_pull(grad_latent)
        grad_state = grad_middle + grad_in
        unused, media_pull = jax.vjp(normalize, media_full, gains[0], shifts[0])
        grad_media_layer, gain_media, shift_media = media_pull(
            grad_joined[:, :PATCH].reshape(images * PATCH, width)
        )
        media_part = media_part + grad_media_layer
        grads[layer] = (
            grad_wq,
            grad_wk,
            grad_wv,
            grad_out,
            grad_up,
            grad_down,
            gain_media,
            shift_media,
            gain_latent,
            shift_latent,
            gain_feed,
            shift_feed,
        )
    media_total, gain_media_all, shift_media_all = (
        lax.psum(media_part.astype(jnp.bfloat16), "mp").astype(jnp.float32),
        lax.psum(jnp.stack([g[6] for g in grads]).astype(jnp.bfloat16), "mp").astype(jnp.float32),
        lax.psum(jnp.stack([g[7] for g in grads]).astype(jnp.bfloat16), "mp").astype(jnp.float32),
    )
    gain_stack = jnp.stack(
        [jnp.stack([gain_media_all[layer], grads[layer][8]]) for layer in range(layers)]
    )
    shift_stack = jnp.stack(
        [jnp.stack([shift_media_all[layer], grads[layer][9]]) for layer in range(layers)]
    )
    feed_stack = jnp.stack(
        [jnp.stack([grads[layer][10], grads[layer][11]]) for layer in range(layers)]
    )
    summed = (
        lax.psum_scatter(jnp.stack([g[0] for g in grads]), "dp", scatter_dimension=1, tiled=True),
        lax.psum_scatter(jnp.stack([g[1] for g in grads]), "dp", scatter_dimension=1, tiled=True),
        lax.psum_scatter(jnp.stack([g[2] for g in grads]), "dp", scatter_dimension=1, tiled=True),
        lax.psum_scatter(jnp.stack([g[3] for g in grads]), "dp", scatter_dimension=2, tiled=True),
        lax.psum_scatter(jnp.stack([g[4] for g in grads]), "dp", scatter_dimension=1, tiled=True),
        lax.psum_scatter(jnp.stack([g[5] for g in grads]), "dp", scatter_dimension=2, tiled=True),
        lax.psum_scatter(gain_stack, "dp", scatter_dimension=2, tiled=True),
        lax.psum_scatter(shift_stack, "dp", scatter_dimension=2, tiled=True),
        lax.psum_scatter(feed_stack, "dp", scatter_dimension=2, tiled=True),
    )
    return (
        result,
        media_total,
        grad_state,
        summed[0],
        summed[1],
        summed[2],
        summed[3],
        summed[4],
        summed[5],
        summed[6],
        summed[7],
        summed[8],
    )


MESH = pl.DeviceIdType.MESH
F32 = jnp.float32
BF16 = jnp.bfloat16
SLOTS = 3
HEADS_HERE = 4
PLANE = 4
ROWS = SLOTS * LATENTS
HALF = LATENTS // 2
WIDTH = 1024
KEYS = PATCH + LATENTS
HEAD_COLS = HEADS_HERE * HEAD_DIM
UNITS = 512
COPIES = 320
LOCALS = 32
QUERY, OUT, KEY_VALUE = (0, 256), (256, 512), (512, 1024)


ORDER = (
    ("enter",), ("vectors_out",), ("AF", 0, "k"), ("SC", 0, "u"), ("AF", 0, "q"), ("OA", 0), ("OF", 0), ("OA", 1),
    ("OF", 1), ("prepare",), ("SC", 0, "d"), ("vectors_in",), ("MN", 0), ("OW", 0), ("OW", 1), ("AN", 0, "k"),
    ("AN", 0, "q"), ("WF", 0, "u"), ("MN", 1), ("A1", 0, "k"), ("A1", 0, "q"), ("MN", 2), ("LN", 0, 0), ("LN", 0, 1),
    ("LN", 0, 2), ("A2", 0, "k"), ("A2", 0, "q"), ("WN", 0, "u"), ("WF", 0, "d"), ("RD", 0, "asecondk"), ("KM", 0, 0),
    ("KM", 0, 1), ("KM", 0, 2), ("RD", 0, "asecondq"), ("SC", 1, "u"), ("SC", 1, "d"), ("AF", 1, "k"), ("AF", 1, "q"),
    ("AT", 0, 0), ("AT", 0, 1), ("MI", 0, 0), ("WN", 0, "d"), ("AT", 0, 2), ("AN", 1, "k"), ("AN", 1, "q"),
    ("WF", 1, "u"), ("MI", 0, 1), ("RH", 0, 0), ("MI", 0, 2), ("RH", 0, 1), ("RD", 0, "nearu"), ("RD", 0, "neard"),
    ("FF", 0, 0), ("RH", 0, 2), ("A1", 1, "k"), ("A1", 1, "q"), ("FS", 0, 0), ("FF", 0, 1), ("FS", 0, 1),
    ("FF", 0, 2), ("WN", 1, "u"), ("WF", 1, "d"), ("NS", 0, 0), ("FS", 0, 2), ("A2", 1, "k"), ("A2", 1, "q"),
    ("LN", 1, 0), ("NS", 0, 1), ("RD", 1, "asecondk"), ("KM", 1, 0), ("KM", 1, 1), ("KM", 1, 2),
    ("RD", 1, "asecondq"), ("LN", 1, 1), ("NS", 0, 2), ("AT", 1, 0), ("LN", 1, 2), ("AT", 1, 1), ("MI", 1, 0),
    ("AT", 1, 2), ("MI", 1, 1), ("RH", 1, 0), ("MI", 1, 2), ("WN", 1, "d"), ("RH", 1, 1), ("RH", 1, 2), ("GO", 1, 0),
    ("GO", 1, 1), ("GO", 1, 2), ("RD", 1, "nearu"), ("RD", 1, "neard"), ("FF", 1, 0), ("FF", 1, 1), ("FF", 1, 2),
    ("FS", 1, 0), ("GH", 1, 0), ("FS", 1, 1), ("GH", 1, 1), ("FS", 1, 2), ("GH", 1, 2), ("NS", 1, 0), ("FB", 1, 0),
    ("NS", 1, 1), ("FB", 1, 1), ("BS", 1, 0), ("NS", 1, 2), ("FB", 1, 2), ("BS", 1, 1),
    ("ST", "scatter", "far", "near"), ("GA", 1, "d"), ("BS", 1, 2), ("GA", 1, "u"), ("SF", 1, 0), ("SF", 1, 1),
    ("SF", 1, 2), ("GB", 1, "d"), ("GB", 1, "u"), ("RE", 0), ("RE", 1), ("RE", 2), ("MB", 1, 0), ("AB", 1, 0),
    ("MB", 1, 1), ("AB", 1, 1), ("MB", 1, 2), ("AB", 1, 2), ("SB", 1, 0), ("SB", 1, 1), ("SB", 1, 2), ("GF", 1, "d"),
    ("MD", 1, 0), ("MD", 1, 1), ("MD", 1, 2), ("GH", 0, 0), ("FB", 0, 0), ("GH", 0, 1), ("FB", 0, 1), ("BS", 0, 0),
    ("GH", 0, 2), ("FB", 0, 2), ("BS", 0, 1), ("GF", 1, "u"), ("ST", "afar", "anear", "afirst", "asecond"),
    ("BS", 0, 2), ("QG", 1), ("KG", 1), ("GP", 1, "d"), ("GA", 0, "d"), ("GA", 0, "u"), ("SF", 0, 0), ("SF", 0, 1),
    ("SF", 0, 2), ("GB", 0, "d"), ("GB", 0, "u"), ("S2", 1, "q"), ("S2", 1, "k"), ("MB", 0, 0), ("AB", 0, 0),
    ("MB", 0, 1), ("AB", 0, 1), ("MB", 0, 2), ("AB", 0, 2), ("GP", 1, "u"), ("SN", 1, "q"), ("SN", 1, "k"),
    ("GF", 0, "d"), ("QG", 0), ("SB", 0, 0), ("SB", 0, 1), ("SB", 0, 2), ("ST", "grad1", "gradhand1"), ("MD", 0, 0),
    ("MD", 0, 1), ("MD", 0, 2), ("KG", 0), ("vector_sums_out",), ("SR", 1, "q"), ("SR", 1, "k"), ("S2", 0, "q"),
    ("GF", 0, "u"), ("S2", 0, "k"), ("SE", 1, "q"), ("SE", 1, "k"), ("GP", 0, "d"), ("SN", 0, "q"), ("SN", 0, "k"),
    ("vector_sums_in",), ("SR", 0, "q"), ("SR", 0, "k"), ("GP", 0, "u"), ("vector_sums_end",), ("SE", 0, "q"),
    ("SE", 0, "k"), ("close",),
)


class Copies:
    def __init__(self, send_sems, recv_sems, local_sems):
        self.send_sems, self.recv_sems, self.local_sems = send_sems, recv_sems, local_sems
        self.used = self.used_local = 0
        self.sending = []

    def start(self, source, target, device):
        copy = pltpu.make_async_remote_copy(
            src_ref=source,
            dst_ref=target,
            send_sem=self.send_sems.at[self.used],
            recv_sem=self.recv_sems.at[self.used],
            device_id=device,
            device_id_type=MESH,
        )
        self.used += 1
        copy.start()
        self.sending.append(copy)
        return copy

    def start_local(self, source, target):
        copy = pltpu.make_async_copy(source, target, self.local_sems.at[self.used_local])
        self.used_local += 1
        copy.start()
        return copy

    def sent(self, copies):
        for copy in copies:
            if any(kept is copy for kept in self.sending):
                copy.wait_send()
                self.sending = [kept for kept in self.sending if kept is not copy]


def matmul(left, right):
    return jnp.dot(left, right, preferred_element_type=F32)


def matmul_nt(left, right):
    return lax.dot_general(left, right, (((1,), (1,)), ((), ())), preferred_element_type=F32)


def matmul_tn(left, right):
    return lax.dot_general(left, right, (((0,), (0,)), ((), ())), preferred_element_type=F32)


def loop(count, body):
    def step(index, carry):
        body(index)
        return carry

    lax.fori_loop(0, count, step, 0)


def centred(values):
    centre = values - jnp.mean(values, -1, keepdims=True)
    scale = lax.rsqrt(jnp.mean(centre * centre, -1, keepdims=True) + 1e-05)
    return centre * scale, scale


def norm_back(grad, gain, unit, scale):
    inner = grad * gain
    return scale * (
        inner
        - jnp.mean(inner, -1, keepdims=True)
        - unit * jnp.mean(inner * unit, -1, keepdims=True)
    )


def column_sums(values):
    return jnp.sum(values, 0, keepdims=True)


def slot_rows(slot):
    return pl.ds(slot * LATENTS, LATENTS)


def fused_kernel(
    patch_rows,
    image_count,
    media,
    latents,
    cotangent,
    vectors,
    w_query,
    w_key,
    w_value,
    w_out_t,
    w_up,
    w_down_t,
    out_latents,
    out_media,
    out_media_pair,
    out_state,
    out_attn,
    out_up,
    out_down_t,
    out_vectors,
    AW,
    FW,
    VG,
    GS,
    J,
    X,
    Y,
    Q,
    KV,
    O,
    PR,
    H,
    GP,
    G,
    DY,
    DU,
    ZP,
    PS,
    PRECV,
    TS,
    TR,
    AS,
    AR,
    DX,
    DH,
    DV,
    DAB,
    DQ,
    DKV,
    MG,
    RF1,
    RF2,
    RA1A,
    RA1B,
    RA2A,
    RA2B,
    RA3,
    RA4,
    VS,
    VR,
    MASK,
    send_sems,
    recv_sems,
    local_sems,
):
    me = lax.axis_index("dp")
    half = lax.axis_index("mp")
    z, c = me // 4, me % 4
    zh, zl = z // 2, z % 2
    y, x = c // 2, c % 2
    columns = (c, y * 2 + 1 - x, (1 - y) * 2 + x, 3 - c)
    plane = tuple((z * 4 + column, half) for column in columns)
    near = ((zh * 2 + 1 - zl) * 4 + c, half)
    far = (((1 - zh) * 2 + zl) * 4 + c, half)
    sibling = (me, 1 - half)
    copies = Copies(send_sems, recv_sems, local_sems)
    mine = pl.ds(pl.multiple_of(half * HALF, 32), HALF)
    other = pl.ds(pl.multiple_of((1 - half) * HALF, 32), HALF)
    first = jnp.where(half == 0, 1.0, 0.0).astype(F32)
    flying = {}
    tasks = {}

    def task(function):
        tasks[function.__name__] = function
        return function

    def keep(name, started):
        flying[name] = started if isinstance(started, list) else [started]

    def arrived(name):
        for copy in flying[name]:
            copy.wait_recv()
        return flying[name]

    def landed(name):
        for copy in flying.pop(name):
            copy.wait()

    def unit_columns(index):
        return pl.ds(pl.multiple_of(columns[index] * UNITS, UNITS), UNITS)

    up_part, down_part = pl.ds(0, UNITS), pl.ds(UNITS, UNITS)
    parts = {"u": up_part, "d": down_part}
    chunks = {"k": ((512, w_key), (768, w_value)), "q": ((0, w_query), (256, w_out_t))}

    @task
    def enter():
        barrier = pltpu.get_barrier_semaphore()
        for step in range(1, 16):
            pl.semaphore_signal(
                barrier, inc=1, device_id=((me + step) % 16, half), device_id_type=MESH
            )
        pl.semaphore_signal(barrier, inc=1, device_id=sibling, device_id_type=MESH)
        pl.semaphore_wait(barrier, 16)

    @task
    def vectors_out():
        keep(
            "vectors",
            [copies.start(vectors, VG.at[me], ((me + step) % 16, half)) for step in range(1, 16)],
        )

    def own_attn(layer):
        keep(
            f"own_attn{layer}",
            [
                copies.start_local(
                    source.at[layer], AW.at[layer, zh, zl, y, x, :, pl.ds(low, 256)]
                )
                for chunk in "kq"
                for low, source in chunks[chunk]
            ],
        )

    def own_feed(layer):
        keep(
            f"own_feed{layer}",
            [
                copies.start_local(
                    source.at[layer, :, unit_columns(0)], FW.at[layer, zh, zl, c, :, part]
                )
                for source, part in ((w_up, up_part), (w_down_t, down_part))
            ],
        )

    def feed_scatter(layer, part):
        source = w_up if part == "u" else w_down_t
        keep(
            f"scatter{part}{layer}",
            [
                copies.start(
                    source.at[layer, :, unit_columns(index)],
                    FW.at[layer, zh, zl, c, :, parts[part]],
                    plane[index],
                )
                for index in (3, 1, 2)
            ],
        )

    def feed_far(layer, part):
        arrived(f"scatter{part}{layer}")
        block = FW.at[layer, zh, zl, :, :, parts[part]]
        keep(f"far{part}{layer}", copies.start(block, block, far))

    def feed_near(layer, part):
        arrived(f"far{part}{layer}")
        block = FW.at[layer, :, zl, :, :, parts[part]]
        keep(f"near{part}{layer}", copies.start(block, block, near))

    def attn_far(layer, chunk):
        keep(
            f"afar{chunk}{layer}",
            [
                copies.start(
                    source.at[layer], AW.at[layer, zh, zl, y, x, :, pl.ds(low, 256)], far
                )
                for low, source in chunks[chunk]
            ],
        )

    def attn_near(layer, chunk):
        arrived(f"afar{chunk}{layer}")
        block = AW.at[layer, :, zl, y, x, :, pl.ds(chunks[chunk][0][0], 512)]
        keep(f"anear{chunk}{layer}", copies.start(block, block, near))

    def attn_first(layer, chunk):
        arrived(f"anear{chunk}{layer}")
        keep(
            f"afirst{chunk}{layer}",
            [
                copies.start(block, block, plane[1 + side])
                for side in range(2)
                for block in [AW.at[layer, :, :, y, x, :, pl.ds(chunks[chunk][side][0], 256)]]
            ],
        )

    def attn_second(layer, chunk):
        arrived(f"afirst{chunk}{layer}")
        block_a = AW.at[layer, :, :, y, :, :, pl.ds(chunks[chunk][0][0], 256)]
        block_b = AW.at[layer, :, :, :, x, :, pl.ds(chunks[chunk][1][0], 256)]
        keep(
            f"asecond{chunk}{layer}",
            [copies.start(block_a, block_a, plane[2]), copies.start(block_b, block_b, plane[1])],
        )

    @task
    def prepare():
        head_row = lax.broadcasted_iota(jnp.int32, (HEAD_COLS, HEAD_COLS), 0) // HEAD_DIM
        head_column = lax.broadcasted_iota(jnp.int32, (HEAD_COLS, HEAD_COLS), 1) // HEAD_DIM
        MASK[...] = jnp.where(head_row == head_column, 1.0, 0.0).astype(F32)
        VG[me] = vectors[...]
        VS[...] = jnp.zeros_like(VS)
        for slot in range(SLOTS):
            rows = slot_rows(slot)
            X[0, rows, :] = latents[rows, :].astype(F32)
            live = jnp.where(slot < image_count[0], 1.0, 0.0).astype(F32)
            grad = cotangent[rows, :].astype(F32) * live
            DX[rows, :] = grad
            DY[1, slot, 0] = grad.astype(BF16)

    @task
    def vectors_in():
        arrived("vectors")
        for tile in range(8):
            GS[:, tile * 128 : tile * 128 + 128] = VG[2 * tile].astype(F32) + VG[
                2 * tile + 1
            ].astype(F32)

    def gain(layer, which):
        return GS[layer * 3 + which : layer * 3 + which + 1, :]

    def shift(layer, which):
        return GS[6 + layer * 3 + which : 7 + layer * 3 + which, :]

    def media_norm(slot):
        def body(index):
            rows = pl.ds(pl.multiple_of(slot * PATCH + index * 64, 64), 64)
            keys = pl.ds(pl.multiple_of(index * 64, 64), 64)
            unit, _ = centred(media[rows, :].astype(F32))
            for layer in range(2):
                J[layer, slot, keys, :] = (unit * gain(layer, 0) + shift(layer, 0)).astype(BF16)

        loop(4, body)

    def latent_norm(layer, slot):
        if layer > 0:
            copies.sent(arrived(f"state{layer}{slot}"))
        unit, _ = centred(X[layer, slot_rows(slot), :])
        J[layer, slot, PATCH:, :] = (unit * gain(layer, 1) + shift(layer, 1)).astype(BF16)

    def attn_weight(layer, span):
        return AW[layer, :, :, :, :, :, span[0] : span[1]].reshape(WIDTH, span[1] - span[0])

    def feed_weight(layer, part):
        low = 0 if part == "u" else UNITS
        return FW[layer, :, :, :, :, low : low + UNITS].reshape(WIDTH, UNITS)

    def stacked(value):
        return (jnp.concatenate([value.astype(F32)] * HEADS_HERE, 0) * MASK[...]).astype(BF16)

    def unstacked(value):
        return jnp.sum((value * MASK[...]).reshape(HEADS_HERE, LATENTS, HEAD_COLS), 0)

    def media_keys(layer, slot):
        KV[layer, slot, 0:PATCH] = matmul(
            J[layer, slot, 0:PATCH, :], attn_weight(layer, KEY_VALUE)
        ).astype(BF16)

    def attention(layer, slot):
        rows = J[layer, slot, PATCH:, :]
        KV[layer, slot, PATCH:] = matmul(rows, attn_weight(layer, KEY_VALUE)).astype(BF16)
        query = matmul(rows, attn_weight(layer, QUERY)).astype(BF16)
        Q[layer, slot] = query
        scores = matmul_nt(stacked(query), KV[layer, slot, :, 0:256]) * 0.125
        key = lax.broadcasted_iota(jnp.int32, (HEAD_COLS, KEYS), 1)
        scores = jnp.where((key >= PATCH) | (key < patch_rows[slot]), scores, NEGATIVE)
        expo = jnp.exp(scores - jnp.max(scores, -1, keepdims=True))
        probs = expo / jnp.sum(expo, -1, keepdims=True)
        PR[layer, slot] = probs
        mixed = unstacked(matmul(probs.astype(BF16), KV[layer, slot, :, 256:512])).astype(BF16)
        O[layer, slot] = mixed
        AS[slot] = matmul_nt(mixed, attn_weight(layer, OUT)).astype(BF16)
        keep(f"mix{layer}{slot}", copies.start(AS.at[slot], AR.at[slot], sibling))

    def spread(name, buffer, layer, slot):
        block = buffer.at[layer, slot, 0, mine]
        keep(
            f"{name}{layer}{slot}",
            [
                copies.start(block, buffer.at[layer, slot, index, mine], plane[index])
                for index in (3, 1, 2)
            ],
        )

    def hand_over(name, buffer, layer, slot):
        started = []
        for index, copy in zip((3, 1, 2), flying[f"{name}{layer}{slot}"]):
            block = buffer.at[layer, slot, index, mine]
            copy.wait_recv()
            started.append(copies.start(block, block, sibling))
        keep(f"{name}hand{layer}{slot}", started)

    def middle(layer, slot):
        copies.sent(arrived(f"mix{layer}{slot}"))
        rows = slot_rows(slot)
        value = X[layer, rows, :] + (AS[slot].astype(F32) + AR[slot].astype(F32))
        Y[layer, rows, :] = value
        unit, _ = centred(value)
        H[layer, slot, 0] = (unit * gain(layer, 2) + shift(layer, 2)).astype(BF16)
        spread("rows", H, layer, slot)

    def send_pair(name, way, slot):
        PS[slot] = ZP[slot, :, other, :].astype(BF16)
        keep(name, copies.start(PS.at[slot], PRECV.at[way, slot], sibling))

    def feed_forward(layer, slot):
        arrived(f"rowshand{layer}{slot}")
        pre_act = matmul(H[layer, slot].reshape(256, WIDTH), feed_weight(layer, "u"))
        bell = 0.5 * (1.0 + lax.erf(pre_act * 0.7071067811865476))
        GP[layer, slot] = bell + pre_act * jnp.exp(-0.5 * pre_act * pre_act) * 0.3989422804014327
        act = (pre_act * bell).astype(BF16)
        G[layer, slot] = act
        ZP[slot] = matmul_nt(act, feed_weight(layer, "d")).reshape(PLANE, LATENTS, WIDTH)
        send_pair(f"pair0{layer}{slot}", 0, slot)

    def plane_sum(way, layer, slot):
        copies.sent(arrived(f"pair{way}{layer}{slot}"))
        started = []
        for index in (3, 1, 2):
            TS[slot, index - 1] = (
                ZP[slot, index, mine, :] + PRECV[way, slot, index].astype(F32)
            ).astype(BF16)
            started.append(
                copies.start(TS.at[slot, index - 1], TR.at[way, slot, index - 1], plane[index])
            )
        keep(f"away{way}{layer}{slot}", started)

    def feed_sum(way, layer, slot):
        total = ZP[slot, 0, mine, :] + PRECV[way, slot, 0].astype(F32)
        copies.sent(arrived(f"away{way}{layer}{slot}"))
        for index in range(3):
            total = total + TR[way, slot, index].astype(F32)
        return total

    def half_rows(slot):
        return pl.ds(pl.multiple_of(slot * LATENTS + half * HALF, HALF), HALF)

    def next_state(layer, slot):
        rows = half_rows(slot)
        X[layer + 1, rows, :] = Y[layer, rows, :] + feed_sum(0, layer, slot)
        block = X.at[layer + 1, rows]
        keep(f"state{layer + 1}{slot}", copies.start(block, block, sibling))

    def result(slot):
        copies.sent(arrived(f"state2{slot}"))
        live = jnp.where(slot < image_count[0], 1.0, 0.0).astype(F32)
        rows = slot_rows(slot)
        out_latents[rows, :] = (X[2, rows, :] * live).astype(BF16)

    def feed_back(layer, slot):
        arrived(f"gradhand{layer}{slot}")
        grad_act = matmul(DY[layer, slot].reshape(256, WIDTH), feed_weight(layer, "d"))
        up_low = (grad_act * GP[layer, slot]).astype(BF16)
        DU[slot] = up_low
        ZP[slot] = matmul_nt(up_low, feed_weight(layer, "u")).reshape(PLANE, LATENTS, WIDTH)
        send_pair(f"pair1{layer}{slot}", 1, slot)

    def swap_feed(layer, slot):
        rows = half_rows(slot)
        DH[rows, :] = feed_sum(1, layer, slot)
        block = DH.at[rows]
        keep(f"feed{layer}{slot}", copies.start(block, block, sibling))

    def add_sums(row_gain, row_shift, grad, unit, factor):
        for row, value in ((row_gain, grad * unit), (row_shift, grad)):
            VS[row : row + 1, :] = VS[row : row + 1, :] + column_sums(value) * factor

    def middle_back(layer, slot):
        copies.sent(arrived(f"feed{layer}{slot}"))
        rows = slot_rows(slot)
        unit, scale = centred(Y[layer, rows, :])
        grad = DH[rows, :]
        grad_middle = DX[rows, :] + norm_back(grad, gain(layer, 2), unit, scale)
        DV[rows, :] = grad_middle
        DAB[rows, :] = grad_middle.astype(BF16)
        add_sums(8 + layer * 2, 9 + layer * 2, grad, unit, first)

    def attention_back(layer, slot):
        grad_mixed = matmul(DAB[slot_rows(slot), :], attn_weight(layer, OUT)).astype(BF16)
        grads = stacked(grad_mixed)
        probs = PR[layer, slot]
        grad_probs = matmul_nt(grads, KV[layer, slot, :, 256:512])
        grad_scores = (
            probs * (grad_probs - jnp.sum(grad_probs * probs, -1, keepdims=True))
        ).astype(BF16)
        DKV[slot, :, 256:512] = matmul_tn(probs.astype(BF16), grads).astype(BF16)
        queries = stacked(Q[layer, slot])
        DKV[slot, :, 0:256] = (matmul_tn(grad_scores, queries) * 0.125).astype(BF16)
        grad_query = unstacked(matmul(grad_scores, KV[layer, slot, :, 0:256])) * 0.125
        DQ[slot] = grad_query.astype(BF16)
        AS[slot] = (
            matmul_nt(DQ[slot], attn_weight(layer, QUERY))
            + matmul_nt(DKV[slot, PATCH:, :], attn_weight(layer, KEY_VALUE))
        ).astype(BF16)
        keep(f"norm{layer}{slot}", copies.start(AS.at[slot], AR.at[slot], sibling))

    def state_back(layer, slot):
        copies.sent(arrived(f"norm{layer}{slot}"))
        rows = slot_rows(slot)
        unit, scale = centred(X[layer, rows, :])
        grad = AS[slot].astype(F32) + AR[slot].astype(F32)
        grad_in = DV[rows, :] + norm_back(grad, gain(layer, 1), unit, scale)
        if layer > 0:
            DX[rows, :] = grad_in
            DY[layer - 1, slot, 0] = grad_in.astype(BF16)
            spread("grad", DY, layer - 1, slot)
        else:
            out_state[rows, :] = grad_in
        add_sums(layer * 2 + 1, layer * 2 + 5, grad, unit, first)

    def media_back(layer, slot):
        def body(index):
            keys = pl.ds(pl.multiple_of(index * 128, 128), 128)
            rows = pl.ds(pl.multiple_of(slot * PATCH + index * 128, 128), 128)
            grad = matmul_nt(DKV[slot, keys, :], attn_weight(layer, KEY_VALUE))
            unit, scale = centred(media[rows, :].astype(F32))
            piece = norm_back(grad, gain(layer, 0), unit, scale)
            if layer == 1:
                MG[rows, :] = piece
            else:
                DY[1, slot, pl.ds(index * 2, 2)] = (
                    (MG[rows, :] + piece).astype(BF16).reshape(2, LATENTS, WIDTH)
                )
            add_sums(layer * 2, layer * 2 + 4, grad, unit, 1.0)

        loop(2, body)
        if layer == 0:
            rows = pl.ds(slot * PATCH, PATCH)
            block = DY.at[1, slot]
            keep(f"media{slot}", copies.start(block, out_media_pair.at[slot], sibling))
            keep(f"media_own{slot}", copies.start_local(block, out_media.at[slot]))

    def add_into(target, received):
        target[...] = (target[...].astype(F32) + received[...].astype(F32)).astype(BF16)

    def feed_grad(layer, part, low):
        left, right = (DY, G.at[layer]) if part == "d" else (H, DU)
        begin = UNITS if part == "d" else 0

        def body(high):
            cols = pl.ds(pl.multiple_of((high * 2 + low) * 256, 256), 256)
            sums = matmul_tn(
                left[layer, :, :, :, cols].reshape(4 * ROWS, 256),
                right[...].reshape(4 * ROWS, UNITS),
            )
            FW[layer, high, low, :, :, begin : begin + UNITS] = sums.astype(BF16).reshape(
                PLANE, 64, UNITS
            )

        loop(2, body)

    def feed_grad_away(layer, part):
        feed_grad(layer, part, 1 - zl)
        keep(
            f"gnear{part}{layer}",
            copies.start(
                FW.at[layer, :, 1 - zl, :, :, parts[part]],
                RF1.at[layer, :, :, :, parts[part]],
                near,
            ),
        )

    def feed_grad_stay(layer, part):
        feed_grad(layer, part, zl)

    def feed_sum_far(layer, part):
        arrived(f"gnear{part}{layer}")

        def add(high):
            for index in range(4):
                add_into(
                    FW.at[layer, high, zl, index, :, parts[part]],
                    RF1.at[layer, high, index, :, parts[part]],
                )

        add(1 - zh)
        block = FW.at[layer, 1 - zh, zl, :, :, parts[part]]
        keep(f"gfar{part}{layer}", copies.start(block, RF2.at[layer, :, :, parts[part]], far))
        add(zh)

    def feed_sum_plane(layer, part):
        arrived(f"gfar{part}{layer}")
        target = out_up if part == "u" else out_down_t
        started = []
        for index in (3, 1, 2, 0):
            column = columns[index]
            block = FW.at[layer, zh, zl, column, :, parts[part]]
            add_into(block, RF2.at[layer, column, :, parts[part]])
            if index > 0:
                started.append(copies.start(block, target.at[layer, c], plane[index]))
            else:
                keep(f"gown{part}{layer}", copies.start_local(block, target.at[layer, c]))
        keep(f"gplane{part}{layer}", started)

    def attn_grad_query(layer):
        def body(index):
            cols = pl.ds(pl.multiple_of(index * 256, 256), 256)
            high, low = index // 2, index % 2
            query_part = matmul_tn(
                J[layer, :, PATCH:, cols].reshape(ROWS, 256), DQ[...].reshape(ROWS, HEAD_COLS)
            )
            AW[layer, high, low, :, :, :, 0:256] = query_part.astype(BF16).reshape(2, 2, 64, 256)
            out_part = matmul_tn(DAB[:, cols], O[layer].reshape(ROWS, HEAD_COLS))
            AW[layer, high, low, :, :, :, 256:512] = out_part.astype(BF16).reshape(2, 2, 64, 256)

        loop(4, body)
        attn_sum_first(layer, "q")

    def attn_grad_key(layer):
        def body(index):
            cols = pl.ds(pl.multiple_of(index * 256, 256), 256)
            high, low = index // 2, index % 2
            key_part = matmul_tn(
                J[layer, :, :, cols].reshape(SLOTS * KEYS, 256), DKV[...].reshape(SLOTS * KEYS, 512)
            )
            AW[layer, high, low, :, :, :, 512:1024] = key_part.astype(BF16).reshape(2, 2, 64, 512)

        loop(4, body)
        attn_sum_first(layer, "k")

    def low_columns(chunk, side):
        return pl.ds(chunks[chunk][side][0], 256)

    def short_columns(chunk):
        return pl.ds(0 if chunk == "q" else 256, 256)

    def attn_sum_first(layer, chunk):
        here = short_columns(chunk)
        keep(
            f"gfirst{chunk}{layer}",
            [
                copies.start(
                    AW.at[layer, :, :, 1 - y, :, :, low_columns(chunk, 0)],
                    RA1A.at[layer, :, :, :, :, here],
                    plane[2],
                ),
                copies.start(
                    AW.at[layer, :, :, :, 1 - x, :, low_columns(chunk, 1)],
                    RA1B.at[layer, :, :, :, :, here],
                    plane[1],
                ),
            ],
        )

    def attn_sum_second(layer, chunk):
        arrived(f"gfirst{chunk}{layer}")
        here, cols_a, cols_b = short_columns(chunk), low_columns(chunk, 0), low_columns(chunk, 1)

        def add(side_a, side_b):
            def body(index):
                high, low = index // 2, index % 2
                add_into(
                    AW.at[layer, high, low, y, side_a, :, cols_a],
                    RA1A.at[layer, high, low, side_a, :, here],
                )
                add_into(
                    AW.at[layer, high, low, side_b, x, :, cols_b],
                    RA1B.at[layer, high, low, side_b, :, here],
                )

            loop(4, body)

        add(1 - x, 1 - y)
        keep(
            f"gsecond{chunk}{layer}",
            [
                copies.start(
                    AW.at[layer, :, :, y, 1 - x, :, cols_a],
                    RA2A.at[layer, :, :, :, here],
                    plane[1],
                ),
                copies.start(
                    AW.at[layer, :, :, 1 - y, x, :, cols_b],
                    RA2B.at[layer, :, :, :, here],
                    plane[2],
                ),
            ],
        )
        add(x, y)

    def attn_sum_near(layer, chunk):
        arrived(f"gsecond{chunk}{layer}")
        here, cols_a, cols_b = short_columns(chunk), low_columns(chunk, 0), low_columns(chunk, 1)
        both = pl.ds(chunks[chunk][0][0], 512)

        def add(low):
            for high in range(2):
                add_into(
                    AW.at[layer, high, low, y, x, :, cols_a], RA2A.at[layer, high, low, :, here]
                )
                add_into(
                    AW.at[layer, high, low, y, x, :, cols_b], RA2B.at[layer, high, low, :, here]
                )

        add(1 - zl)
        keep(
            f"ganear{chunk}{layer}",
            copies.start(AW.at[layer, :, 1 - zl, y, x, :, both], RA3.at[layer, :, :, both], near),
        )
        add(zl)

    def attn_sum_far(layer, chunk):
        arrived(f"ganear{chunk}{layer}")
        both = pl.ds(chunks[chunk][0][0], 512)

        def add(high):
            add_into(AW.at[layer, high, zl, y, x, :, both], RA3.at[layer, high, :, both])

        add(1 - zh)
        keep(
            f"gafar{chunk}{layer}",
            copies.start(
                AW.at[layer, 1 - zh, zl, y, x, :, both], RA4.at[layer, :, both], far
            ),
        )
        add(zh)

    def attn_sum_end(layer, chunk):
        arrived(f"gafar{chunk}{layer}")
        both = pl.ds(chunks[chunk][0][0], 512)
        out_attn[layer, :, both] = AW[layer, zh, zl, y, x, :, both].astype(F32) + RA4[
            layer, :, both
        ].astype(F32)

    @task
    def vector_sums_out():
        keep(
            "sums",
            [
                copies.start(
                    VS.at[:, pl.ds(pl.multiple_of((((me + step) % 16) // 2) * 128, 128), 128)],
                    VR.at[step],
                    ((me + step) % 16, half),
                )
                for step in range(1, 16)
            ],
        )

    @task
    def vector_sums_in():
        arrived("sums")
        total = VS[:, pl.ds(pl.multiple_of((me // 2) * 128, 128), 128)]
        for step in range(1, 16):
            total = total + VR[step]
        VR[0] = total
        keep("sums_pair", copies.start(VR.at[0], VR.at[16], sibling))

    @task
    def vector_sums_end():
        arrived("sums_pair")
        out_vectors[...] = VR[0] + VR[16]

    def settle(*names):
        for name, started in flying.items():
            if name.startswith(names):
                copies.sent(started)

    @task
    def close():
        for slot in range(SLOTS):
            arrived(f"media{slot}")
            landed(f"media_own{slot}")
        for layer in range(2):
            for part in "ud":
                arrived(f"gplane{part}{layer}")
                landed(f"gown{part}{layer}")
        copies.sent(list(copies.sending))

    def grad_spread(layer, slot):
        spread("grad", DY, layer, slot)

    def grad_hand(layer, slot):
        hand_over("grad", DY, layer, slot)

    def rows_hand(layer, slot):
        hand_over("rows", H, layer, slot)

    def forward_sum(layer, slot):
        plane_sum(0, layer, slot)

    def backward_sum(layer, slot):
        plane_sum(1, layer, slot)

    def own_wait(layer):
        landed(f"own_attn{layer}")
        landed(f"own_feed{layer}")

    def ready(layer, name):
        arrived(f"{name}{layer}")

    steps = dict(
        MN=media_norm, LN=latent_norm, KM=media_keys, AT=attention, MI=middle, RH=rows_hand,
        FF=feed_forward, FS=forward_sum, NS=next_state, RE=result, GO=grad_spread, GH=grad_hand,
        FB=feed_back, BS=backward_sum, SF=swap_feed, MB=middle_back, AB=attention_back,
        SB=state_back, MD=media_back, OA=own_attn, OF=own_feed, OW=own_wait, SC=feed_scatter,
        WF=feed_far, WN=feed_near, AF=attn_far, AN=attn_near, A1=attn_first, A2=attn_second,
        RD=ready, GA=feed_grad_away, GB=feed_grad_stay, GF=feed_sum_far, GP=feed_sum_plane,
        QG=attn_grad_query, KG=attn_grad_key, S2=attn_sum_second, SN=attn_sum_near,
        SR=attn_sum_far, SE=attn_sum_end, ST=settle,
    )
    for name, *arguments in ORDER:
        if name in tasks:
            tasks[name]()
        else:
            steps[name](*arguments)


def fused(
    media, latents, patch_rows, image_count, cotangent, w_query, w_key, w_value, w_out, w_up, w_down,
    norm_gains, norm_shifts,
):
    w_out_t = jnp.swapaxes(w_out, 1, 2)
    w_down_t = jnp.swapaxes(w_down, 1, 2)
    piece = norm_gains.shape[2]
    vectors = jnp.concatenate([norm_gains.reshape(6, piece), norm_shifts.reshape(6, piece)], 0)
    vectors = jnp.pad(vectors, ((0, 4), (0, 0)))
    odd = lax.axis_index("dp") % 2 == 1
    blank = jnp.zeros_like(vectors)
    vectors = jnp.concatenate([jnp.where(odd, blank, vectors), jnp.where(odd, vectors, blank)], 1)

    vmem = pl.BlockSpec(memory_space=pltpu.VMEM)
    smem = pl.BlockSpec(memory_space=pltpu.SMEM)
    anywhere = pl.BlockSpec(memory_space=pl.ANY)

    def shape(dims, kind):
        return jax.ShapeDtypeStruct(dims, kind)

    results = pl.pallas_call(
        fused_kernel,
        name="resampler",
        out_shape=[
            shape((ROWS, WIDTH), BF16),
            shape((SLOTS, 4, LATENTS, WIDTH), BF16),
            shape((SLOTS, 4, LATENTS, WIDTH), BF16),
            shape((ROWS, WIDTH), F32),
            shape((2, 64, WIDTH), F32),
            shape((2, 4, 64, UNITS), BF16),
            shape((2, 4, 64, UNITS), BF16),
            shape((16, 128), F32),
        ],
        in_specs=[smem, smem, vmem, vmem, vmem, vmem] + [anywhere] * 6,
        out_specs=[vmem, anywhere, anywhere, vmem, vmem, anywhere, anywhere, vmem],
        scratch_shapes=[
            pltpu.VMEM((2, 2, 2, 2, 2, 64, 1024), BF16),
            pltpu.VMEM((2, 2, 2, 4, 64, 1024), BF16),
            pltpu.VMEM((16, 16, 128), BF16),
            pltpu.VMEM((16, WIDTH), F32),
            pltpu.VMEM((2, SLOTS, KEYS, WIDTH), BF16),
            pltpu.VMEM((3, ROWS, WIDTH), F32),
            pltpu.VMEM((2, ROWS, WIDTH), F32),
            pltpu.VMEM((2, SLOTS, LATENTS, HEAD_COLS), BF16),
            pltpu.VMEM((2, SLOTS, KEYS, 2 * HEAD_COLS), BF16),
            pltpu.VMEM((2, SLOTS, LATENTS, HEAD_COLS), BF16),
            pltpu.VMEM((2, SLOTS, HEAD_COLS, KEYS), F32),
            pltpu.VMEM((2, SLOTS, PLANE, LATENTS, WIDTH), BF16),
            pltpu.VMEM((2, SLOTS, 4 * LATENTS, UNITS), F32),
            pltpu.VMEM((2, SLOTS, 4 * LATENTS, UNITS), BF16),
            pltpu.VMEM((2, SLOTS, PLANE, LATENTS, WIDTH), BF16),
            pltpu.VMEM((SLOTS, 4 * LATENTS, UNITS), BF16),
            pltpu.VMEM((SLOTS, PLANE, LATENTS, WIDTH), F32),
            pltpu.VMEM((SLOTS, PLANE, HALF, WIDTH), BF16),
            pltpu.VMEM((2, SLOTS, PLANE, HALF, WIDTH), BF16),
            pltpu.VMEM((SLOTS, 3, HALF, WIDTH), BF16),
            pltpu.VMEM((2, SLOTS, 3, HALF, WIDTH), BF16),
            pltpu.VMEM((SLOTS, LATENTS, WIDTH), BF16),
            pltpu.VMEM((SLOTS, LATENTS, WIDTH), BF16),
            pltpu.VMEM((ROWS, WIDTH), F32),
            pltpu.VMEM((ROWS, WIDTH), F32),
            pltpu.VMEM((ROWS, WIDTH), F32),
            pltpu.VMEM((ROWS, WIDTH), BF16),
            pltpu.VMEM((SLOTS, LATENTS, HEAD_COLS), BF16),
            pltpu.VMEM((SLOTS, KEYS, 2 * HEAD_COLS), BF16),
            pltpu.VMEM((SLOTS * PATCH, WIDTH), F32),
            pltpu.VMEM((2, 2, 4, 64, 1024), BF16),
            pltpu.VMEM((2, 4, 64, 1024), BF16),
            pltpu.VMEM((2, 2, 2, 2, 64, 512), BF16),
            pltpu.VMEM((2, 2, 2, 2, 64, 512), BF16),
            pltpu.VMEM((2, 2, 2, 64, 512), BF16),
            pltpu.VMEM((2, 2, 2, 64, 512), BF16),
            pltpu.VMEM((2, 2, 64, 1024), BF16),
            pltpu.VMEM((2, 64, 1024), BF16),
            pltpu.VMEM((16, WIDTH), F32),
            pltpu.VMEM((17, 16, 128), F32),
            pltpu.VMEM((HEAD_COLS, HEAD_COLS), F32),
            pltpu.SemaphoreType.DMA((COPIES,)),
            pltpu.SemaphoreType.DMA((COPIES,)),
            pltpu.SemaphoreType.DMA((LOCALS,)),
        ],
        compiler_params=pltpu.CompilerParams(
            collective_id=0, has_side_effects=True, vmem_limit_bytes=64 * 2**20
        ),
        cost_estimate=pl.CostEstimate(
            flops=18 * 10**9, bytes_accessed=20 * 10**6, transcendentals=10**6
        ),
    )(
        patch_rows, image_count, media, latents, cotangent, vectors, w_query, w_key, w_value,
        w_out_t, w_up, w_down_t,
    )
    out_latents, media_own, media_pair, out_state, attn, up, down_t, sums = results
    out_media = (media_own.astype(F32) + media_pair.astype(F32)).reshape(SLOTS * PATCH, WIDTH)
    sums = jnp.where(odd, sums[:, piece:], sums[:, :piece])
    up = jnp.swapaxes(up, 1, 2).reshape(2, 64, 4 * UNITS).astype(F32)
    down = jnp.swapaxes(down_t, 2, 3).reshape(2, 4 * UNITS, 64).astype(F32)
    return (
        out_latents,
        out_media,
        out_state,
        attn[:, :, 0:256],
        attn[:, :, 512:768],
        attn[:, :, 768:1024],
        jnp.swapaxes(attn[:, :, 256:512], 1, 2),
        up,
        down,
        sums[0:4].reshape(2, 2, piece),
        sums[4:8].reshape(2, 2, piece),
        sums[8:12].reshape(2, 2, piece),
    )


def solution(mesh):
    body = fused if (mesh.shape["dp"], mesh.shape["mp"]) == (16, 2) else local
    placed = (
        P("dp", None),
        P("dp", None),
        P("dp"),
        P("dp"),
        P("dp", None),
        P(None, "dp", "mp"),
        P(None, "dp", "mp"),
        P(None, "dp", "mp"),
        P(None, "mp", "dp"),
        P(None, "dp", "mp"),
        P(None, "mp", "dp"),
        P(None, None, "dp"),
        P(None, None, "dp"),
    )
    return jax.shard_map(
        body,
        mesh=mesh,
        in_specs=placed,
        out_specs=(
            P("dp", None),
            P("dp", None),
            P("dp", None),
            P(None, "dp", "mp"),
            P(None, "dp", "mp"),
            P(None, "dp", "mp"),
            P(None, "mp", "dp"),
            P(None, "dp", "mp"),
            P(None, "mp", "dp"),
            P(None, None, "dp"),
            P(None, None, "dp"),
            P(None, None, "dp"),
        ),
        check_vma=False,
    )
```

```python
from functools import partial

import jax
import jax.numpy as jnp
from jax import lax
from jax.experimental import pallas as pl
from jax.experimental.pallas import tpu as pltpu
from jax.sharding import PartitionSpec as P

HEAD_DIM = 64
LATENTS = 64
PATCH = 256


NEGATIVE = -1000000000.0


def normalize(values, gain, shift):
    centre = values - jnp.mean(values, -1, keepdims=True)
    spread = jnp.mean(centre * centre, -1, keepdims=True)
    return centre * lax.rsqrt(spread + 1e-05) * gain + shift


def product(left, right):
    return jnp.dot(left, right, preferred_element_type=jnp.float32)


def outer_sum(left, right):
    return lax.dot_general(
        left, right, (((0,), (0,)), ((), ())), preferred_element_type=jnp.float32
    )


def back_product(left, right):
    return lax.dot_general(
        left, right, (((1,), (1,)), ((), ())), preferred_element_type=jnp.float32
    )


def forward_reduce(values):
    return lax.psum(values.astype(jnp.bfloat16), "mp").astype(jnp.float32)


def backward_reduce(values):
    return lax.psum(values.astype(jnp.bfloat16), "mp").astype(jnp.float32)


def key_scores(query_heads, key_heads, key_mask):
    scores = (
        jnp.einsum("iqhd,ikhd->ihqk", query_heads, key_heads, preferred_element_type=jnp.float32)
        * 0.125
    )
    return jnp.where(key_mask[:, None, None, :], scores, NEGATIVE)


def local(
    media,
    latents,
    patch_rows,
    image_count,
    cotangent,
    w_query,
    w_key,
    w_value,
    w_out,
    w_up,
    w_down,
    norm_gains,
    norm_shifts,
):
    images = patch_rows.shape[0]
    width = media.shape[1]
    heads_here = w_query.shape[2] // HEAD_DIM
    layers = w_query.shape[0]
    keys_len = PATCH + LATENTS
    key_mask = jnp.concatenate(
        [
            jnp.arange(PATCH, dtype=jnp.int32)[None, :] < patch_rows[:, None],
            jnp.ones((images, LATENTS), bool),
        ],
        1,
    )
    live = (jnp.arange(images, dtype=jnp.int32) < image_count[0]).astype(jnp.float32)
    live_rows = jnp.repeat(live, LATENTS)[:, None]
    media_full = media.astype(jnp.float32)
    state = latents.astype(jnp.float32)
    saved = []
    for layer in range(layers):
        gathered = (
            lax.all_gather(w_query[layer], "dp", axis=0, tiled=True),
            lax.all_gather(w_key[layer], "dp", axis=0, tiled=True),
            lax.all_gather(w_value[layer], "dp", axis=0, tiled=True),
            lax.all_gather(w_out[layer], "dp", axis=1, tiled=True),
            lax.all_gather(w_up[layer], "dp", axis=0, tiled=True),
            lax.all_gather(w_down[layer], "dp", axis=1, tiled=True),
            lax.all_gather(norm_gains[layer], "dp", axis=1, tiled=True),
            lax.all_gather(norm_shifts[layer], "dp", axis=1, tiled=True),
        )
        full_query, full_key, full_value, full_out, full_up, full_down, gain_rows, shift_rows = (
            gathered
        )
        gains = gain_rows.astype(jnp.float32)
        shifts = shift_rows.astype(jnp.float32)
        media_low = normalize(media_full, gains[0], shifts[0]).astype(jnp.bfloat16)
        latent_low = normalize(state, gains[1], shifts[1]).astype(jnp.bfloat16)
        query = product(latent_low, full_query).astype(jnp.bfloat16)
        joined = jnp.concatenate(
            [media_low.reshape(images, PATCH, width), latent_low.reshape(images, LATENTS, width)], 1
        ).reshape(images * keys_len, width)
        keys = product(joined, full_key).astype(jnp.bfloat16)
        values = product(joined, full_value).astype(jnp.bfloat16)
        scores = key_scores(
            query.reshape(images, LATENTS, heads_here, HEAD_DIM),
            keys.reshape(images, keys_len, heads_here, HEAD_DIM),
            key_mask,
        )
        top = jnp.max(scores, -1, keepdims=True)
        expo = jnp.exp(scores - top)
        total = jnp.sum(expo, -1, keepdims=True)
        probs_low = (expo / total).astype(jnp.bfloat16)
        log_total = top + jnp.log(total)
        mixed = jnp.einsum(
            "ihqk,ikhd->iqhd",
            probs_low,
            values.reshape(images, keys_len, heads_here, HEAD_DIM),
            preferred_element_type=jnp.float32,
        )
        mixed_low = mixed.astype(jnp.bfloat16).reshape(images * LATENTS, heads_here * HEAD_DIM)
        middle = state + forward_reduce(product(mixed_low, full_out))
        hidden_low = normalize(middle, gains[2], shifts[2]).astype(jnp.bfloat16)
        pre_act = product(hidden_low, full_up)
        act_low = jax.nn.gelu(pre_act, approximate=False).astype(jnp.bfloat16)
        kept_weights = None
        saved.append(
            (
                kept_weights,
                state,
                latent_low,
                joined,
                query,
                keys,
                values,
                log_total,
                mixed_low,
                middle,
                hidden_low,
                pre_act,
                act_low,
            )
        )
        state = middle + forward_reduce(product(act_low, full_down))
    result = (state * live_rows).astype(jnp.bfloat16)
    grad_state = cotangent.astype(jnp.float32) * live_rows
    media_part = jnp.zeros_like(media_full)
    grads = [None] * layers
    for layer in reversed(range(layers)):
        (
            kept_weights,
            state_in,
            latent_low,
            joined,
            query,
            keys,
            values,
            log_total,
            mixed_low,
            middle,
            hidden_low,
            pre_act,
            act_low,
        ) = saved[layer]
        weights_now = (
            lax.all_gather(w_query[layer], "dp", axis=0, tiled=True),
            lax.all_gather(w_key[layer], "dp", axis=0, tiled=True),
            lax.all_gather(w_value[layer], "dp", axis=0, tiled=True),
            lax.all_gather(w_out[layer], "dp", axis=1, tiled=True),
            lax.all_gather(w_up[layer], "dp", axis=0, tiled=True),
            lax.all_gather(w_down[layer], "dp", axis=1, tiled=True),
            lax.all_gather(norm_gains[layer], "dp", axis=1, tiled=True),
            lax.all_gather(norm_shifts[layer], "dp", axis=1, tiled=True),
        )
        full_query, full_key, full_value, full_out, full_up, full_down, gain_rows, shift_rows = (
            weights_now
        )
        gains = gain_rows.astype(jnp.float32)
        shifts = shift_rows.astype(jnp.float32)
        down_low = grad_state.astype(jnp.bfloat16)
        grad_down = outer_sum(act_low, down_low)
        grad_act = back_product(down_low, full_down)
        unused, gelu_pull = jax.vjp(partial(jax.nn.gelu, approximate=False), pre_act)
        up_low = gelu_pull(grad_act)[0].astype(jnp.bfloat16)
        grad_up = outer_sum(hidden_low, up_low)
        grad_hidden = backward_reduce(back_product(up_low, full_up))
        unused, norm_pull = jax.vjp(normalize, middle, gains[2], shifts[2])
        grad_middle, gain_feed, shift_feed = norm_pull(grad_hidden)
        grad_middle = grad_middle + grad_state
        out_low = grad_middle.astype(jnp.bfloat16)
        grad_out = outer_sum(mixed_low, out_low)
        grad_mixed = (
            back_product(out_low, full_out)
            .astype(jnp.bfloat16)
            .reshape(images, LATENTS, heads_here, HEAD_DIM)
        )
        query_heads = query.reshape(images, LATENTS, heads_here, HEAD_DIM)
        key_heads = keys.reshape(images, keys_len, heads_here, HEAD_DIM)
        value_heads = values.reshape(images, keys_len, heads_here, HEAD_DIM)
        probs = jnp.exp(key_scores(query_heads, key_heads, key_mask) - log_total)
        probs_low = probs.astype(jnp.bfloat16)
        grad_probs = jnp.einsum(
            "iqhd,ikhd->ihqk", grad_mixed, value_heads, preferred_element_type=jnp.float32
        )
        grad_scores = (
            probs * (grad_probs - jnp.sum(grad_probs * probs, -1, keepdims=True))
        ).astype(jnp.bfloat16)
        grad_values = jnp.einsum(
            "ihqk,iqhd->ikhd", probs_low, grad_mixed, preferred_element_type=jnp.float32
        ).astype(jnp.bfloat16)
        grad_query = (
            jnp.einsum(
                "ihqk,ikhd->iqhd", grad_scores, key_heads, preferred_element_type=jnp.float32
            )
            * 0.125
        ).astype(jnp.bfloat16)
        grad_keys = (
            jnp.einsum(
                "ihqk,iqhd->ikhd", grad_scores, query_heads, preferred_element_type=jnp.float32
            )
            * 0.125
        ).astype(jnp.bfloat16)
        grad_query = grad_query.reshape(images * LATENTS, heads_here * HEAD_DIM)
        grad_keys = grad_keys.reshape(images * keys_len, heads_here * HEAD_DIM)
        grad_values = grad_values.reshape(images * keys_len, heads_here * HEAD_DIM)
        grad_wq = outer_sum(latent_low, grad_query)
        grad_wk = outer_sum(joined, grad_keys)
        grad_wv = outer_sum(joined, grad_values)
        grad_joined = (
            back_product(grad_keys, full_key) + back_product(grad_values, full_value)
        ).reshape(images, keys_len, width)
        grad_latent = backward_reduce(
            back_product(grad_query, full_query)
            + grad_joined[:, PATCH:].reshape(images * LATENTS, width)
        )
        unused, norm_pull = jax.vjp(normalize, state_in, gains[1], shifts[1])
        grad_in, gain_latent, shift_latent = norm_pull(grad_latent)
        grad_state = grad_middle + grad_in
        unused, media_pull = jax.vjp(normalize, media_full, gains[0], shifts[0])
        grad_media_layer, gain_media, shift_media = media_pull(
            grad_joined[:, :PATCH].reshape(images * PATCH, width)
        )
        media_part = media_part + grad_media_layer
        grads[layer] = (
            grad_wq,
            grad_wk,
            grad_wv,
            grad_out,
            grad_up,
            grad_down,
            gain_media,
            shift_media,
            gain_latent,
            shift_latent,
            gain_feed,
            shift_feed,
        )
    media_total, gain_media_all, shift_media_all = (
        lax.psum(media_part.astype(jnp.bfloat16), "mp").astype(jnp.float32),
        lax.psum(jnp.stack([g[6] for g in grads]).astype(jnp.bfloat16), "mp").astype(jnp.float32),
        lax.psum(jnp.stack([g[7] for g in grads]).astype(jnp.bfloat16), "mp").astype(jnp.float32),
    )
    gain_stack = jnp.stack(
        [jnp.stack([gain_media_all[layer], grads[layer][8]]) for layer in range(layers)]
    )
    shift_stack = jnp.stack(
        [jnp.stack([shift_media_all[layer], grads[layer][9]]) for layer in range(layers)]
    )
    feed_stack = jnp.stack(
        [jnp.stack([grads[layer][10], grads[layer][11]]) for layer in range(layers)]
    )
    summed = (
        lax.psum_scatter(jnp.stack([g[0] for g in grads]), "dp", scatter_dimension=1, tiled=True),
        lax.psum_scatter(jnp.stack([g[1] for g in grads]), "dp", scatter_dimension=1, tiled=True),
        lax.psum_scatter(jnp.stack([g[2] for g in grads]), "dp", scatter_dimension=1, tiled=True),
        lax.psum_scatter(jnp.stack([g[3] for g in grads]), "dp", scatter_dimension=2, tiled=True),
        lax.psum_scatter(jnp.stack([g[4] for g in grads]), "dp", scatter_dimension=1, tiled=True),
        lax.psum_scatter(jnp.stack([g[5] for g in grads]), "dp", scatter_dimension=2, tiled=True),
        lax.psum_scatter(gain_stack, "dp", scatter_dimension=2, tiled=True),
        lax.psum_scatter(shift_stack, "dp", scatter_dimension=2, tiled=True),
        lax.psum_scatter(feed_stack, "dp", scatter_dimension=2, tiled=True),
    )
    return (
        result,
        media_total,
        grad_state,
        summed[0],
        summed[1],
        summed[2],
        summed[3],
        summed[4],
        summed[5],
        summed[6],
        summed[7],
        summed[8],
    )


MESH = pl.DeviceIdType.MESH
F32 = jnp.float32
BF16 = jnp.bfloat16
SLOTS = 3
HEADS_HERE = 4
PLANE = 4
ROWS = SLOTS * LATENTS
HALF = LATENTS // 2
WIDTH = 1024
KEYS = PATCH + LATENTS
HEAD_COLS = HEADS_HERE * HEAD_DIM
UNITS = 512
COPIES = 320
LOCALS = 32
QUERY, OUT, KEY_VALUE = (0, 256), (256, 512), (512, 1024)


ORDER = (
    ("enter",), ("SC", 0, "u"), ("AF", 0, "q"), ("OA", 0), ("prepare",), ("OF", 0), ("OW", 0), ("AF", 0, "k"),
    ("SC", 1, "d"), ("GO", 1, 0), ("OA", 1), ("OF", 1), ("OW", 1), ("vectors_out",), ("GO", 1, 1), ("AF", 1, "q"),
    ("AN", 0, "q"), ("WF", 0, "u"), ("vectors_in",), ("LN", 0, 0), ("LN", 0, 1), ("MN", 2), ("AN", 0, "k"), ("MN", 1),
    ("LN", 0, 2), ("AN", 1, "q"), ("MN", 0), ("AF", 1, "k"), ("GH", 1, 0), ("SC", 0, "d"), ("GH", 1, 1),
    ("A1", 0, "q"), ("AN", 1, "k"), ("A1", 0, "k"), ("A1", 1, "q"), ("WN", 0, "u"), ("WF", 0, "d"), ("A2", 0, "q"),
    ("SC", 1, "u"), ("A1", 1, "k"), ("A2", 0, "k"), ("A2", 1, "q"), ("WN", 0, "d"), ("A2", 1, "k"), ("WF", 1, "u"),
    ("RD", 0, "nearu"), ("RD", 0, "asecondq"), ("RD", 0, "asecondk"), ("KM", 0, 1), ("AT", 0, 1), ("KM", 0, 0),
    ("AT", 0, 0), ("MI", 0, 1), ("RD", 1, "asecondq"), ("KM", 0, 2), ("AT", 0, 2), ("MI", 0, 0), ("WN", 1, "u"),
    ("WF", 1, "d"), ("RD", 1, "asecondk"), ("KM", 1, 2), ("KM", 1, 0), ("KM", 1, 1), ("MI", 0, 2), ("RH", 0, 1),
    ("RD", 0, "neard"), ("FF", 0, 1), ("RH", 0, 0), ("RH", 0, 2), ("FS", 0, 1), ("FF", 0, 0), ("FF", 0, 2),
    ("FS", 0, 0), ("FS", 0, 2), ("NS", 0, 1), ("WN", 1, "d"), ("LN", 1, 1), ("AT", 1, 1), ("MI", 1, 1), ("NS", 0, 0),
    ("NS", 0, 2), ("LN", 1, 0), ("AT", 1, 0), ("LN", 1, 2), ("AT", 1, 2), ("RD", 1, "nearu"),
    ("ST", "afar", "anear", "afirst", "asecond"), ("MI", 1, 0), ("RH", 1, 1), ("MI", 1, 2), ("GO", 1, 2),
    ("RD", 1, "neard"), ("FF", 1, 1), ("RH", 1, 0), ("FS", 1, 1), ("FF", 1, 0), ("RH", 1, 2), ("GH", 1, 2),
    ("FS", 1, 0), ("FF", 1, 2), ("ST", "scatter", "far", "near"), ("NS", 1, 1), ("FB", 1, 1), ("FS", 1, 2), ("RE", 1),
    ("BS", 1, 1), ("NS", 1, 0), ("FB", 1, 0), ("RE", 0), ("BS", 1, 0), ("NS", 1, 2), ("FB", 1, 2), ("GA", 1, "d"),
    ("GA", 1, "u"), ("BS", 1, 2), ("SF", 1, 1), ("GB", 1, "u"), ("SF", 1, 0), ("GB", 1, "d"), ("MB", 1, 1),
    ("AB", 1, 1), ("MB", 1, 0), ("AB", 1, 0), ("SF", 1, 2), ("SB", 1, 1), ("MD", 1, 0), ("SB", 1, 0), ("MB", 1, 2),
    ("AB", 1, 2), ("MD", 1, 2), ("ST", "grad1", "gradhand1"), ("SB", 1, 2), ("MD", 1, 1), ("KG", 1), ("GH", 0, 1),
    ("GH", 0, 0), ("QG", 1), ("RE", 2), ("FB", 0, 1), ("GH", 0, 2), ("FB", 0, 0), ("BS", 0, 1), ("FB", 0, 2),
    ("GA", 0, "d"), ("BS", 0, 0), ("GB", 0, "d"), ("BS", 0, 2), ("GF", 1, "u"), ("GA", 0, "u"), ("GF", 1, "d"),
    ("S2", 1, "k"), ("SF", 0, 1), ("MB", 0, 1), ("AB", 0, 1), ("MD", 0, 1), ("SF", 0, 2), ("SF", 0, 0),
    ("SN", 1, "k"), ("SB", 0, 1), ("MB", 0, 2), ("AB", 0, 2), ("MD", 0, 2), ("MB", 0, 0), ("AB", 0, 0), ("MD", 0, 0),
    ("KG", 0), ("SB", 0, 0), ("QG", 0), ("GB", 0, "u"), ("S2", 1, "q"), ("GP", 1, "d"), ("SB", 0, 2),
    ("vector_sums_out",), ("SR", 1, "k"), ("GF", 0, "d"), ("SE", 1, "k"), ("vector_sums_in",), ("GF", 0, "u"),
    ("vector_sums_end",), ("SN", 1, "q"), ("S2", 0, "k"), ("S2", 0, "q"), ("SN", 0, "k"), ("SN", 0, "q"),
    ("SR", 1, "q"), ("GP", 1, "u"), ("GP", 0, "d"), ("SE", 1, "q"), ("SR", 0, "k"), ("SR", 0, "q"), ("GP", 0, "u"),
    ("SE", 0, "k"), ("SE", 0, "q"), ("close",),
)


class Copies:
    def __init__(self, send_sems, recv_sems, local_sems):
        self.send_sems, self.recv_sems, self.local_sems = send_sems, recv_sems, local_sems
        self.used = self.used_local = 0
        self.sending = []

    def start(self, source, target, device):
        copy = pltpu.make_async_remote_copy(
            src_ref=source,
            dst_ref=target,
            send_sem=self.send_sems.at[self.used],
            recv_sem=self.recv_sems.at[self.used],
            device_id=device,
            device_id_type=MESH,
        )
        self.used += 1
        copy.start()
        self.sending.append(copy)
        return copy

    def start_local(self, source, target):
        copy = pltpu.make_async_copy(source, target, self.local_sems.at[self.used_local])
        self.used_local += 1
        copy.start()
        return copy

    def sent(self, copies):
        for copy in copies:
            if any(kept is copy for kept in self.sending):
                copy.wait_send()
                self.sending = [kept for kept in self.sending if kept is not copy]


def matmul(left, right):
    return jnp.dot(left, right, preferred_element_type=F32)


def matmul_nt(left, right):
    return lax.dot_general(left, right, (((1,), (1,)), ((), ())), preferred_element_type=F32)


def matmul_tn(left, right):
    return lax.dot_general(left, right, (((0,), (0,)), ((), ())), preferred_element_type=F32)


def loop(count, body):
    def step(index, carry):
        body(index)
        return carry

    lax.fori_loop(0, count, step, 0)


def centred(values):
    centre = values - jnp.mean(values, -1, keepdims=True)
    scale = lax.rsqrt(jnp.mean(centre * centre, -1, keepdims=True) + 1e-05)
    return centre * scale, scale


def norm_back(grad, gain, unit, scale):
    inner = grad * gain
    return scale * (
        inner
        - jnp.mean(inner, -1, keepdims=True)
        - unit * jnp.mean(inner * unit, -1, keepdims=True)
    )


def column_sums(values):
    return jnp.sum(values, 0, keepdims=True)


def slot_rows(slot):
    return pl.ds(slot * LATENTS, LATENTS)


def fused_kernel(
    patch_rows,
    image_count,
    media,
    latents,
    cotangent,
    gains,
    shifts,
    w_query,
    w_key,
    w_value,
    w_out_t,
    w_up,
    w_down_t,
    out_latents,
    out_media,
    out_media_pair,
    out_state,
    out_attn,
    out_up,
    out_down_t,
    out_vectors,
    AW,
    FW,
    VB,
    VG,
    GS,
    J,
    X,
    Y,
    Q,
    KV,
    O,
    PR,
    H,
    GP,
    G,
    DY,
    DU,
    ZP,
    PS,
    PRECV,
    TS,
    TR,
    AS,
    AR,
    DX,
    DH,
    DV,
    DAB,
    DQ,
    DKV,
    MG,
    RF1,
    RF2,
    RA1A,
    RA1B,
    RA2A,
    RA2B,
    RA3,
    RA4,
    VS,
    VR,
    MASK,
    send_sems,
    recv_sems,
    local_sems,
):
    me = lax.axis_index("dp")
    half = lax.axis_index("mp")
    z, c = me // 4, me % 4
    zh, zl = z // 2, z % 2
    y, x = c // 2, c % 2
    columns = (c, y * 2 + 1 - x, (1 - y) * 2 + x, 3 - c)
    plane = tuple((z * 4 + column, half) for column in columns)
    near = ((zh * 2 + 1 - zl) * 4 + c, half)
    far = (((1 - zh) * 2 + zl) * 4 + c, half)
    sibling = (me, 1 - half)
    copies = Copies(send_sems, recv_sems, local_sems)
    mine = pl.ds(pl.multiple_of(half * HALF, 32), HALF)
    other = pl.ds(pl.multiple_of((1 - half) * HALF, 32), HALF)
    first = jnp.where(half == 0, 1.0, 0.0).astype(F32)
    flying = {}
    tasks = {}

    def task(function):
        tasks[function.__name__] = function
        return function

    def keep(name, started):
        flying[name] = started if isinstance(started, list) else [started]

    def arrived(name):
        for copy in flying[name]:
            copy.wait_recv()
        return flying[name]

    def landed(name):
        for copy in flying.pop(name):
            copy.wait()

    def unit_columns(index):
        return pl.ds(pl.multiple_of(columns[index] * UNITS, UNITS), UNITS)

    up_part, down_part = pl.ds(0, UNITS), pl.ds(UNITS, UNITS)
    parts = {"u": up_part, "d": down_part}
    chunks = {"k": ((512, w_key), (768, w_value)), "q": ((0, w_query), (256, w_out_t))}

    @task
    def enter():
        blank = jnp.zeros((1, gains.shape[2]), F32)
        piece = jnp.concatenate(
            [
                source[which, layer : layer + 1, :].astype(F32)
                for source in (gains, shifts)
                for layer in range(2)
                for which in range(3)
            ]
            + [blank] * 4,
            0,
        )
        odd = c % 2 == 1
        VB[...] = jnp.concatenate(
            [jnp.where(odd, 0.0, piece), jnp.where(odd, piece, 0.0)], 1
        ).astype(BF16)
        barrier = pltpu.get_barrier_semaphore()
        for step in range(1, 16):
            pl.semaphore_signal(
                barrier, inc=1, device_id=((me + step) % 16, half), device_id_type=MESH
            )
        pl.semaphore_signal(barrier, inc=1, device_id=sibling, device_id_type=MESH)
        pl.semaphore_wait(barrier, 16)

    @task
    def vectors_out():
        keep(
            "vectors",
            [copies.start(VB, VG.at[me], ((me + step) % 16, half)) for step in range(1, 16)],
        )

    def own_attn(layer):
        keep(
            f"own_attn{layer}",
            [
                copies.start_local(
                    source.at[layer], AW.at[layer, zh, zl, y, x, :, pl.ds(low, 256)]
                )
                for chunk in "kq"
                for low, source in chunks[chunk]
            ],
        )

    def own_feed(layer):
        keep(
            f"own_feed{layer}",
            [
                copies.start_local(
                    source.at[layer, :, unit_columns(0)], FW.at[layer, zh, zl, c, :, part]
                )
                for source, part in ((w_up, up_part), (w_down_t, down_part))
            ],
        )

    def feed_scatter(layer, part):
        source = w_up if part == "u" else w_down_t
        keep(
            f"scatter{part}{layer}",
            [
                copies.start(
                    source.at[layer, :, unit_columns(index)],
                    FW.at[layer, zh, zl, c, :, parts[part]],
                    plane[index],
                )
                for index in (3, 1, 2)
            ],
        )

    def feed_far(layer, part):
        arrived(f"scatter{part}{layer}")
        block = FW.at[layer, zh, zl, :, :, parts[part]]
        keep(f"far{part}{layer}", copies.start(block, block, far))

    def feed_near(layer, part):
        arrived(f"far{part}{layer}")
        block = FW.at[layer, :, zl, :, :, parts[part]]
        keep(f"near{part}{layer}", copies.start(block, block, near))

    def attn_far(layer, chunk):
        keep(
            f"afar{chunk}{layer}",
            [
                copies.start(
                    source.at[layer], AW.at[layer, zh, zl, y, x, :, pl.ds(low, 256)], far
                )
                for low, source in chunks[chunk]
            ],
        )

    def attn_near(layer, chunk):
        arrived(f"afar{chunk}{layer}")
        block = AW.at[layer, :, zl, y, x, :, pl.ds(chunks[chunk][0][0], 512)]
        keep(f"anear{chunk}{layer}", copies.start(block, block, near))

    def attn_first(layer, chunk):
        arrived(f"anear{chunk}{layer}")
        keep(
            f"afirst{chunk}{layer}",
            [
                copies.start(block, block, plane[1 + side])
                for side in range(2)
                for block in [AW.at[layer, :, :, y, x, :, pl.ds(chunks[chunk][side][0], 256)]]
            ],
        )

    def attn_second(layer, chunk):
        arrived(f"afirst{chunk}{layer}")
        block_a = AW.at[layer, :, :, y, :, :, pl.ds(chunks[chunk][0][0], 256)]
        block_b = AW.at[layer, :, :, :, x, :, pl.ds(chunks[chunk][1][0], 256)]
        keep(
            f"asecond{chunk}{layer}",
            [copies.start(block_a, block_a, plane[2]), copies.start(block_b, block_b, plane[1])],
        )

    @task
    def prepare():
        head_row = lax.broadcasted_iota(jnp.int32, (HEAD_COLS, HEAD_COLS), 0) // HEAD_DIM
        head_column = lax.broadcasted_iota(jnp.int32, (HEAD_COLS, HEAD_COLS), 1) // HEAD_DIM
        MASK[...] = jnp.where(head_row == head_column, 1.0, 0.0).astype(F32)
        VG[me] = VB[...]
        VS[...] = jnp.zeros_like(VS)
        for slot in range(SLOTS):
            rows = slot_rows(slot)
            X[0, rows, :] = latents[rows, :].astype(F32)
            live = jnp.where(slot < image_count[0], 1.0, 0.0).astype(F32)
            grad = cotangent[rows, :].astype(F32) * live
            DX[rows, :] = grad
            DY[1, slot, 0] = grad.astype(BF16)

    @task
    def vectors_in():
        arrived("vectors")
        for tile in range(8):
            GS[:, tile * 128 : tile * 128 + 128] = VG[2 * tile].astype(F32) + VG[
                2 * tile + 1
            ].astype(F32)

    def gain(layer, which):
        return GS[layer * 3 + which : layer * 3 + which + 1, :]

    def shift(layer, which):
        return GS[6 + layer * 3 + which : 7 + layer * 3 + which, :]

    def media_norm(slot):
        def body(index):
            rows = pl.ds(pl.multiple_of(slot * PATCH + index * 64, 64), 64)
            keys = pl.ds(pl.multiple_of(index * 64, 64), 64)
            unit, _ = centred(media[rows, :].astype(F32))
            for layer in range(2):
                J[layer, slot, keys, :] = (unit * gain(layer, 0) + shift(layer, 0)).astype(BF16)

        loop(4, body)

    def latent_norm(layer, slot):
        if layer > 0:
            copies.sent(arrived(f"state{layer}{slot}"))
        unit, _ = centred(X[layer, slot_rows(slot), :])
        J[layer, slot, PATCH:, :] = (unit * gain(layer, 1) + shift(layer, 1)).astype(BF16)

    def attn_weight(layer, span):
        return AW[layer, :, :, :, :, :, span[0] : span[1]].reshape(WIDTH, span[1] - span[0])

    def feed_weight(layer, part):
        low = 0 if part == "u" else UNITS
        return FW[layer, :, :, :, :, low : low + UNITS].reshape(WIDTH, UNITS)

    def stacked(value):
        return (jnp.concatenate([value.astype(F32)] * HEADS_HERE, 0) * MASK[...]).astype(BF16)

    def unstacked(value):
        return jnp.sum((value * MASK[...]).reshape(HEADS_HERE, LATENTS, HEAD_COLS), 0)

    def media_keys(layer, slot):
        KV[layer, slot, 0:PATCH] = matmul(
            J[layer, slot, 0:PATCH, :], attn_weight(layer, KEY_VALUE)
        ).astype(BF16)

    def attention(layer, slot):
        rows = J[layer, slot, PATCH:, :]
        KV[layer, slot, PATCH:] = matmul(rows, attn_weight(layer, KEY_VALUE)).astype(BF16)
        query = matmul(rows, attn_weight(layer, QUERY)).astype(BF16)
        Q[layer, slot] = query
        scores = matmul_nt(stacked(query), KV[layer, slot, :, 0:256]) * 0.125
        key = lax.broadcasted_iota(jnp.int32, (HEAD_COLS, KEYS), 1)
        scores = jnp.where((key >= PATCH) | (key < patch_rows[slot]), scores, NEGATIVE)
        expo = jnp.exp(scores - jnp.max(scores, -1, keepdims=True))
        probs = expo / jnp.sum(expo, -1, keepdims=True)
        PR[layer, slot] = probs
        mixed = unstacked(matmul(probs.astype(BF16), KV[layer, slot, :, 256:512])).astype(BF16)
        O[layer, slot] = mixed
        AS[slot] = matmul_nt(mixed, attn_weight(layer, OUT)).astype(BF16)
        keep(f"mix{layer}{slot}", copies.start(AS.at[slot], AR.at[slot], sibling))

    def spread(name, buffer, layer, slot):
        block = buffer.at[layer, slot, 0, mine]
        keep(
            f"{name}{layer}{slot}",
            [
                copies.start(block, buffer.at[layer, slot, index, mine], plane[index])
                for index in (3, 1, 2)
            ],
        )

    def hand_over(name, buffer, layer, slot):
        started = []
        for index, copy in zip((3, 1, 2), flying[f"{name}{layer}{slot}"]):
            block = buffer.at[layer, slot, index, mine]
            copy.wait_recv()
            started.append(copies.start(block, block, sibling))
        keep(f"{name}hand{layer}{slot}", started)

    def middle(layer, slot):
        copies.sent(arrived(f"mix{layer}{slot}"))
        rows = slot_rows(slot)
        value = X[layer, rows, :] + (AS[slot].astype(F32) + AR[slot].astype(F32))
        Y[layer, rows, :] = value
        unit, _ = centred(value)
        H[layer, slot, 0] = (unit * gain(layer, 2) + shift(layer, 2)).astype(BF16)
        spread("rows", H, layer, slot)

    def send_pair(name, way, slot):
        PS[slot] = ZP[slot, :, other, :].astype(BF16)
        keep(name, copies.start(PS.at[slot], PRECV.at[way, slot], sibling))

    def feed_forward(layer, slot):
        arrived(f"rowshand{layer}{slot}")
        pre_act = matmul(H[layer, slot].reshape(256, WIDTH), feed_weight(layer, "u"))
        bell = 0.5 * (1.0 + lax.erf(pre_act * 0.7071067811865476))
        GP[layer, slot] = bell + pre_act * jnp.exp(-0.5 * pre_act * pre_act) * 0.3989422804014327
        act = (pre_act * bell).astype(BF16)
        G[layer, slot] = act
        ZP[slot] = matmul_nt(act, feed_weight(layer, "d")).reshape(PLANE, LATENTS, WIDTH)
        send_pair(f"pair0{layer}{slot}", 0, slot)

    def plane_sum(way, layer, slot):
        copies.sent(arrived(f"pair{way}{layer}{slot}"))
        started = []
        for index in (3, 1, 2):
            TS[slot, index - 1] = (
                ZP[slot, index, mine, :] + PRECV[way, slot, index].astype(F32)
            ).astype(BF16)
            started.append(
                copies.start(TS.at[slot, index - 1], TR.at[way, slot, index - 1], plane[index])
            )
        keep(f"away{way}{layer}{slot}", started)

    def feed_sum(way, layer, slot):
        total = ZP[slot, 0, mine, :] + PRECV[way, slot, 0].astype(F32)
        copies.sent(arrived(f"away{way}{layer}{slot}"))
        for index in range(3):
            total = total + TR[way, slot, index].astype(F32)
        return total

    def half_rows(slot):
        return pl.ds(pl.multiple_of(slot * LATENTS + half * HALF, HALF), HALF)

    def next_state(layer, slot):
        rows = half_rows(slot)
        X[layer + 1, rows, :] = Y[layer, rows, :] + feed_sum(0, layer, slot)
        block = X.at[layer + 1, rows]
        keep(f"state{layer + 1}{slot}", copies.start(block, block, sibling))

    def result(slot):
        copies.sent(arrived(f"state2{slot}"))
        live = jnp.where(slot < image_count[0], 1.0, 0.0).astype(F32)
        rows = slot_rows(slot)
        out_latents[rows, :] = (X[2, rows, :] * live).astype(BF16)

    def feed_back(layer, slot):
        arrived(f"gradhand{layer}{slot}")
        grad_act = matmul(DY[layer, slot].reshape(256, WIDTH), feed_weight(layer, "d"))
        up_low = (grad_act * GP[layer, slot]).astype(BF16)
        DU[slot] = up_low
        ZP[slot] = matmul_nt(up_low, feed_weight(layer, "u")).reshape(PLANE, LATENTS, WIDTH)
        send_pair(f"pair1{layer}{slot}", 1, slot)

    def swap_feed(layer, slot):
        rows = half_rows(slot)
        DH[rows, :] = feed_sum(1, layer, slot)
        block = DH.at[rows]
        keep(f"feed{layer}{slot}", copies.start(block, block, sibling))

    def add_sums(row_gain, row_shift, grad, unit, factor):
        for row, value in ((row_gain, grad * unit), (row_shift, grad)):
            VS[row : row + 1, :] = VS[row : row + 1, :] + column_sums(value) * factor

    def middle_back(layer, slot):
        copies.sent(arrived(f"feed{layer}{slot}"))
        rows = slot_rows(slot)
        unit, scale = centred(Y[layer, rows, :])
        grad = DH[rows, :]
        grad_middle = DX[rows, :] + norm_back(grad, gain(layer, 2), unit, scale)
        DV[rows, :] = grad_middle
        DAB[rows, :] = grad_middle.astype(BF16)
        add_sums(8 + layer * 2, 9 + layer * 2, grad, unit, first)

    def attention_back(layer, slot):
        grad_mixed = matmul(DAB[slot_rows(slot), :], attn_weight(layer, OUT)).astype(BF16)
        grads = stacked(grad_mixed)
        probs = PR[layer, slot]
        grad_probs = matmul_nt(grads, KV[layer, slot, :, 256:512])
        grad_scores = (
            probs * (grad_probs - jnp.sum(grad_probs * probs, -1, keepdims=True))
        ).astype(BF16)
        DKV[slot, :, 256:512] = matmul_tn(probs.astype(BF16), grads).astype(BF16)
        queries = stacked(Q[layer, slot])
        DKV[slot, :, 0:256] = (matmul_tn(grad_scores, queries) * 0.125).astype(BF16)
        grad_query = unstacked(matmul(grad_scores, KV[layer, slot, :, 0:256])) * 0.125
        DQ[slot] = grad_query.astype(BF16)
        AS[slot] = (
            matmul_nt(DQ[slot], attn_weight(layer, QUERY))
            + matmul_nt(DKV[slot, PATCH:, :], attn_weight(layer, KEY_VALUE))
        ).astype(BF16)
        keep(f"norm{layer}{slot}", copies.start(AS.at[slot], AR.at[slot], sibling))

    def state_back(layer, slot):
        copies.sent(arrived(f"norm{layer}{slot}"))
        rows = slot_rows(slot)
        unit, scale = centred(X[layer, rows, :])
        grad = AS[slot].astype(F32) + AR[slot].astype(F32)
        grad_in = DV[rows, :] + norm_back(grad, gain(layer, 1), unit, scale)
        if layer > 0:
            DX[rows, :] = grad_in
            DY[layer - 1, slot, 0] = grad_in.astype(BF16)
            spread("grad", DY, layer - 1, slot)
        else:
            out_state[rows, :] = grad_in
        add_sums(layer * 2 + 1, layer * 2 + 5, grad, unit, first)

    def media_back(layer, slot):
        def body(index):
            keys = pl.ds(pl.multiple_of(index * 128, 128), 128)
            rows = pl.ds(pl.multiple_of(slot * PATCH + index * 128, 128), 128)
            grad = matmul_nt(DKV[slot, keys, :], attn_weight(layer, KEY_VALUE))
            unit, scale = centred(media[rows, :].astype(F32))
            piece = norm_back(grad, gain(layer, 0), unit, scale)
            if layer == 1:
                MG[rows, :] = piece
            else:
                DY[1, slot, pl.ds(index * 2, 2)] = (
                    (MG[rows, :] + piece).astype(BF16).reshape(2, LATENTS, WIDTH)
                )
            add_sums(layer * 2, layer * 2 + 4, grad, unit, 1.0)

        loop(2, body)
        if layer == 0:
            rows = pl.ds(slot * PATCH, PATCH)
            block = DY.at[1, slot]
            keep(f"media{slot}", copies.start(block, out_media_pair.at[slot], sibling))
            keep(f"media_own{slot}", copies.start_local(block, out_media.at[slot]))

    def add_into(target, received):
        target[...] = (target[...].astype(F32) + received[...].astype(F32)).astype(BF16)

    def feed_grad(layer, part, low):
        left, right = (DY, G.at[layer]) if part == "d" else (H, DU)
        begin = UNITS if part == "d" else 0

        def body(high):
            cols = pl.ds(pl.multiple_of((high * 2 + low) * 256, 256), 256)
            sums = matmul_tn(
                left[layer, :, :, :, cols].reshape(4 * ROWS, 256),
                right[...].reshape(4 * ROWS, UNITS),
            )
            FW[layer, high, low, :, :, begin : begin + UNITS] = sums.astype(BF16).reshape(
                PLANE, 64, UNITS
            )

        loop(2, body)

    def feed_grad_away(layer, part):
        feed_grad(layer, part, 1 - zl)
        keep(
            f"gnear{part}{layer}",
            copies.start(
                FW.at[layer, :, 1 - zl, :, :, parts[part]],
                RF1.at[layer, :, :, :, parts[part]],
                near,
            ),
        )

    def feed_grad_stay(layer, part):
        feed_grad(layer, part, zl)

    def feed_sum_far(layer, part):
        arrived(f"gnear{part}{layer}")

        def add(high):
            for index in range(4):
                add_into(
                    FW.at[layer, high, zl, index, :, parts[part]],
                    RF1.at[layer, high, index, :, parts[part]],
                )

        add(1 - zh)
        block = FW.at[layer, 1 - zh, zl, :, :, parts[part]]
        keep(f"gfar{part}{layer}", copies.start(block, RF2.at[layer, :, :, parts[part]], far))
        add(zh)

    def feed_sum_plane(layer, part):
        arrived(f"gfar{part}{layer}")
        target = out_up if part == "u" else out_down_t
        started = []
        for index in (3, 1, 2, 0):
            column = columns[index]
            block = FW.at[layer, zh, zl, column, :, parts[part]]
            add_into(block, RF2.at[layer, column, :, parts[part]])
            if index > 0:
                started.append(copies.start(block, target.at[layer, c], plane[index]))
            else:
                keep(f"gown{part}{layer}", copies.start_local(block, target.at[layer, c]))
        keep(f"gplane{part}{layer}", started)

    def attn_grad_query(layer):
        def body(index):
            cols = pl.ds(pl.multiple_of(index * 256, 256), 256)
            high, low = index // 2, index % 2
            query_part = matmul_tn(
                J[layer, :, PATCH:, cols].reshape(ROWS, 256), DQ[...].reshape(ROWS, HEAD_COLS)
            )
            AW[layer, high, low, :, :, :, 0:256] = query_part.astype(BF16).reshape(2, 2, 64, 256)
            out_part = matmul_tn(DAB[:, cols], O[layer].reshape(ROWS, HEAD_COLS))
            AW[layer, high, low, :, :, :, 256:512] = out_part.astype(BF16).reshape(2, 2, 64, 256)

        loop(4, body)
        attn_sum_first(layer, "q")

    def attn_grad_key(layer):
        def body(index):
            cols = pl.ds(pl.multiple_of(index * 256, 256), 256)
            high, low = index // 2, index % 2
            key_part = matmul_tn(
                J[layer, :, :, cols].reshape(SLOTS * KEYS, 256), DKV[...].reshape(SLOTS * KEYS, 512)
            )
            AW[layer, high, low, :, :, :, 512:1024] = key_part.astype(BF16).reshape(2, 2, 64, 512)

        loop(4, body)
        attn_sum_first(layer, "k")

    def low_columns(chunk, side):
        return pl.ds(chunks[chunk][side][0], 256)

    def short_columns(chunk):
        return pl.ds(0 if chunk == "q" else 256, 256)

    def attn_sum_first(layer, chunk):
        here = short_columns(chunk)
        keep(
            f"gfirst{chunk}{layer}",
            [
                copies.start(
                    AW.at[layer, :, :, 1 - y, :, :, low_columns(chunk, 0)],
                    RA1A.at[layer, :, :, :, :, here],
                    plane[2],
                ),
                copies.start(
                    AW.at[layer, :, :, :, 1 - x, :, low_columns(chunk, 1)],
                    RA1B.at[layer, :, :, :, :, here],
                    plane[1],
                ),
            ],
        )

    def attn_sum_second(layer, chunk):
        arrived(f"gfirst{chunk}{layer}")
        here, cols_a, cols_b = short_columns(chunk), low_columns(chunk, 0), low_columns(chunk, 1)

        def add(side_a, side_b):
            def body(index):
                high, low = index // 2, index % 2
                add_into(
                    AW.at[layer, high, low, y, side_a, :, cols_a],
                    RA1A.at[layer, high, low, side_a, :, here],
                )
                add_into(
                    AW.at[layer, high, low, side_b, x, :, cols_b],
                    RA1B.at[layer, high, low, side_b, :, here],
                )

            loop(4, body)

        add(1 - x, 1 - y)
        keep(
            f"gsecond{chunk}{layer}",
            [
                copies.start(
                    AW.at[layer, :, :, y, 1 - x, :, cols_a],
                    RA2A.at[layer, :, :, :, here],
                    plane[1],
                ),
                copies.start(
                    AW.at[layer, :, :, 1 - y, x, :, cols_b],
                    RA2B.at[layer, :, :, :, here],
                    plane[2],
                ),
            ],
        )
        add(x, y)

    def attn_sum_near(layer, chunk):
        arrived(f"gsecond{chunk}{layer}")
        here, cols_a, cols_b = short_columns(chunk), low_columns(chunk, 0), low_columns(chunk, 1)
        both = pl.ds(chunks[chunk][0][0], 512)

        def add(low):
            for high in range(2):
                add_into(
                    AW.at[layer, high, low, y, x, :, cols_a], RA2A.at[layer, high, low, :, here]
                )
                add_into(
                    AW.at[layer, high, low, y, x, :, cols_b], RA2B.at[layer, high, low, :, here]
                )

        add(1 - zl)
        keep(
            f"ganear{chunk}{layer}",
            copies.start(AW.at[layer, :, 1 - zl, y, x, :, both], RA3.at[layer, :, :, both], near),
        )
        add(zl)

    def attn_sum_far(layer, chunk):
        arrived(f"ganear{chunk}{layer}")
        both = pl.ds(chunks[chunk][0][0], 512)

        def add(high):
            add_into(AW.at[layer, high, zl, y, x, :, both], RA3.at[layer, high, :, both])

        add(1 - zh)
        keep(
            f"gafar{chunk}{layer}",
            copies.start(
                AW.at[layer, 1 - zh, zl, y, x, :, both], RA4.at[layer, :, both], far
            ),
        )
        add(zh)

    def attn_sum_end(layer, chunk):
        arrived(f"gafar{chunk}{layer}")
        both = pl.ds(chunks[chunk][0][0], 512)
        out_attn[layer, :, both] = AW[layer, zh, zl, y, x, :, both].astype(F32) + RA4[
            layer, :, both
        ].astype(F32)

    @task
    def vector_sums_out():
        keep(
            "sums",
            [
                copies.start(
                    VS.at[:, pl.ds(pl.multiple_of((((me + step) % 16) // 2) * 128, 128), 128)],
                    VR.at[step],
                    ((me + step) % 16, half),
                )
                for step in range(1, 16)
            ],
        )

    @task
    def vector_sums_in():
        arrived("sums")
        total = VS[:, pl.ds(pl.multiple_of((me // 2) * 128, 128), 128)]
        for step in range(1, 16):
            total = total + VR[step]
        VR[0] = total
        keep("sums_pair", copies.start(VR.at[0], VR.at[16], sibling))

    @task
    def vector_sums_end():
        arrived("sums_pair")
        out_vectors[...] = VR[0] + VR[16]

    def settle(*names):
        for name, started in flying.items():
            if name.startswith(names):
                copies.sent(started)

    @task
    def close():
        for slot in range(SLOTS):
            arrived(f"media{slot}")
            landed(f"media_own{slot}")
        for layer in range(2):
            for part in "ud":
                arrived(f"gplane{part}{layer}")
                landed(f"gown{part}{layer}")
        copies.sent(list(copies.sending))

    def grad_spread(layer, slot):
        spread("grad", DY, layer, slot)

    def grad_hand(layer, slot):
        hand_over("grad", DY, layer, slot)

    def rows_hand(layer, slot):
        hand_over("rows", H, layer, slot)

    def forward_sum(layer, slot):
        plane_sum(0, layer, slot)

    def backward_sum(layer, slot):
        plane_sum(1, layer, slot)

    def own_wait(layer):
        landed(f"own_attn{layer}")
        landed(f"own_feed{layer}")

    def ready(layer, name):
        arrived(f"{name}{layer}")

    steps = dict(
        MN=media_norm, LN=latent_norm, KM=media_keys, AT=attention, MI=middle, RH=rows_hand,
        FF=feed_forward, FS=forward_sum, NS=next_state, RE=result, GO=grad_spread, GH=grad_hand,
        FB=feed_back, BS=backward_sum, SF=swap_feed, MB=middle_back, AB=attention_back,
        SB=state_back, MD=media_back, OA=own_attn, OF=own_feed, OW=own_wait, SC=feed_scatter,
        WF=feed_far, WN=feed_near, AF=attn_far, AN=attn_near, A1=attn_first, A2=attn_second,
        RD=ready, GA=feed_grad_away, GB=feed_grad_stay, GF=feed_sum_far, GP=feed_sum_plane,
        QG=attn_grad_query, KG=attn_grad_key, S2=attn_sum_second, SN=attn_sum_near,
        SR=attn_sum_far, SE=attn_sum_end, ST=settle,
    )
    for name, *arguments in ORDER:
        if name in tasks:
            tasks[name]()
        else:
            steps[name](*arguments)


def finish_kernel(
    latents, media_own, media_pair, state, attn, up, down_t, sums,
    to_latents, to_media, to_state, to_query, to_key, to_value, to_out_t, to_up, to_down_t,
    to_gains, to_shifts, to_feed,
):
    piece = to_gains.shape[2]
    odd = lax.axis_index("dp") % 2 == 1
    to_latents[...] = latents[...]
    to_state[...] = state[...]
    to_media[...] = media_own[...].astype(F32) + media_pair[...].astype(F32)
    to_query[...] = attn[:, :, 0:256]
    to_out_t[...] = attn[:, :, 256:512]
    to_key[...] = attn[:, :, 512:768]
    to_value[...] = attn[:, :, 768:1024]
    for layer in range(2):
        to_up[layer] = up[layer, 0].astype(F32)
        to_down_t[layer] = down_t[layer, 0].astype(F32)

    @pl.when(pl.program_id(0) == 0)
    def _():
        mine = jnp.where(odd, sums[:, piece:], sums[:, :piece])
        for index, target in enumerate((to_gains, to_shifts, to_feed)):
            for layer in range(2):
                row = index * 4 + layer * 2
                target[layer] = mine[row : row + 2, :]


def finish(latents, media_own, media_pair, state, attn, up, down_t, sums):
    steps = 4
    media_rows, rows, piece = SLOTS * PATCH // steps, ROWS // steps, attn.shape[1]
    spot = pl.BlockSpec((2, 2, piece), lambda step: (0, 0, 0))
    part = piece // steps
    media_block = pl.BlockSpec((media_rows, WIDTH), lambda step: (step, 0))
    row_block = pl.BlockSpec((rows, WIDTH), lambda step: (step, 0))
    head_block = pl.BlockSpec((2, part, HEAD_COLS), lambda step: (0, step, 0))
    unit_block = pl.BlockSpec((2, 1, piece, UNITS), lambda step: (0, step, 0, 0))

    def shape(*dims):
        return jax.ShapeDtypeStruct(dims, F32)

    flat = (SLOTS * PATCH, WIDTH)
    return pl.pallas_call(
        finish_kernel,
        name="finish",
        grid=(steps,),
        out_shape=[
            jax.ShapeDtypeStruct((ROWS, WIDTH), BF16),
            shape(*flat),
            shape(ROWS, WIDTH),
            shape(2, piece, HEAD_COLS),
            shape(2, piece, HEAD_COLS),
            shape(2, piece, HEAD_COLS),
            shape(2, piece, HEAD_COLS),
            shape(2, piece, steps * UNITS),
            shape(2, piece, steps * UNITS),
            shape(2, 2, piece),
            shape(2, 2, piece),
            shape(2, 2, piece),
        ],
        in_specs=[
            row_block,
            media_block,
            media_block,
            row_block,
            pl.BlockSpec((2, part, WIDTH), lambda step: (0, step, 0)),
            unit_block,
            unit_block,
            pl.BlockSpec((16, 128), lambda step: (0, 0)),
        ],
        out_specs=[
            row_block,
            media_block,
            row_block,
            head_block,
            head_block,
            head_block,
            head_block,
            pl.BlockSpec((2, piece, UNITS), lambda step: (0, 0, step)),
            pl.BlockSpec((2, piece, UNITS), lambda step: (0, 0, step)),
            spot,
            spot,
            spot,
        ],
        compiler_params=pltpu.CompilerParams(vmem_limit_bytes=64 * 2**20),
    )(latents, media_own.reshape(flat), media_pair.reshape(flat), state, attn, up, down_t, sums)


def fused(
    media, latents, patch_rows, image_count, cotangent, w_query, w_key, w_value, w_out, w_up, w_down,
    norm_gains, norm_shifts,
):
    w_out_t = jnp.swapaxes(w_out, 1, 2)
    w_down_t = jnp.swapaxes(w_down, 1, 2)
    gains = jnp.swapaxes(norm_gains, 0, 1)
    shifts = jnp.swapaxes(norm_shifts, 0, 1)

    vmem = pl.BlockSpec(memory_space=pltpu.VMEM)
    smem = pl.BlockSpec(memory_space=pltpu.SMEM)
    anywhere = pl.BlockSpec(memory_space=pl.ANY)

    def shape(dims, kind):
        return jax.ShapeDtypeStruct(dims, kind)

    results = pl.pallas_call(
        fused_kernel,
        name="resampler",
        out_shape=[
            shape((ROWS, WIDTH), BF16),
            shape((SLOTS, 4, LATENTS, WIDTH), BF16),
            shape((SLOTS, 4, LATENTS, WIDTH), BF16),
            shape((ROWS, WIDTH), F32),
            shape((2, 64, WIDTH), F32),
            shape((2, 4, 64, UNITS), BF16),
            shape((2, 4, 64, UNITS), BF16),
            shape((16, 128), F32),
        ],
        in_specs=[smem, smem] + [vmem] * 5 + [anywhere] * 6,
        out_specs=[vmem, anywhere, anywhere, vmem, vmem, anywhere, anywhere, vmem],
        scratch_shapes=[
            pltpu.VMEM((2, 2, 2, 2, 2, 64, 1024), BF16),
            pltpu.VMEM((2, 2, 2, 4, 64, 1024), BF16),
            pltpu.VMEM((16, 128), BF16),
            pltpu.VMEM((16, 16, 128), BF16),
            pltpu.VMEM((16, WIDTH), F32),
            pltpu.VMEM((2, SLOTS, KEYS, WIDTH), BF16),
            pltpu.VMEM((3, ROWS, WIDTH), F32),
            pltpu.VMEM((2, ROWS, WIDTH), F32),
            pltpu.VMEM((2, SLOTS, LATENTS, HEAD_COLS), BF16),
            pltpu.VMEM((2, SLOTS, KEYS, 2 * HEAD_COLS), BF16),
            pltpu.VMEM((2, SLOTS, LATENTS, HEAD_COLS), BF16),
            pltpu.VMEM((2, SLOTS, HEAD_COLS, KEYS), F32),
            pltpu.VMEM((2, SLOTS, PLANE, LATENTS, WIDTH), BF16),
            pltpu.VMEM((2, SLOTS, 4 * LATENTS, UNITS), F32),
            pltpu.VMEM((2, SLOTS, 4 * LATENTS, UNITS), BF16),
            pltpu.VMEM((2, SLOTS, PLANE, LATENTS, WIDTH), BF16),
            pltpu.VMEM((SLOTS, 4 * LATENTS, UNITS), BF16),
            pltpu.VMEM((SLOTS, PLANE, LATENTS, WIDTH), F32),
            pltpu.VMEM((SLOTS, PLANE, HALF, WIDTH), BF16),
            pltpu.VMEM((2, SLOTS, PLANE, HALF, WIDTH), BF16),
            pltpu.VMEM((SLOTS, 3, HALF, WIDTH), BF16),
            pltpu.VMEM((2, SLOTS, 3, HALF, WIDTH), BF16),
            pltpu.VMEM((SLOTS, LATENTS, WIDTH), BF16),
            pltpu.VMEM((SLOTS, LATENTS, WIDTH), BF16),
            pltpu.VMEM((ROWS, WIDTH), F32),
            pltpu.VMEM((ROWS, WIDTH), F32),
            pltpu.VMEM((ROWS, WIDTH), F32),
            pltpu.VMEM((ROWS, WIDTH), BF16),
            pltpu.VMEM((SLOTS, LATENTS, HEAD_COLS), BF16),
            pltpu.VMEM((SLOTS, KEYS, 2 * HEAD_COLS), BF16),
            pltpu.VMEM((SLOTS * PATCH, WIDTH), F32),
            pltpu.VMEM((2, 2, 4, 64, 1024), BF16),
            pltpu.VMEM((2, 4, 64, 1024), BF16),
            pltpu.VMEM((2, 2, 2, 2, 64, 512), BF16),
            pltpu.VMEM((2, 2, 2, 2, 64, 512), BF16),
            pltpu.VMEM((2, 2, 2, 64, 512), BF16),
            pltpu.VMEM((2, 2, 2, 64, 512), BF16),
            pltpu.VMEM((2, 2, 64, 1024), BF16),
            pltpu.VMEM((2, 64, 1024), BF16),
            pltpu.VMEM((16, WIDTH), F32),
            pltpu.VMEM((17, 16, 128), F32),
            pltpu.VMEM((HEAD_COLS, HEAD_COLS), F32),
            pltpu.SemaphoreType.DMA((COPIES,)),
            pltpu.SemaphoreType.DMA((COPIES,)),
            pltpu.SemaphoreType.DMA((LOCALS,)),
        ],
        compiler_params=pltpu.CompilerParams(
            collective_id=0, has_side_effects=True, vmem_limit_bytes=64 * 2**20
        ),
        cost_estimate=pl.CostEstimate(
            flops=18 * 10**9, bytes_accessed=20 * 10**6, transcendentals=10**6
        ),
    )(
        patch_rows, image_count, media, latents, cotangent, gains, shifts, w_query, w_key, w_value,
        w_out_t, w_up, w_down_t,
    )
    out_latents, media_own, media_pair, out_state, attn, up, down_t, sums = results
    whole = finish(out_latents, media_own, media_pair, out_state, attn, up, down_t, sums)
    turned = {6: True, 8: True}
    return tuple(
        jnp.swapaxes(array, 1, 2) if index in turned else array
        for index, array in enumerate(whole)
    )


def solution(mesh):
    body = fused if (mesh.shape["dp"], mesh.shape["mp"]) == (16, 2) else local
    placed = (
        P("dp", None),
        P("dp", None),
        P("dp"),
        P("dp"),
        P("dp", None),
        P(None, "dp", "mp"),
        P(None, "dp", "mp"),
        P(None, "dp", "mp"),
        P(None, "mp", "dp"),
        P(None, "dp", "mp"),
        P(None, "mp", "dp"),
        P(None, None, "dp"),
        P(None, None, "dp"),
    )
    return jax.shard_map(
        body,
        mesh=mesh,
        in_specs=placed,
        out_specs=(
            P("dp", None),
            P("dp", None),
            P("dp", None),
            P(None, "dp", "mp"),
            P(None, "dp", "mp"),
            P(None, "dp", "mp"),
            P(None, "mp", "dp"),
            P(None, "dp", "mp"),
            P(None, "mp", "dp"),
            P(None, None, "dp"),
            P(None, None, "dp"),
            P(None, None, "dp"),
        ),
        check_vma=False,
    )
```

```python
from functools import partial

import jax
import jax.numpy as jnp
from jax import lax
from jax.experimental import pallas as pl
from jax.experimental.pallas import tpu as pltpu
from jax.sharding import PartitionSpec as P

HEAD_DIM = 64
LATENTS = 64
PATCH = 256


NEGATIVE = -1000000000.0


def normalize(values, gain, shift):
    centre = values - jnp.mean(values, -1, keepdims=True)
    spread = jnp.mean(centre * centre, -1, keepdims=True)
    return centre * lax.rsqrt(spread + 1e-05) * gain + shift


def product(left, right):
    return jnp.dot(left, right, preferred_element_type=jnp.float32)


def outer_sum(left, right):
    return lax.dot_general(
        left, right, (((0,), (0,)), ((), ())), preferred_element_type=jnp.float32
    )


def back_product(left, right):
    return lax.dot_general(
        left, right, (((1,), (1,)), ((), ())), preferred_element_type=jnp.float32
    )


def forward_reduce(values):
    return lax.psum(values.astype(jnp.bfloat16), "mp").astype(jnp.float32)


def backward_reduce(values):
    return lax.psum(values.astype(jnp.bfloat16), "mp").astype(jnp.float32)


def key_scores(query_heads, key_heads, key_mask):
    scores = (
        jnp.einsum("iqhd,ikhd->ihqk", query_heads, key_heads, preferred_element_type=jnp.float32)
        * 0.125
    )
    return jnp.where(key_mask[:, None, None, :], scores, NEGATIVE)


def local(
    media,
    latents,
    patch_rows,
    image_count,
    cotangent,
    w_query,
    w_key,
    w_value,
    w_out,
    w_up,
    w_down,
    norm_gains,
    norm_shifts,
):
    images = patch_rows.shape[0]
    width = media.shape[1]
    heads_here = w_query.shape[2] // HEAD_DIM
    layers = w_query.shape[0]
    keys_len = PATCH + LATENTS
    key_mask = jnp.concatenate(
        [
            jnp.arange(PATCH, dtype=jnp.int32)[None, :] < patch_rows[:, None],
            jnp.ones((images, LATENTS), bool),
        ],
        1,
    )
    live = (jnp.arange(images, dtype=jnp.int32) < image_count[0]).astype(jnp.float32)
    live_rows = jnp.repeat(live, LATENTS)[:, None]
    media_full = media.astype(jnp.float32)
    state = latents.astype(jnp.float32)
    saved = []
    for layer in range(layers):
        gathered = (
            lax.all_gather(w_query[layer], "dp", axis=0, tiled=True),
            lax.all_gather(w_key[layer], "dp", axis=0, tiled=True),
            lax.all_gather(w_value[layer], "dp", axis=0, tiled=True),
            lax.all_gather(w_out[layer], "dp", axis=1, tiled=True),
            lax.all_gather(w_up[layer], "dp", axis=0, tiled=True),
            lax.all_gather(w_down[layer], "dp", axis=1, tiled=True),
            lax.all_gather(norm_gains[layer], "dp", axis=1, tiled=True),
            lax.all_gather(norm_shifts[layer], "dp", axis=1, tiled=True),
        )
        full_query, full_key, full_value, full_out, full_up, full_down, gain_rows, shift_rows = (
            gathered
        )
        gains = gain_rows.astype(jnp.float32)
        shifts = shift_rows.astype(jnp.float32)
        media_low = normalize(media_full, gains[0], shifts[0]).astype(jnp.bfloat16)
        latent_low = normalize(state, gains[1], shifts[1]).astype(jnp.bfloat16)
        query = product(latent_low, full_query).astype(jnp.bfloat16)
        joined = jnp.concatenate(
            [media_low.reshape(images, PATCH, width), latent_low.reshape(images, LATENTS, width)], 1
        ).reshape(images * keys_len, width)
        keys = product(joined, full_key).astype(jnp.bfloat16)
        values = product(joined, full_value).astype(jnp.bfloat16)
        scores = key_scores(
            query.reshape(images, LATENTS, heads_here, HEAD_DIM),
            keys.reshape(images, keys_len, heads_here, HEAD_DIM),
            key_mask,
        )
        top = jnp.max(scores, -1, keepdims=True)
        expo = jnp.exp(scores - top)
        total = jnp.sum(expo, -1, keepdims=True)
        probs_low = (expo / total).astype(jnp.bfloat16)
        log_total = top + jnp.log(total)
        mixed = jnp.einsum(
            "ihqk,ikhd->iqhd",
            probs_low,
            values.reshape(images, keys_len, heads_here, HEAD_DIM),
            preferred_element_type=jnp.float32,
        )
        mixed_low = mixed.astype(jnp.bfloat16).reshape(images * LATENTS, heads_here * HEAD_DIM)
        middle = state + forward_reduce(product(mixed_low, full_out))
        hidden_low = normalize(middle, gains[2], shifts[2]).astype(jnp.bfloat16)
        pre_act = product(hidden_low, full_up)
        act_low = jax.nn.gelu(pre_act, approximate=False).astype(jnp.bfloat16)
        kept_weights = None
        saved.append(
            (
                kept_weights,
                state,
                latent_low,
                joined,
                query,
                keys,
                values,
                log_total,
                mixed_low,
                middle,
                hidden_low,
                pre_act,
                act_low,
            )
        )
        state = middle + forward_reduce(product(act_low, full_down))
    result = (state * live_rows).astype(jnp.bfloat16)
    grad_state = cotangent.astype(jnp.float32) * live_rows
    media_part = jnp.zeros_like(media_full)
    grads = [None] * layers
    for layer in reversed(range(layers)):
        (
            kept_weights,
            state_in,
            latent_low,
            joined,
            query,
            keys,
            values,
            log_total,
            mixed_low,
            middle,
            hidden_low,
            pre_act,
            act_low,
        ) = saved[layer]
        weights_now = (
            lax.all_gather(w_query[layer], "dp", axis=0, tiled=True),
            lax.all_gather(w_key[layer], "dp", axis=0, tiled=True),
            lax.all_gather(w_value[layer], "dp", axis=0, tiled=True),
            lax.all_gather(w_out[layer], "dp", axis=1, tiled=True),
            lax.all_gather(w_up[layer], "dp", axis=0, tiled=True),
            lax.all_gather(w_down[layer], "dp", axis=1, tiled=True),
            lax.all_gather(norm_gains[layer], "dp", axis=1, tiled=True),
            lax.all_gather(norm_shifts[layer], "dp", axis=1, tiled=True),
        )
        full_query, full_key, full_value, full_out, full_up, full_down, gain_rows, shift_rows = (
            weights_now
        )
        gains = gain_rows.astype(jnp.float32)
        shifts = shift_rows.astype(jnp.float32)
        down_low = grad_state.astype(jnp.bfloat16)
        grad_down = outer_sum(act_low, down_low)
        grad_act = back_product(down_low, full_down)
        unused, gelu_pull = jax.vjp(partial(jax.nn.gelu, approximate=False), pre_act)
        up_low = gelu_pull(grad_act)[0].astype(jnp.bfloat16)
        grad_up = outer_sum(hidden_low, up_low)
        grad_hidden = backward_reduce(back_product(up_low, full_up))
        unused, norm_pull = jax.vjp(normalize, middle, gains[2], shifts[2])
        grad_middle, gain_feed, shift_feed = norm_pull(grad_hidden)
        grad_middle = grad_middle + grad_state
        out_low = grad_middle.astype(jnp.bfloat16)
        grad_out = outer_sum(mixed_low, out_low)
        grad_mixed = (
            back_product(out_low, full_out)
            .astype(jnp.bfloat16)
            .reshape(images, LATENTS, heads_here, HEAD_DIM)
        )
        query_heads = query.reshape(images, LATENTS, heads_here, HEAD_DIM)
        key_heads = keys.reshape(images, keys_len, heads_here, HEAD_DIM)
        value_heads = values.reshape(images, keys_len, heads_here, HEAD_DIM)
        probs = jnp.exp(key_scores(query_heads, key_heads, key_mask) - log_total)
        probs_low = probs.astype(jnp.bfloat16)
        grad_probs = jnp.einsum(
            "iqhd,ikhd->ihqk", grad_mixed, value_heads, preferred_element_type=jnp.float32
        )
        grad_scores = (
            probs * (grad_probs - jnp.sum(grad_probs * probs, -1, keepdims=True))
        ).astype(jnp.bfloat16)
        grad_values = jnp.einsum(
            "ihqk,iqhd->ikhd", probs_low, grad_mixed, preferred_element_type=jnp.float32
        ).astype(jnp.bfloat16)
        grad_query = (
            jnp.einsum(
                "ihqk,ikhd->iqhd", grad_scores, key_heads, preferred_element_type=jnp.float32
            )
            * 0.125
        ).astype(jnp.bfloat16)
        grad_keys = (
            jnp.einsum(
                "ihqk,iqhd->ikhd", grad_scores, query_heads, preferred_element_type=jnp.float32
            )
            * 0.125
        ).astype(jnp.bfloat16)
        grad_query = grad_query.reshape(images * LATENTS, heads_here * HEAD_DIM)
        grad_keys = grad_keys.reshape(images * keys_len, heads_here * HEAD_DIM)
        grad_values = grad_values.reshape(images * keys_len, heads_here * HEAD_DIM)
        grad_wq = outer_sum(latent_low, grad_query)
        grad_wk = outer_sum(joined, grad_keys)
        grad_wv = outer_sum(joined, grad_values)
        grad_joined = (
            back_product(grad_keys, full_key) + back_product(grad_values, full_value)
        ).reshape(images, keys_len, width)
        grad_latent = backward_reduce(
            back_product(grad_query, full_query)
            + grad_joined[:, PATCH:].reshape(images * LATENTS, width)
        )
        unused, norm_pull = jax.vjp(normalize, state_in, gains[1], shifts[1])
        grad_in, gain_latent, shift_latent = norm_pull(grad_latent)
        grad_state = grad_middle + grad_in
        unused, media_pull = jax.vjp(normalize, media_full, gains[0], shifts[0])
        grad_media_layer, gain_media, shift_media = media_pull(
            grad_joined[:, :PATCH].reshape(images * PATCH, width)
        )
        media_part = media_part + grad_media_layer
        grads[layer] = (
            grad_wq,
            grad_wk,
            grad_wv,
            grad_out,
            grad_up,
            grad_down,
            gain_media,
            shift_media,
            gain_latent,
            shift_latent,
            gain_feed,
            shift_feed,
        )
    media_total, gain_media_all, shift_media_all = (
        lax.psum(media_part.astype(jnp.bfloat16), "mp").astype(jnp.float32),
        lax.psum(jnp.stack([g[6] for g in grads]).astype(jnp.bfloat16), "mp").astype(jnp.float32),
        lax.psum(jnp.stack([g[7] for g in grads]).astype(jnp.bfloat16), "mp").astype(jnp.float32),
    )
    gain_stack = jnp.stack(
        [jnp.stack([gain_media_all[layer], grads[layer][8]]) for layer in range(layers)]
    )
    shift_stack = jnp.stack(
        [jnp.stack([shift_media_all[layer], grads[layer][9]]) for layer in range(layers)]
    )
    feed_stack = jnp.stack(
        [jnp.stack([grads[layer][10], grads[layer][11]]) for layer in range(layers)]
    )
    summed = (
        lax.psum_scatter(jnp.stack([g[0] for g in grads]), "dp", scatter_dimension=1, tiled=True),
        lax.psum_scatter(jnp.stack([g[1] for g in grads]), "dp", scatter_dimension=1, tiled=True),
        lax.psum_scatter(jnp.stack([g[2] for g in grads]), "dp", scatter_dimension=1, tiled=True),
        lax.psum_scatter(jnp.stack([g[3] for g in grads]), "dp", scatter_dimension=2, tiled=True),
        lax.psum_scatter(jnp.stack([g[4] for g in grads]), "dp", scatter_dimension=1, tiled=True),
        lax.psum_scatter(jnp.stack([g[5] for g in grads]), "dp", scatter_dimension=2, tiled=True),
        lax.psum_scatter(gain_stack, "dp", scatter_dimension=2, tiled=True),
        lax.psum_scatter(shift_stack, "dp", scatter_dimension=2, tiled=True),
        lax.psum_scatter(feed_stack, "dp", scatter_dimension=2, tiled=True),
    )
    return (
        result,
        media_total,
        grad_state,
        summed[0],
        summed[1],
        summed[2],
        summed[3],
        summed[4],
        summed[5],
        summed[6],
        summed[7],
        summed[8],
    )


MESH = pl.DeviceIdType.MESH
F32 = jnp.float32
BF16 = jnp.bfloat16
SLOTS = 3
HEADS_HERE = 4
PLANE = 4
ROWS = SLOTS * LATENTS
HALF = LATENTS // 2
WIDTH = 1024
KEYS = PATCH + LATENTS
HEAD_COLS = HEADS_HERE * HEAD_DIM
UNITS = 512
COPIES = 320
LOCALS = 32
QUERY, OUT, KEY_VALUE = (0, 256), (256, 512), (512, 1024)


ORDER = (
    ("enter",), ("AF", 0, "k"), ("SC", 0, "u"), ("OA", 0), ("vectors_out",), ("OF", 0), ("OW", 0), ("prepare",),
    ("OA", 1), ("GO", 1, 0), ("OF", 1), ("OW", 1), ("AF", 0, "q"), ("GO", 1, 1), ("AN", 0, "k"), ("vectors_in",),
    ("MN", 1), ("LN", 0, 1), ("WF", 0, "u"), ("SC", 0, "d"), ("MN", 2), ("MN", 0), ("LN", 0, 0), ("AN", 0, "q"),
    ("AF", 1, "q"), ("LN", 0, 2), ("GH", 1, 0), ("GH", 1, 1), ("RD", 0, "gradhand1"), ("A1", 0, "k"),
    ("RD", 1, "gradhand1"), ("AN", 1, "q"), ("A2", 0, "k"), ("A1", 0, "q"), ("WN", 0, "u"), ("WF", 0, "d"),
    ("AF", 1, "k"), ("A1", 1, "q"), ("A2", 0, "q"), ("SC", 1, "u"), ("SC", 1, "d"), ("RD", 0, "asecondk"),
    ("KM", 0, 1), ("KM", 0, 0), ("KM", 0, 2), ("AN", 1, "k"), ("A2", 1, "q"), ("GO", 1, 2), ("A1", 1, "k"),
    ("WN", 0, "d"), ("RD", 0, "asecondq"), ("AT", 0, 0), ("WF", 1, "u"), ("AT", 0, 2), ("AT", 0, 1),
    ("RD", 0, "nearu"), ("MI", 0, 0), ("MI", 0, 2), ("A2", 1, "k"), ("MI", 0, 1), ("RD", 1, "asecondq"), ("RH", 0, 0),
    ("WN", 1, "u"), ("WF", 1, "d"), ("FU", 0, 0), ("RH", 0, 2), ("RD", 0, "neard"), ("FD", 0, 0), ("RH", 0, 1),
    ("FU", 0, 2), ("FD", 0, 2), ("FS", 0, 0), ("FU", 0, 1), ("RD", 1, "asecondk"), ("KM", 1, 1), ("KM", 1, 0),
    ("KM", 1, 2), ("FD", 0, 1), ("GH", 1, 2), ("FS", 0, 2), ("FS", 0, 1), ("RD", 2, "gradhand1"), ("NS", 0, 0),
    ("LN", 1, 0), ("AT", 1, 0), ("WN", 1, "d"), ("NS", 0, 2), ("MI", 1, 0), ("NS", 0, 1), ("LN", 1, 2), ("AT", 1, 2),
    ("LN", 1, 1), ("AT", 1, 1), ("ST", "afar", "anear", "afirst", "asecond"), ("MI", 1, 2), ("MI", 1, 1),
    ("RH", 1, 0), ("RD", 1, "nearu"), ("FU", 1, 0), ("RH", 1, 2), ("RH", 1, 1), ("FU", 1, 2), ("FU", 1, 1),
    ("GA", 1, "d"), ("RD", 1, "neard"), ("FB", 1, 0), ("FB", 1, 2), ("FB", 1, 1), ("GB", 1, "d"),
    ("ST", "grad1", "gradhand1"), ("ST", "scatter", "far", "near"), ("BS", 1, 0), ("GA", 1, "u"), ("GB", 1, "u"),
    ("BS", 1, 1), ("BS", 1, 2), ("SF", 1, 0), ("FD", 1, 0), ("MB", 1, 0), ("AB", 1, 0), ("SF", 1, 1), ("FS", 1, 0),
    ("SF", 1, 2), ("FD", 1, 2), ("MD", 1, 0), ("SB", 1, 0), ("MB", 1, 1), ("MB", 1, 2), ("AB", 1, 2), ("FS", 1, 2),
    ("AB", 1, 1), ("MD", 1, 1), ("SB", 1, 2), ("FD", 1, 1), ("SB", 1, 1), ("NS", 1, 0), ("GF", 1, "d"), ("FS", 1, 1),
    ("RE", 0), ("GF", 1, "u"), ("GH", 0, 0), ("RD", 0, "gradhand0"), ("FB", 0, 0), ("NS", 1, 2), ("BS", 0, 0),
    ("MD", 1, 2), ("KG", 1), ("GH", 0, 2), ("NS", 1, 1), ("RE", 2), ("GH", 0, 1), ("RD", 2, "gradhand0"),
    ("FB", 0, 2), ("RD", 1, "gradhand0"), ("FB", 0, 1), ("GA", 0, "u"), ("SF", 0, 0), ("RE", 1), ("GB", 0, "u"),
    ("BS", 0, 2), ("QG", 1), ("BS", 0, 1), ("MB", 0, 0), ("AB", 0, 0), ("MD", 0, 0), ("GP", 1, "d"), ("GA", 0, "d"),
    ("SB", 0, 0), ("S2", 1, "k"), ("SF", 0, 2), ("MB", 0, 2), ("SF", 0, 1), ("AB", 0, 2), ("MD", 0, 2), ("MB", 0, 1),
    ("AB", 0, 1), ("QG", 0), ("SB", 0, 2), ("MD", 0, 1), ("SB", 0, 1), ("vector_sums_out",), ("S2", 1, "q"),
    ("SN", 1, "k"), ("GB", 0, "d"), ("KG", 0), ("GF", 0, "u"), ("vector_sums_in",), ("vector_sums_end",),
    ("GF", 0, "d"), ("SR", 1, "k"), ("GP", 1, "u"), ("SN", 1, "q"), ("S2", 0, "q"), ("S2", 0, "k"), ("SN", 0, "q"),
    ("SE", 1, "k"), ("SN", 0, "k"), ("SR", 1, "q"), ("GP", 0, "u"), ("SE", 1, "q"), ("SR", 0, "q"), ("SR", 0, "k"),
    ("GP", 0, "d"), ("SE", 0, "q"), ("SE", 0, "k"), ("close",),
)


class Copies:
    def __init__(self, send_sems, recv_sems, local_sems):
        self.send_sems, self.recv_sems, self.local_sems = send_sems, recv_sems, local_sems
        self.used = self.used_local = 0
        self.sending = []

    def start(self, source, target, device):
        copy = pltpu.make_async_remote_copy(
            src_ref=source,
            dst_ref=target,
            send_sem=self.send_sems.at[self.used],
            recv_sem=self.recv_sems.at[self.used],
            device_id=device,
            device_id_type=MESH,
        )
        self.used += 1
        copy.start()
        self.sending.append(copy)
        return copy

    def start_local(self, source, target):
        copy = pltpu.make_async_copy(source, target, self.local_sems.at[self.used_local])
        self.used_local += 1
        copy.start()
        return copy

    def sent(self, copies):
        for copy in copies:
            if any(kept is copy for kept in self.sending):
                copy.wait_send()
                self.sending = [kept for kept in self.sending if kept is not copy]


def matmul(left, right):
    return jnp.dot(left, right, preferred_element_type=F32)


def matmul_nt(left, right):
    return lax.dot_general(left, right, (((1,), (1,)), ((), ())), preferred_element_type=F32)


def matmul_tn(left, right):
    return lax.dot_general(left, right, (((0,), (0,)), ((), ())), preferred_element_type=F32)


def loop(count, body):
    def step(index, carry):
        body(index)
        return carry

    lax.fori_loop(0, count, step, 0)


def centred(values):
    centre = values - jnp.mean(values, -1, keepdims=True)
    scale = lax.rsqrt(jnp.mean(centre * centre, -1, keepdims=True) + 1e-05)
    return centre * scale, scale


def norm_back(grad, gain, unit, scale):
    inner = grad * gain
    return scale * (
        inner
        - jnp.mean(inner, -1, keepdims=True)
        - unit * jnp.mean(inner * unit, -1, keepdims=True)
    )


def column_sums(values):
    return jnp.sum(values, 0, keepdims=True)


def slot_rows(slot):
    return pl.ds(slot * LATENTS, LATENTS)


def fused_kernel(
    patch_rows,
    image_count,
    media,
    latents,
    cotangent,
    gains,
    shifts,
    w_query,
    w_key,
    w_value,
    w_out_t,
    w_up,
    w_down_t,
    out_latents,
    out_media,
    out_media_pair,
    out_state,
    out_attn,
    out_up,
    out_down_t,
    out_vectors,
    AW,
    FW,
    VB,
    VG,
    GS,
    J,
    X,
    Y,
    Q,
    KV,
    O,
    PR,
    H,
    GP,
    G,
    DY,
    DU,
    ZP,
    PS,
    PRECV,
    TS,
    TR,
    AS,
    AR,
    DX,
    DH,
    DV,
    DAB,
    DQ,
    DKV,
    MG,
    GD,
    RF1,
    RF2,
    RA1A,
    RA1B,
    RA2A,
    RA2B,
    RA3,
    RA4,
    VS,
    VR,
    MASK,
    send_sems,
    recv_sems,
    local_sems,
):
    me = lax.axis_index("dp")
    half = lax.axis_index("mp")
    z, c = me // 4, me % 4
    zh, zl = z // 2, z % 2
    y, x = c // 2, c % 2
    columns = (c, y * 2 + 1 - x, (1 - y) * 2 + x, 3 - c)
    plane = tuple((z * 4 + column, half) for column in columns)
    near = ((zh * 2 + 1 - zl) * 4 + c, half)
    far = (((1 - zh) * 2 + zl) * 4 + c, half)
    sibling = (me, 1 - half)
    copies = Copies(send_sems, recv_sems, local_sems)
    mine = pl.ds(pl.multiple_of(half * HALF, 32), HALF)
    other = pl.ds(pl.multiple_of((1 - half) * HALF, 32), HALF)
    first = jnp.where(half == 0, 1.0, 0.0).astype(F32)
    flying = {}
    tasks = {}

    def task(function):
        tasks[function.__name__] = function
        return function

    def keep(name, started):
        flying[name] = started if isinstance(started, list) else [started]

    def arrived(name):
        for copy in flying[name]:
            copy.wait_recv()
        return flying[name]

    def landed(name):
        for copy in flying.pop(name):
            copy.wait()

    def unit_columns(index):
        return pl.ds(pl.multiple_of(columns[index] * UNITS, UNITS), UNITS)

    up_part, down_part = pl.ds(0, UNITS), pl.ds(UNITS, UNITS)
    parts = {"u": up_part, "d": down_part}
    chunks = {"k": ((512, w_key), (768, w_value)), "q": ((0, w_query), (256, w_out_t))}

    @task
    def enter():
        blank = jnp.zeros((1, gains.shape[2]), F32)
        piece = jnp.concatenate(
            [
                source[which, layer : layer + 1, :].astype(F32)
                for source in (gains, shifts)
                for layer in range(2)
                for which in range(3)
            ]
            + [blank] * 4,
            0,
        )
        odd = c % 2 == 1
        VB[...] = jnp.concatenate(
            [jnp.where(odd, 0.0, piece), jnp.where(odd, piece, 0.0)], 1
        ).astype(BF16)
        barrier = pltpu.get_barrier_semaphore()
        for step in range(1, 16):
            pl.semaphore_signal(
                barrier, inc=1, device_id=((me + step) % 16, half), device_id_type=MESH
            )
        pl.semaphore_signal(barrier, inc=1, device_id=sibling, device_id_type=MESH)
        pl.semaphore_wait(barrier, 16)

    @task
    def vectors_out():
        keep(
            "vectors",
            [copies.start(VB, VG.at[me], ((me + step) % 16, half)) for step in range(1, 16)],
        )

    def own_attn(layer):
        keep(
            f"own_attn{layer}",
            [
                copies.start_local(
                    source.at[layer], AW.at[layer, zh, zl, y, x, :, pl.ds(low, 256)]
                )
                for chunk in "kq"
                for low, source in chunks[chunk]
            ],
        )

    def own_feed(layer):
        keep(
            f"own_feed{layer}",
            [
                copies.start_local(
                    source.at[layer, :, unit_columns(0)], FW.at[layer, zh, zl, c, :, part]
                )
                for source, part in ((w_up, up_part), (w_down_t, down_part))
            ],
        )

    def feed_scatter(layer, part):
        source = w_up if part == "u" else w_down_t
        keep(
            f"scatter{part}{layer}",
            [
                copies.start(
                    source.at[layer, :, unit_columns(index)],
                    FW.at[layer, zh, zl, c, :, parts[part]],
                    plane[index],
                )
                for index in (3, 1, 2)
            ],
        )

    def feed_far(layer, part):
        arrived(f"scatter{part}{layer}")
        block = FW.at[layer, zh, zl, :, :, parts[part]]
        keep(f"far{part}{layer}", copies.start(block, block, far))

    def feed_near(layer, part):
        arrived(f"far{part}{layer}")
        block = FW.at[layer, :, zl, :, :, parts[part]]
        keep(f"near{part}{layer}", copies.start(block, block, near))

    def attn_far(layer, chunk):
        keep(
            f"afar{chunk}{layer}",
            [
                copies.start(
                    source.at[layer], AW.at[layer, zh, zl, y, x, :, pl.ds(low, 256)], far
                )
                for low, source in chunks[chunk]
            ],
        )

    def attn_near(layer, chunk):
        arrived(f"afar{chunk}{layer}")
        block = AW.at[layer, :, zl, y, x, :, pl.ds(chunks[chunk][0][0], 512)]
        keep(f"anear{chunk}{layer}", copies.start(block, block, near))

    def attn_first(layer, chunk):
        arrived(f"anear{chunk}{layer}")
        keep(
            f"afirst{chunk}{layer}",
            [
                copies.start(block, block, plane[1 + side])
                for side in range(2)
                for block in [AW.at[layer, :, :, y, x, :, pl.ds(chunks[chunk][side][0], 256)]]
            ],
        )

    def attn_second(layer, chunk):
        arrived(f"afirst{chunk}{layer}")
        block_a = AW.at[layer, :, :, y, :, :, pl.ds(chunks[chunk][0][0], 256)]
        block_b = AW.at[layer, :, :, :, x, :, pl.ds(chunks[chunk][1][0], 256)]
        keep(
            f"asecond{chunk}{layer}",
            [copies.start(block_a, block_a, plane[2]), copies.start(block_b, block_b, plane[1])],
        )

    @task
    def prepare():
        head_row = lax.broadcasted_iota(jnp.int32, (HEAD_COLS, HEAD_COLS), 0) // HEAD_DIM
        head_column = lax.broadcasted_iota(jnp.int32, (HEAD_COLS, HEAD_COLS), 1) // HEAD_DIM
        MASK[...] = jnp.where(head_row == head_column, 1.0, 0.0).astype(F32)
        VG[me] = VB[...]
        VS[...] = jnp.zeros_like(VS)
        for slot in range(SLOTS):
            rows = slot_rows(slot)
            X[0, rows, :] = latents[rows, :].astype(F32)
            live = jnp.where(slot < image_count[0], 1.0, 0.0).astype(F32)
            grad = cotangent[rows, :].astype(F32) * live
            DX[rows, :] = grad
            DY[1, slot, 0] = grad.astype(BF16)

    @task
    def vectors_in():
        arrived("vectors")
        for tile in range(8):
            GS[:, tile * 128 : tile * 128 + 128] = VG[2 * tile].astype(F32) + VG[
                2 * tile + 1
            ].astype(F32)

    def gain(layer, which):
        return GS[layer * 3 + which : layer * 3 + which + 1, :]

    def shift(layer, which):
        return GS[6 + layer * 3 + which : 7 + layer * 3 + which, :]

    def media_norm(slot):
        def body(index):
            rows = pl.ds(pl.multiple_of(slot * PATCH + index * 64, 64), 64)
            keys = pl.ds(pl.multiple_of(index * 64, 64), 64)
            unit, _ = centred(media[rows, :].astype(F32))
            for layer in range(2):
                J[layer, slot, keys, :] = (unit * gain(layer, 0) + shift(layer, 0)).astype(BF16)

        loop(4, body)

    def latent_norm(layer, slot):
        if layer > 0:
            copies.sent(arrived(f"state{layer}{slot}"))
        unit, _ = centred(X[layer, slot_rows(slot), :])
        J[layer, slot, PATCH:, :] = (unit * gain(layer, 1) + shift(layer, 1)).astype(BF16)

    def attn_weight(layer, span):
        return AW[layer, :, :, :, :, :, span[0] : span[1]].reshape(WIDTH, span[1] - span[0])

    def feed_weight(layer, part):
        low = 0 if part == "u" else UNITS
        return FW[layer, :, :, :, :, low : low + UNITS].reshape(WIDTH, UNITS)

    def stacked(value):
        return (jnp.concatenate([value.astype(F32)] * HEADS_HERE, 0) * MASK[...]).astype(BF16)

    def unstacked(value):
        return jnp.sum((value * MASK[...]).reshape(HEADS_HERE, LATENTS, HEAD_COLS), 0)

    def media_keys(layer, slot):
        KV[layer, slot, 0:PATCH] = matmul(
            J[layer, slot, 0:PATCH, :], attn_weight(layer, KEY_VALUE)
        ).astype(BF16)

    def attention(layer, slot):
        rows = J[layer, slot, PATCH:, :]
        KV[layer, slot, PATCH:] = matmul(rows, attn_weight(layer, KEY_VALUE)).astype(BF16)
        query = matmul(rows, attn_weight(layer, QUERY)).astype(BF16)
        Q[layer, slot] = query
        scores = matmul_nt(stacked(query), KV[layer, slot, :, 0:256]) * 0.125
        key = lax.broadcasted_iota(jnp.int32, (HEAD_COLS, KEYS), 1)
        scores = jnp.where((key >= PATCH) | (key < patch_rows[slot]), scores, NEGATIVE)
        expo = jnp.exp(scores - jnp.max(scores, -1, keepdims=True))
        probs = expo / jnp.sum(expo, -1, keepdims=True)
        PR[layer, slot] = probs
        mixed = unstacked(matmul(probs.astype(BF16), KV[layer, slot, :, 256:512])).astype(BF16)
        O[layer, slot] = mixed
        AS[slot] = matmul_nt(mixed, attn_weight(layer, OUT)).astype(BF16)
        keep(f"mix{layer}{slot}", copies.start(AS.at[slot], AR.at[slot], sibling))

    def spread(name, buffer, layer, slot):
        block = buffer.at[layer, slot, 0, mine]
        keep(
            f"{name}{layer}{slot}",
            [
                copies.start(block, buffer.at[layer, slot, index, mine], plane[index])
                for index in (3, 1, 2)
            ],
        )

    def hand_over(name, buffer, layer, slot):
        started = []
        for index, copy in zip((3, 1, 2), flying[f"{name}{layer}{slot}"]):
            block = buffer.at[layer, slot, index, mine]
            copy.wait_recv()
            started.append(copies.start(block, block, sibling))
        keep(f"{name}hand{layer}{slot}", started)

    def middle(layer, slot):
        copies.sent(arrived(f"mix{layer}{slot}"))
        rows = slot_rows(slot)
        value = X[layer, rows, :] + (AS[slot].astype(F32) + AR[slot].astype(F32))
        Y[layer, rows, :] = value
        unit, _ = centred(value)
        H[layer, slot, 0] = (unit * gain(layer, 2) + shift(layer, 2)).astype(BF16)
        spread("rows", H, layer, slot)

    def send_pair(name, way, slot):
        PS[slot] = ZP[slot, :, other, :].astype(BF16)
        keep(name, copies.start(PS.at[slot], PRECV.at[way, slot], sibling))

    def feed_up(layer, slot):
        arrived(f"rowshand{layer}{slot}")
        pre_act = matmul(H[layer, slot].reshape(256, WIDTH), feed_weight(layer, "u"))
        bell = 0.5 * (1.0 + lax.erf(pre_act * 0.7071067811865476))
        GP[layer, slot] = bell + pre_act * jnp.exp(-0.5 * pre_act * pre_act) * 0.3989422804014327
        act = (pre_act * bell).astype(BF16)
        G[layer, slot] = act

    def feed_down(layer, slot):
        ZP[slot] = matmul_nt(G[layer, slot], feed_weight(layer, "d")).reshape(
            PLANE, LATENTS, WIDTH
        )
        send_pair(f"pair0{layer}{slot}", 0, slot)

    def plane_sum(way, layer, slot):
        copies.sent(arrived(f"pair{way}{layer}{slot}"))
        started = []
        for index in (3, 1, 2):
            TS[slot, index - 1] = (
                ZP[slot, index, mine, :] + PRECV[way, slot, index].astype(F32)
            ).astype(BF16)
            started.append(
                copies.start(TS.at[slot, index - 1], TR.at[way, slot, index - 1], plane[index])
            )
        keep(f"away{way}{layer}{slot}", started)

    def feed_sum(way, layer, slot):
        total = ZP[slot, 0, mine, :] + PRECV[way, slot, 0].astype(F32)
        copies.sent(arrived(f"away{way}{layer}{slot}"))
        for index in range(3):
            total = total + TR[way, slot, index].astype(F32)
        return total

    def half_rows(slot):
        return pl.ds(pl.multiple_of(slot * LATENTS + half * HALF, HALF), HALF)

    def next_state(layer, slot):
        rows = half_rows(slot)
        X[layer + 1, rows, :] = Y[layer, rows, :] + feed_sum(0, layer, slot)
        block = X.at[layer + 1, rows]
        keep(f"state{layer + 1}{slot}", copies.start(block, block, sibling))

    def result(slot):
        copies.sent(arrived(f"state2{slot}"))
        live = jnp.where(slot < image_count[0], 1.0, 0.0).astype(F32)
        rows = slot_rows(slot)
        out_latents[rows, :] = (X[2, rows, :] * live).astype(BF16)

    def feed_back(layer, slot):
        grad_act = matmul(DY[layer, slot].reshape(256, WIDTH), feed_weight(layer, "d"))
        up_low = (grad_act * GP[layer, slot]).astype(BF16)
        DU[slot] = up_low
        ZP[slot] = matmul_nt(up_low, feed_weight(layer, "u")).reshape(PLANE, LATENTS, WIDTH)
        send_pair(f"pair1{layer}{slot}", 1, slot)

    def swap_feed(layer, slot):
        rows = half_rows(slot)
        DH[rows, :] = feed_sum(1, layer, slot)
        block = DH.at[rows]
        keep(f"feed{layer}{slot}", copies.start(block, block, sibling))

    def add_sums(row_gain, row_shift, grad, unit, factor):
        for row, value in ((row_gain, grad * unit), (row_shift, grad)):
            VS[row : row + 1, :] = VS[row : row + 1, :] + column_sums(value) * factor

    def middle_back(layer, slot):
        copies.sent(arrived(f"feed{layer}{slot}"))
        rows = slot_rows(slot)
        unit, scale = centred(Y[layer, rows, :])
        grad = DH[rows, :]
        grad_middle = DX[rows, :] + norm_back(grad, gain(layer, 2), unit, scale)
        DV[rows, :] = grad_middle
        DAB[rows, :] = grad_middle.astype(BF16)
        add_sums(8 + layer * 2, 9 + layer * 2, grad, unit, first)

    def attention_back(layer, slot):
        grad_mixed = matmul(DAB[slot_rows(slot), :], attn_weight(layer, OUT)).astype(BF16)
        grads = stacked(grad_mixed)
        probs = PR[layer, slot]
        grad_probs = matmul_nt(grads, KV[layer, slot, :, 256:512])
        grad_scores = (
            probs * (grad_probs - jnp.sum(grad_probs * probs, -1, keepdims=True))
        ).astype(BF16)
        DKV[slot, :, 256:512] = matmul_tn(probs.astype(BF16), grads).astype(BF16)
        queries = stacked(Q[layer, slot])
        DKV[slot, :, 0:256] = (matmul_tn(grad_scores, queries) * 0.125).astype(BF16)
        grad_query = unstacked(matmul(grad_scores, KV[layer, slot, :, 0:256])) * 0.125
        DQ[slot] = grad_query.astype(BF16)
        AS[slot] = (
            matmul_nt(DQ[slot], attn_weight(layer, QUERY))
            + matmul_nt(DKV[slot, PATCH:, :], attn_weight(layer, KEY_VALUE))
        ).astype(BF16)
        keep(f"norm{layer}{slot}", copies.start(AS.at[slot], AR.at[slot], sibling))

    def state_back(layer, slot):
        copies.sent(arrived(f"norm{layer}{slot}"))
        rows = slot_rows(slot)
        unit, scale = centred(X[layer, rows, :])
        grad = AS[slot].astype(F32) + AR[slot].astype(F32)
        grad_in = DV[rows, :] + norm_back(grad, gain(layer, 1), unit, scale)
        if layer > 0:
            DX[rows, :] = grad_in
            DY[layer - 1, slot, 0] = grad_in.astype(BF16)
            spread("grad", DY, layer - 1, slot)
        else:
            out_state[rows, :] = grad_in
        add_sums(layer * 2 + 1, layer * 2 + 5, grad, unit, first)

    def media_back(layer, slot):
        def body(index):
            keys = pl.ds(pl.multiple_of(index * 128, 128), 128)
            rows = pl.ds(pl.multiple_of(slot * PATCH + index * 128, 128), 128)
            grad = matmul_nt(DKV[slot, keys, :], attn_weight(layer, KEY_VALUE))
            unit, scale = centred(media[rows, :].astype(F32))
            piece = norm_back(grad, gain(layer, 0), unit, scale)
            if layer == 1:
                MG[rows, :] = piece
            else:
                DY[1, slot, pl.ds(index * 2, 2)] = (
                    (MG[rows, :] + piece).astype(BF16).reshape(2, LATENTS, WIDTH)
                )
            add_sums(layer * 2, layer * 2 + 4, grad, unit, 1.0)

        loop(2, body)
        if layer == 0:
            rows = pl.ds(slot * PATCH, PATCH)
            block = DY.at[1, slot]
            keep(f"media{slot}", copies.start(block, out_media_pair.at[slot], sibling))
            keep(f"media_own{slot}", copies.start_local(block, out_media.at[slot]))

    def add_into(target, received):
        target[...] = (target[...].astype(F32) + received[...].astype(F32)).astype(BF16)

    def grad_home(layer, part, high, low, block=slice(None)):
        if (layer, part) == (1, "d"):
            return GD.at[high, low, block]
        return FW.at[layer, high, low, block, :, parts[part]]

    def feed_grad(layer, part, low):
        left, right = (DY, G.at[layer]) if part == "d" else (H, DU)

        def body(high):
            cols = pl.ds(pl.multiple_of((high * 2 + low) * 256, 256), 256)
            sums = matmul_tn(
                left[layer, :, :, :, cols].reshape(4 * ROWS, 256),
                right[...].reshape(4 * ROWS, UNITS),
            )
            grad_home(layer, part, high, low)[...] = sums.astype(BF16).reshape(PLANE, 64, UNITS)

        loop(2, body)

    def feed_grad_away(layer, part):
        feed_grad(layer, part, 1 - zl)
        keep(
            f"gnear{part}{layer}",
            copies.start(
                grad_home(layer, part, slice(None), 1 - zl),
                RF1.at[layer, :, :, :, parts[part]],
                near,
            ),
        )

    def feed_grad_stay(layer, part):
        feed_grad(layer, part, zl)

    def feed_sum_far(layer, part):
        arrived(f"gnear{part}{layer}")

        def add(high):
            for index in range(4):
                add_into(
                    grad_home(layer, part, high, zl, index),
                    RF1.at[layer, high, index, :, parts[part]],
                )

        add(1 - zh)
        block = grad_home(layer, part, 1 - zh, zl)
        keep(f"gfar{part}{layer}", copies.start(block, RF2.at[layer, :, :, parts[part]], far))
        add(zh)

    def feed_sum_plane(layer, part):
        arrived(f"gfar{part}{layer}")
        target = out_up if part == "u" else out_down_t
        started = []
        for index in (3, 1, 2, 0):
            column = columns[index]
            block = grad_home(layer, part, zh, zl, column)
            add_into(block, RF2.at[layer, column, :, parts[part]])
            if index > 0:
                started.append(copies.start(block, target.at[layer, c], plane[index]))
            else:
                keep(f"gown{part}{layer}", copies.start_local(block, target.at[layer, c]))
        keep(f"gplane{part}{layer}", started)

    def attn_grad_query(layer):
        def body(index):
            cols = pl.ds(pl.multiple_of(index * 256, 256), 256)
            high, low = index // 2, index % 2
            query_part = matmul_tn(
                J[layer, :, PATCH:, cols].reshape(ROWS, 256), DQ[...].reshape(ROWS, HEAD_COLS)
            )
            AW[layer, high, low, :, :, :, 0:256] = query_part.astype(BF16).reshape(2, 2, 64, 256)
            out_part = matmul_tn(DAB[:, cols], O[layer].reshape(ROWS, HEAD_COLS))
            AW[layer, high, low, :, :, :, 256:512] = out_part.astype(BF16).reshape(2, 2, 64, 256)

        loop(4, body)
        attn_sum_first(layer, "q")

    def attn_grad_key(layer):
        def body(index):
            cols = pl.ds(pl.multiple_of(index * 256, 256), 256)
            high, low = index // 2, index % 2
            key_part = matmul_tn(
                J[layer, :, :, cols].reshape(SLOTS * KEYS, 256), DKV[...].reshape(SLOTS * KEYS, 512)
            )
            AW[layer, high, low, :, :, :, 512:1024] = key_part.astype(BF16).reshape(2, 2, 64, 512)

        loop(4, body)
        attn_sum_first(layer, "k")

    def low_columns(chunk, side):
        return pl.ds(chunks[chunk][side][0], 256)

    def short_columns(chunk):
        return pl.ds(0 if chunk == "q" else 256, 256)

    def attn_sum_first(layer, chunk):
        here = short_columns(chunk)
        keep(
            f"gfirst{chunk}{layer}",
            [
                copies.start(
                    AW.at[layer, :, :, 1 - y, :, :, low_columns(chunk, 0)],
                    RA1A.at[layer, :, :, :, :, here],
                    plane[2],
                ),
                copies.start(
                    AW.at[layer, :, :, :, 1 - x, :, low_columns(chunk, 1)],
                    RA1B.at[layer, :, :, :, :, here],
                    plane[1],
                ),
            ],
        )

    def attn_sum_second(layer, chunk):
        arrived(f"gfirst{chunk}{layer}")
        here, cols_a, cols_b = short_columns(chunk), low_columns(chunk, 0), low_columns(chunk, 1)

        def add(side_a, side_b):
            def body(index):
                high, low = index // 2, index % 2
                add_into(
                    AW.at[layer, high, low, y, side_a, :, cols_a],
                    RA1A.at[layer, high, low, side_a, :, here],
                )
                add_into(
                    AW.at[layer, high, low, side_b, x, :, cols_b],
                    RA1B.at[layer, high, low, side_b, :, here],
                )

            loop(4, body)

        add(1 - x, 1 - y)
        keep(
            f"gsecond{chunk}{layer}",
            [
                copies.start(
                    AW.at[layer, :, :, y, 1 - x, :, cols_a],
                    RA2A.at[layer, :, :, :, here],
                    plane[1],
                ),
                copies.start(
                    AW.at[layer, :, :, 1 - y, x, :, cols_b],
                    RA2B.at[layer, :, :, :, here],
                    plane[2],
                ),
            ],
        )
        add(x, y)

    def attn_sum_near(layer, chunk):
        arrived(f"gsecond{chunk}{layer}")
        here, cols_a, cols_b = short_columns(chunk), low_columns(chunk, 0), low_columns(chunk, 1)
        both = pl.ds(chunks[chunk][0][0], 512)

        def add(low):
            for high in range(2):
                add_into(
                    AW.at[layer, high, low, y, x, :, cols_a], RA2A.at[layer, high, low, :, here]
                )
                add_into(
                    AW.at[layer, high, low, y, x, :, cols_b], RA2B.at[layer, high, low, :, here]
                )

        add(1 - zl)
        keep(
            f"ganear{chunk}{layer}",
            copies.start(AW.at[layer, :, 1 - zl, y, x, :, both], RA3.at[layer, :, :, both], near),
        )
        add(zl)

    def attn_sum_far(layer, chunk):
        arrived(f"ganear{chunk}{layer}")
        both = pl.ds(chunks[chunk][0][0], 512)

        def add(high):
            add_into(AW.at[layer, high, zl, y, x, :, both], RA3.at[layer, high, :, both])

        add(1 - zh)
        keep(
            f"gafar{chunk}{layer}",
            copies.start(
                AW.at[layer, 1 - zh, zl, y, x, :, both], RA4.at[layer, :, both], far
            ),
        )
        add(zh)

    def attn_sum_end(layer, chunk):
        arrived(f"gafar{chunk}{layer}")
        both = pl.ds(chunks[chunk][0][0], 512)
        out_attn[layer, :, both] = AW[layer, zh, zl, y, x, :, both].astype(F32) + RA4[
            layer, :, both
        ].astype(F32)

    @task
    def vector_sums_out():
        keep(
            "sums",
            [
                copies.start(
                    VS.at[:, pl.ds(pl.multiple_of((((me + step) % 16) // 2) * 128, 128), 128)],
                    VR.at[step],
                    ((me + step) % 16, half),
                )
                for step in range(1, 16)
            ],
        )

    @task
    def vector_sums_in():
        arrived("sums")
        total = VS[:, pl.ds(pl.multiple_of((me // 2) * 128, 128), 128)]
        for step in range(1, 16):
            total = total + VR[step]
        VR[0] = total
        keep("sums_pair", copies.start(VR.at[0], VR.at[16], sibling))

    @task
    def vector_sums_end():
        arrived("sums_pair")
        out_vectors[...] = VR[0] + VR[16]

    def settle(*names):
        for name, started in flying.items():
            if name.startswith(names):
                copies.sent(started)

    @task
    def close():
        for slot in range(SLOTS):
            arrived(f"media{slot}")
            landed(f"media_own{slot}")
        for layer in range(2):
            for part in "ud":
                arrived(f"gplane{part}{layer}")
                landed(f"gown{part}{layer}")
        copies.sent(list(copies.sending))

    def grad_spread(layer, slot):
        spread("grad", DY, layer, slot)

    def grad_hand(layer, slot):
        hand_over("grad", DY, layer, slot)

    def rows_hand(layer, slot):
        hand_over("rows", H, layer, slot)

    def forward_sum(layer, slot):
        plane_sum(0, layer, slot)

    def backward_sum(layer, slot):
        plane_sum(1, layer, slot)

    def own_wait(layer):
        landed(f"own_attn{layer}")
        landed(f"own_feed{layer}")

    def ready(layer, name):
        arrived(f"{name}{layer}")

    steps = dict(
        MN=media_norm, LN=latent_norm, KM=media_keys, AT=attention, MI=middle, RH=rows_hand,
        FU=feed_up, FD=feed_down, FS=forward_sum, NS=next_state, RE=result, GO=grad_spread, GH=grad_hand,
        FB=feed_back, BS=backward_sum, SF=swap_feed, MB=middle_back, AB=attention_back,
        SB=state_back, MD=media_back, OA=own_attn, OF=own_feed, OW=own_wait, SC=feed_scatter,
        WF=feed_far, WN=feed_near, AF=attn_far, AN=attn_near, A1=attn_first, A2=attn_second,
        RD=ready, GA=feed_grad_away, GB=feed_grad_stay, GF=feed_sum_far, GP=feed_sum_plane,
        QG=attn_grad_query, KG=attn_grad_key, S2=attn_sum_second, SN=attn_sum_near,
        SR=attn_sum_far, SE=attn_sum_end, ST=settle,
    )
    for name, *arguments in ORDER:
        if name in tasks:
            tasks[name]()
        else:
            steps[name](*arguments)


def finish_kernel(
    latents, media_own, media_pair, state, attn, up, down_t, sums,
    to_latents, to_media, to_state, to_query, to_key, to_value, to_out_t, to_up, to_down_t,
    to_gains, to_shifts, to_feed,
):
    piece = to_gains.shape[2]
    odd = lax.axis_index("dp") % 2 == 1
    to_latents[...] = latents[...]
    to_state[...] = state[...]
    to_media[...] = media_own[...].astype(F32) + media_pair[...].astype(F32)
    to_query[...] = attn[:, :, 0:256]
    to_out_t[...] = attn[:, :, 256:512]
    to_key[...] = attn[:, :, 512:768]
    to_value[...] = attn[:, :, 768:1024]
    for layer in range(2):
        to_up[layer] = up[layer, 0].astype(F32)
        to_down_t[layer] = down_t[layer, 0].astype(F32)

    @pl.when(pl.program_id(0) == 0)
    def _():
        mine = jnp.where(odd, sums[:, piece:], sums[:, :piece])
        for index, target in enumerate((to_gains, to_shifts, to_feed)):
            for layer in range(2):
                row = index * 4 + layer * 2
                target[layer] = mine[row : row + 2, :]


def finish(latents, media_own, media_pair, state, attn, up, down_t, sums):
    steps = 4
    media_rows, rows, piece = SLOTS * PATCH // steps, ROWS // steps, attn.shape[1]
    spot = pl.BlockSpec((2, 2, piece), lambda step: (0, 0, 0))
    part = piece // steps
    media_block = pl.BlockSpec((media_rows, WIDTH), lambda step: (step, 0))
    row_block = pl.BlockSpec((rows, WIDTH), lambda step: (step, 0))
    head_block = pl.BlockSpec((2, part, HEAD_COLS), lambda step: (0, step, 0))
    unit_block = pl.BlockSpec((2, 1, piece, UNITS), lambda step: (0, step, 0, 0))

    def shape(*dims):
        return jax.ShapeDtypeStruct(dims, F32)

    flat = (SLOTS * PATCH, WIDTH)
    return pl.pallas_call(
        finish_kernel,
        name="finish",
        grid=(steps,),
        out_shape=[
            jax.ShapeDtypeStruct((ROWS, WIDTH), BF16),
            shape(*flat),
            shape(ROWS, WIDTH),
            shape(2, piece, HEAD_COLS),
            shape(2, piece, HEAD_COLS),
            shape(2, piece, HEAD_COLS),
            shape(2, piece, HEAD_COLS),
            shape(2, piece, steps * UNITS),
            shape(2, piece, steps * UNITS),
            shape(2, 2, piece),
            shape(2, 2, piece),
            shape(2, 2, piece),
        ],
        in_specs=[
            row_block,
            media_block,
            media_block,
            row_block,
            pl.BlockSpec((2, part, WIDTH), lambda step: (0, step, 0)),
            unit_block,
            unit_block,
            pl.BlockSpec((16, 128), lambda step: (0, 0)),
        ],
        out_specs=[
            row_block,
            media_block,
            row_block,
            head_block,
            head_block,
            head_block,
            head_block,
            pl.BlockSpec((2, piece, UNITS), lambda step: (0, 0, step)),
            pl.BlockSpec((2, piece, UNITS), lambda step: (0, 0, step)),
            spot,
            spot,
            spot,
        ],
        compiler_params=pltpu.CompilerParams(vmem_limit_bytes=64 * 2**20),
    )(latents, media_own.reshape(flat), media_pair.reshape(flat), state, attn, up, down_t, sums)


def fused(
    media, latents, patch_rows, image_count, cotangent, w_query, w_key, w_value, w_out, w_up, w_down,
    norm_gains, norm_shifts,
):
    w_out_t = jnp.swapaxes(w_out, 1, 2)
    w_down_t = jnp.swapaxes(w_down, 1, 2)
    gains = jnp.swapaxes(norm_gains, 0, 1)
    shifts = jnp.swapaxes(norm_shifts, 0, 1)

    vmem = pl.BlockSpec(memory_space=pltpu.VMEM)
    smem = pl.BlockSpec(memory_space=pltpu.SMEM)
    anywhere = pl.BlockSpec(memory_space=pl.ANY)

    def shape(dims, kind):
        return jax.ShapeDtypeStruct(dims, kind)

    results = pl.pallas_call(
        fused_kernel,
        name="resampler",
        out_shape=[
            shape((ROWS, WIDTH), BF16),
            shape((SLOTS, 4, LATENTS, WIDTH), BF16),
            shape((SLOTS, 4, LATENTS, WIDTH), BF16),
            shape((ROWS, WIDTH), F32),
            shape((2, 64, WIDTH), F32),
            shape((2, 4, 64, UNITS), BF16),
            shape((2, 4, 64, UNITS), BF16),
            shape((16, 128), F32),
        ],
        in_specs=[smem, smem] + [vmem] * 5 + [anywhere] * 6,
        out_specs=[vmem, anywhere, anywhere, vmem, vmem, anywhere, anywhere, vmem],
        scratch_shapes=[
            pltpu.VMEM((2, 2, 2, 2, 2, 64, 1024), BF16),
            pltpu.VMEM((2, 2, 2, 4, 64, 1024), BF16),
            pltpu.VMEM((16, 128), BF16),
            pltpu.VMEM((16, 16, 128), BF16),
            pltpu.VMEM((16, WIDTH), F32),
            pltpu.VMEM((2, SLOTS, KEYS, WIDTH), BF16),
            pltpu.VMEM((3, ROWS, WIDTH), F32),
            pltpu.VMEM((2, ROWS, WIDTH), F32),
            pltpu.VMEM((2, SLOTS, LATENTS, HEAD_COLS), BF16),
            pltpu.VMEM((2, SLOTS, KEYS, 2 * HEAD_COLS), BF16),
            pltpu.VMEM((2, SLOTS, LATENTS, HEAD_COLS), BF16),
            pltpu.VMEM((2, SLOTS, HEAD_COLS, KEYS), F32),
            pltpu.VMEM((2, SLOTS, PLANE, LATENTS, WIDTH), BF16),
            pltpu.VMEM((2, SLOTS, 4 * LATENTS, UNITS), F32),
            pltpu.VMEM((2, SLOTS, 4 * LATENTS, UNITS), BF16),
            pltpu.VMEM((2, SLOTS, PLANE, LATENTS, WIDTH), BF16),
            pltpu.VMEM((SLOTS, 4 * LATENTS, UNITS), BF16),
            pltpu.VMEM((SLOTS, PLANE, LATENTS, WIDTH), F32),
            pltpu.VMEM((SLOTS, PLANE, HALF, WIDTH), BF16),
            pltpu.VMEM((2, SLOTS, PLANE, HALF, WIDTH), BF16),
            pltpu.VMEM((SLOTS, 3, HALF, WIDTH), BF16),
            pltpu.VMEM((2, SLOTS, 3, HALF, WIDTH), BF16),
            pltpu.VMEM((SLOTS, LATENTS, WIDTH), BF16),
            pltpu.VMEM((SLOTS, LATENTS, WIDTH), BF16),
            pltpu.VMEM((ROWS, WIDTH), F32),
            pltpu.VMEM((ROWS, WIDTH), F32),
            pltpu.VMEM((ROWS, WIDTH), F32),
            pltpu.VMEM((ROWS, WIDTH), BF16),
            pltpu.VMEM((SLOTS, LATENTS, HEAD_COLS), BF16),
            pltpu.VMEM((SLOTS, KEYS, 2 * HEAD_COLS), BF16),
            pltpu.VMEM((SLOTS * PATCH, WIDTH), F32),
            pltpu.VMEM((2, 2, 4, 64, UNITS), BF16),
            pltpu.VMEM((2, 2, 4, 64, 1024), BF16),
            pltpu.VMEM((2, 4, 64, 1024), BF16),
            pltpu.VMEM((2, 2, 2, 2, 64, 512), BF16),
            pltpu.VMEM((2, 2, 2, 2, 64, 512), BF16),
            pltpu.VMEM((2, 2, 2, 64, 512), BF16),
            pltpu.VMEM((2, 2, 2, 64, 512), BF16),
            pltpu.VMEM((2, 2, 64, 1024), BF16),
            pltpu.VMEM((2, 64, 1024), BF16),
            pltpu.VMEM((16, WIDTH), F32),
            pltpu.VMEM((17, 16, 128), F32),
            pltpu.VMEM((HEAD_COLS, HEAD_COLS), F32),
            pltpu.SemaphoreType.DMA((COPIES,)),
            pltpu.SemaphoreType.DMA((COPIES,)),
            pltpu.SemaphoreType.DMA((LOCALS,)),
        ],
        compiler_params=pltpu.CompilerParams(
            collective_id=0, has_side_effects=True, vmem_limit_bytes=64 * 2**20
        ),
        cost_estimate=pl.CostEstimate(
            flops=18 * 10**9, bytes_accessed=20 * 10**6, transcendentals=10**6
        ),
    )(
        patch_rows, image_count, media, latents, cotangent, gains, shifts, w_query, w_key, w_value,
        w_out_t, w_up, w_down_t,
    )
    out_latents, media_own, media_pair, out_state, attn, up, down_t, sums = results
    whole = finish(out_latents, media_own, media_pair, out_state, attn, up, down_t, sums)
    turned = {6: True, 8: True}
    return tuple(
        jnp.swapaxes(array, 1, 2) if index in turned else array
        for index, array in enumerate(whole)
    )


def solution(mesh):
    body = fused if (mesh.shape["dp"], mesh.shape["mp"]) == (16, 2) else local
    placed = (
        P("dp", None),
        P("dp", None),
        P("dp"),
        P("dp"),
        P("dp", None),
        P(None, "dp", "mp"),
        P(None, "dp", "mp"),
        P(None, "dp", "mp"),
        P(None, "mp", "dp"),
        P(None, "dp", "mp"),
        P(None, "mp", "dp"),
        P(None, None, "dp"),
        P(None, None, "dp"),
    )
    return jax.shard_map(
        body,
        mesh=mesh,
        in_specs=placed,
        out_specs=(
            P("dp", None),
            P("dp", None),
            P("dp", None),
            P(None, "dp", "mp"),
            P(None, "dp", "mp"),
            P(None, "dp", "mp"),
            P(None, "mp", "dp"),
            P(None, "dp", "mp"),
            P(None, "mp", "dp"),
            P(None, None, "dp"),
            P(None, None, "dp"),
            P(None, None, "dp"),
        ),
        check_vma=False,
    )
```
